512 devices in a mesh: panel: 2 (over core), lat: 8 (over y), lon: 32 (over z, x).
Axes of the slice: x: 4, y: 8, z: 8, core: 2. Of those that a mesh axis runs over, the one named last changes fastest.
Arguments:
- fields: bfloat16 [2, 6, 24, 128, 4096], P('panel', None, None, 'lat', 'lon'), may hold values from -6 to 6
- departure_frac: float32 [2, 24, 128, 4096], P('panel', None, 'lat', 'lon'), may hold values from 0 to 1
- block_shift: int32 [2, 128, 32], P('panel', 'lat'), may hold values from 0 to 3, as said below
- level_mix: float32 [6, 24], replicated, may hold values from -2.5 to 2.5
- projection: float32 [24, 24], replicated, may hold values from -1.25 to 1.25
- mode_shift: float32 [24], replicated, may hold values from 0.02 to 2
- margin_cells: int32 [2, 8, 8192], P('panel', 'lat', 'lon'), may hold values from 0 to 2047, as said below
- margin_source: int32 [2, 8, 8192, 4], P('panel', 'lat', 'lon'), may hold values from 0 to 2047
- margin_weight: float32 [2, 8, 8192, 4], P('panel', 'lat', 'lon'), may hold values from 0.05 to 0.45
Outputs:
- advected: bfloat16 [2, 6, 24, 128, 4096], P('panel', None, None, 'lat', 'lon')
- solution: float32 [2, 24, 128, 4096], P('panel', None, 'lat', 'lon')
- residual: float32 [2, 24, 128, 4096], P('panel', None, 'lat', 'lon')
The draws below stay inside these ranges and needn't reach their ends.
Inputs may be any that keep to these rules, and one draw needn't show every extreme that they name: Row r of panel p on lon device d takes its departure points 32 * block_shift[p, r, d] columns below its own. On every device the rows 2i and 2i + 1 of its block have values summing to at most 3, so the sum of block_shift + 1 over one device's 16 rows is at most 40, and some device reaches 40 in every draw. `margin_cells`: for each device, 256 distinct cell numbers row * 128 + column of its own block. `margin_source`: cell numbers row * 128 + column in the block of the device with the same lat and lon indices on the other panel.
All inputs are finite; a program needn't handle non-finite values.
Results may differ from the reference program's by a relative error of at most 0.0026.
Values may be sent and summed in bfloat16 or wider, within the bound.
No kernel may reach another device: no remote copies, remote signals or barrier semaphores. Data moves between devices by JAX's collectives and lax.ppermute only.
A program may use at most 64 MiB of HBM per device.

```python
import math
import jax
import jax.numpy as jnp
from jax import lax

NF = 6
LEV = 24
BW = 32
CLAT = 16
CLON = 128
OV = 256
ITERS = 3
NB = 4
NLAT = 128
NLON = 4096
N_LAT = 8
N_LON = 32


def panel_texture(noise):
    running = noise
    for offset in range(1, 6):
        running = running + jnp.roll(noise, offset, axis=4)
    running = running * (1.0 / jnp.sqrt(6.0))
    panels = lax.broadcasted_iota(jnp.int32, noise.shape, 0)
    return jnp.where(panels == 1, running, noise)


def draw_fields(key, part):
    key = jax.random.fold_in(key, 5)
    first_key = jax.random.fold_in(key, 0)
    shape = (2, NF, LEV, NLAT, NLON)
    lat_ramp = 0.5 + jnp.arange(NLAT, dtype=jnp.float32) / NLAT
    lon_ramp = 0.5 + jnp.arange(NLON, dtype=jnp.float32) / NLON
    ramp = lat_ramp[:, None] * lon_ramp[None, :]
    values = panel_texture(jax.random.normal(first_key, shape, jnp.float32)) * ramp
    return jnp.clip(values, -6.0, 6.0).astype(jnp.bfloat16)


def draw_block_shift(key, part):
    key = jax.random.fold_in(key, 7)
    keys = jax.random.split(key, 8)
    shape = (2, NLAT // 2, N_LON)
    first = jnp.minimum(jax.random.randint(keys[0], shape, 0, NB, dtype=jnp.int32), jax.random.randint(keys[1], shape, 0, NB, dtype=jnp.int32))
    first = jnp.minimum(first, jax.random.randint(keys[2], shape, 0, NB, dtype=jnp.int32))
    room = NB - first
    second = jnp.minimum(jax.random.randint(keys[3], shape, 0, room, dtype=jnp.int32), jax.random.randint(keys[4], shape, 0, room, dtype=jnp.int32))
    panel_pick = jax.random.randint(keys[5], (), 0, 2, dtype=jnp.int32)
    lat_pick = jax.random.randint(keys[6], (), 0, N_LAT, dtype=jnp.int32)
    lon_pick = jax.random.randint(keys[7], (), 0, N_LON, dtype=jnp.int32)
    panels = lax.broadcasted_iota(jnp.int32, shape, 0)
    pairs = lax.broadcasted_iota(jnp.int32, shape, 1)
    columns = lax.broadcasted_iota(jnp.int32, shape, 2)
    chosen = (panels == panel_pick) & (pairs // (CLAT // 2) == lat_pick) & (columns == lon_pick)
    leading = chosen & (pairs % (CLAT // 2) == 0)
    first = jnp.where(leading, NB - 1, first).astype(jnp.int32)
    second = jnp.where(chosen, NB - 1 - first, second).astype(jnp.int32)
    return jnp.stack([first, second], axis=2).reshape(2, NLAT, N_LON)


def draw_margin_cells(key, part):
    key = jax.random.fold_in(key, 9)
    keys = jax.random.split(key, 2 * N_LAT * N_LON)

    def device_pick(device_key):
        return jax.random.permutation(device_key, CLAT * CLON)[:OV].astype(jnp.int32)
    picks = jax.vmap(device_pick)(keys)
    return picks.reshape(2, N_LAT, N_LON * OV).astype(jnp.int32)


def with_ends(array, own_key, smallest, top_value):
    longest = array.shape.index(max(array.shape))
    spots = []
    for shift in (0, 1):
        where = [jax.random.randint(jax.random.fold_in(own_key, axis), (), 0, length) for axis, length in enumerate(array.shape)]
        where[longest] = (where[longest] + shift) % array.shape[longest]
        spots.append(tuple(where))
    return array.at[spots[0]].set(smallest).at[spots[1]].set(top_value)


def levels(rng, dims, pieces, least, high):
    gain, own = 1.0, jax.random.fold_in(rng, 6)
    for position, blocks in pieces:
        heights = jnp.exp(jax.random.uniform(jax.random.fold_in(own, position), (blocks,), jnp.float32, least / len(pieces), high / len(pieces)))
        gain = gain * jnp.repeat(heights, dims[position] // blocks).reshape([-1 if axis == position else 1 for axis in range(len(dims))])
    return gain


def scatter_about(stream_key, shape, deviation, reach, kind=jnp.bfloat16):
    values = deviation * jax.random.normal(stream_key, shape, jnp.float32)
    return jnp.clip(values, min=-reach, max=reach).astype(kind)


def setup_inputs(seed: int = 0) -> dict:
    splits = jax.random.split(jax.random.key(seed), 10)
    return {
        "fields": draw_fields(jax.random.fold_in(splits[9], 71), 0),
        "departure_frac": jnp.clip(1.0 * jax.random.uniform(splits[1], (2, LEV, NLAT, NLON), jnp.float32) ** levels(splits[1], (2, LEV, NLAT, NLON), ((0, 2), (2, 8), (3, 32)), -0.2, 0.2), 0.0, 1.0),
        "block_shift": draw_block_shift(jax.random.fold_in(splits[9], 71), 0),
        "level_mix": scatter_about(splits[3], (NF, LEV), NF ** -0.5, 2.5, jnp.float32),
        "projection": scatter_about(splits[4], (LEV, LEV), LEV ** -0.5, 1.25, jnp.float32),
        "mode_shift": jnp.clip(jnp.exp(jax.random.uniform(splits[5], (LEV,), jnp.float32, math.log(0.02), math.log(2.0))), 0.02, 2.0),
        "margin_cells": draw_margin_cells(jax.random.fold_in(splits[9], 71), 0),
        "margin_source": with_ends(jax.random.randint(splits[7], (2, N_LAT, N_LON * OV, 4), 0, CLAT * CLON), jax.random.fold_in(splits[7], 1), 0, (CLAT * CLON) - 1).astype(jnp.int32),
        "margin_weight": jnp.clip(0.05 + 0.39999999 * jax.random.uniform(splits[8], (2, N_LAT, N_LON * OV, 4), jnp.float32) ** levels(splits[8], (2, N_LAT, N_LON * OV, 4), ((0, 2), (1, 8), (2, 32)), -0.2, 0.2), 0.05, 0.45),
    }


def cubic_values(window, offset):
    width = offset.shape[-1]
    weight_a = -offset * (offset - 1.0) * (offset - 2.0) / 6.0
    weight_b = (offset + 1.0) * (offset - 1.0) * (offset - 2.0) / 2.0
    weight_c = -(offset + 1.0) * offset * (offset - 2.0) / 2.0
    weight_d = (offset + 1.0) * offset * (offset - 1.0) / 6.0
    total = weight_a * window[..., 0:width].astype(jnp.float32)
    total = total + weight_b * window[..., 1:width + 1].astype(jnp.float32)
    total = total + weight_c * window[..., 2:width + 2].astype(jnp.float32)
    return total + weight_d * window[..., 3:width + 3].astype(jnp.float32)


def advect_panel(field_panel, frac_panel, shift_panel):
    columns = jnp.arange(N_LON, dtype=jnp.int32) * CLON
    starts = (CLON - 1 + columns[None, :] - shift_panel * BW).astype(jnp.int32)
    frac_blocks = frac_panel.reshape(LEV, NLAT, N_LON, CLON)

    def slice_window(strip, start):
        return lax.dynamic_slice_in_dim(strip, start, CLON + 3, axis=1)

    def one_row(strip, row_starts):
        return jax.vmap(slice_window, in_axes=(None, 0), out_axes=1)(strip, row_starts)

    def one_field(grid):
        padded = jnp.pad(grid, ((0, 0), (0, 0), (CLON, 2)))
        windows = jax.vmap(one_row, in_axes=(1, 0), out_axes=1)(padded, starts)
        values = cubic_values(windows, frac_blocks)
        return values.reshape(LEV, NLAT, NLON).astype(jnp.bfloat16)

    return lax.map(one_field, field_panel)


def operate(field, mode_shift):
    padded = jnp.pad(field, ((0, 0), (0, 0), (1, 1), (1, 1)))
    beside = padded[:, :, 2:, 1:-1] + padded[:, :, :-2, 1:-1] + padded[:, :, 1:-1, 2:] + padded[:, :, 1:-1, :-2]
    return (4.0 + mode_shift[None, :, None, None]) * field - beside


def local_inner(left, right):
    return jnp.sum(left * right, axis=(0, 2, 3))


def expand(scalars):
    return scalars[None, :, None, None]


def fill_block(block, other, source, weight, target):
    picked = other[:, source]
    values = jnp.sum(picked * weight[None], axis=2)
    return block.at[:, target].set(values)


def reference(fields, departure_frac, block_shift, level_mix, projection, mode_shift, margin_cells, margin_source, margin_weight):
    advected = jnp.stack([advect_panel(fields[panel], departure_frac[panel], block_shift[panel]) for panel in range(2)])
    level_rhs = jnp.zeros((2, LEV, NLAT, NLON), jnp.float32)
    for field_index in range(NF):
        level_rhs = level_rhs + level_mix[field_index][None, :, None, None] * advected[:, field_index].astype(jnp.float32)
    blocks = level_rhs.reshape(2, LEV, N_LAT, CLAT, N_LON, CLON).transpose(0, 2, 4, 1, 3, 5).reshape(2, N_LAT, N_LON, LEV, CLAT * CLON)
    partner = blocks[::-1]
    source_table = margin_source.reshape(2, N_LAT, N_LON, OV, 4)
    weight_table = margin_weight.reshape(2, N_LAT, N_LON, OV, 4)
    targets = margin_cells.reshape(2, N_LAT, N_LON, OV)
    filled = jax.vmap(jax.vmap(jax.vmap(fill_block)))(blocks, partner, source_table, weight_table, targets)
    joined_rhs = filled.reshape(2, N_LAT, N_LON, LEV, CLAT, CLON).transpose(0, 3, 1, 4, 2, 5).reshape(2, LEV, NLAT, NLON)
    modal_rhs = jnp.einsum('ml,plxy->pmxy', projection, joined_rhs, precision=lax.Precision.HIGHEST)
    solution = jnp.zeros_like(modal_rhs)
    residual = modal_rhs
    directions = [modal_rhs]
    images = [operate(modal_rhs, mode_shift)]
    for iteration in range(ITERS):
        along = local_inner(residual, images[iteration])
        square = local_inner(images[iteration], images[iteration])
        ratio = along / square
        solution = solution + expand(ratio) * directions[iteration]
        residual = residual - expand(ratio) * images[iteration]
        if iteration + 1 < ITERS:
            fresh = operate(residual, mode_shift)
            direction, image_next = residual, fresh
            for earlier in range(iteration + 1):
                beta = -local_inner(fresh, images[earlier]) / local_inner(images[earlier], images[earlier])
                direction = direction + expand(beta) * directions[earlier]
                image_next = image_next + expand(beta) * images[earlier]
            directions.append(direction)
            images.append(image_next)
    return advected, solution, residual
```

```python
import jax
import jax.numpy as jnp
from jax import lax
from jax.experimental import pallas as pl
from jax.experimental.pallas import tpu as pltpu
from jax.sharding import PartitionSpec as P

F32 = jnp.float32
BF16 = jnp.bfloat16
NF = 6
LEV = 24
ROWS = 16
COLS = 128
G = 3
OV = 256
VMEM_LIMIT = 48 * 1024 * 1024


def lane_iota(shape):
    return lax.broadcasted_iota(jnp.int32, shape, len(shape) - 1)


def roll_lanes(x, by):
    by = by % COLS
    if by == 0:
        return x
    return pltpu.roll(x, by, x.ndim - 1)


def params():
    return pltpu.CompilerParams(vmem_limit_bytes=VMEM_LIMIT)


def pack_east_kernel(fields_ref, out_ref):
    lane = lane_iota((ROWS, COLS))
    acc = jnp.zeros((ROWS, COLS), F32)
    for f in range(NF):
        for l8 in range(8):
            i = f * 8 + l8
            x = roll_lanes(fields_ref[f, l8].astype(F32), 2 * i)
            acc = jnp.where((lane >> 1) == i, x, acc)
    out_ref[0] = acc.astype(BF16)


def pack_east(fields):
    return pl.pallas_call(
        pack_east_kernel,
        grid=(G,),
        in_specs=[pl.BlockSpec((NF, 8, ROWS, COLS), lambda g: (0, g, 0, 0))],
        out_specs=pl.BlockSpec((1, ROWS, COLS), lambda g: (g, 0, 0)),
        out_shape=jax.ShapeDtypeStruct((G, ROWS, COLS), BF16),
        compiler_params=params(),
        name="pack_east",
    )(fields)


def advect_kernel(mix_ref, shift_ref, frac_ref, fields_ref, west_ref, east_ref, adv_ref, rhs_ref, half_ref):
    g = pl.program_id(0)
    lon = lax.axis_index("lon")
    table = shift_ref[...]
    own = jnp.sum(jnp.where(lane_iota(table.shape) == lon, table, 0), axis=1, keepdims=True)
    shift = jnp.broadcast_to(own, (ROWS, COLS))
    lane = lane_iota((ROWS, COLS))
    odd = (shift & 1) == 1
    two = (shift & 2) == 2

    def turn(x, sign):
        x = jnp.where(odd, roll_lanes(x, 32 * sign), x)
        return jnp.where(two, roll_lanes(x, 64), x)

    def beyond(j):
        at = ((lane - j + 32 * shift) & (COLS - 1)) - 32 * shift + j
        return (at < 0) | (at >= COLS)

    taps = (-1, 0, 1, 2)
    masks = [beyond(j) for j in taps]
    edge = lane < 2
    east = east_ref[0].astype(F32)
    for l8 in range(8):
        t = turn(frac_ref[l8], -1)
        tm1, tm2, tp1 = t - 1.0, t - 2.0, t + 1.0
        weights = (
            -t * tm1 * tm2 * (1.0 / 6.0),
            tp1 * tm1 * tm2 * 0.5,
            -tp1 * t * tm2 * 0.5,
            tp1 * t * tm1 * (1.0 / 6.0),
        )
        total = jnp.zeros((ROWS, COLS), F32)
        for f in range(NF):
            own_row = fields_ref[f, l8].astype(F32)
            other = jnp.where(edge, roll_lanes(east, -2 * (f * 8 + l8)), west_ref[f, l8].astype(F32))
            acc = None
            for j, mask, weight in zip(taps, masks, weights):
                term = weight * roll_lanes(jnp.where(mask, other, own_row), -j)
                acc = term if acc is None else acc + term
            rounded = acc.astype(BF16)
            acc = rounded.astype(F32)
            adv_ref[f, l8] = turn(acc, 1).astype(BF16)
            total = total + mix_ref[f, g * 8 + l8] * acc
        rhs_ref[0, pl.ds(l8, ROWS, stride=8), :] = turn(total, 1)
    half_ref[0] = rhs_ref[0].astype(BF16)


def advect(mix, shift, frac, fields, west, east):
    block = pl.BlockSpec((NF, 8, ROWS, COLS), lambda g: (0, g, 0, 0))
    group = pl.BlockSpec((1, 128, COLS), lambda g: (g, 0, 0))
    return pl.pallas_call(
        advect_kernel,
        grid=(G,),
        in_specs=[
            pl.BlockSpec(memory_space=pltpu.SMEM),
            pl.BlockSpec((ROWS, 32), lambda g: (0, 0)),
            pl.BlockSpec((8, ROWS, COLS), lambda g: (g, 0, 0)),
            block,
            block,
            pl.BlockSpec((1, ROWS, COLS), lambda g: (g, 0, 0)),
        ],
        out_specs=[block, group, group],
        out_shape=[
            jax.ShapeDtypeStruct((NF, LEV, ROWS, COLS), BF16),
            jax.ShapeDtypeStruct((G, 128, COLS), F32),
            jax.ShapeDtypeStruct((G, 128, COLS), BF16),
        ],
        compiler_params=params(),
        name="advect",
    )(mix, shift, frac, fields, west, east)


def split3(x):
    a = x.astype(BF16)
    rest = x - a.astype(F32)
    b = rest.astype(BF16)
    c = (rest - b.astype(F32)).astype(BF16)
    return a, b, c


def margin_kernel(rhs_ref, both_ref, cells_ref, source_ref, weight_ref, proj_ref, b_ref, top_ref, bottom_ref):
    other = 1 - lax.axis_index("panel")
    src = jnp.concatenate([source_ref[q : q + 1, :] for q in range(4)], axis=1)
    wgt = jnp.concatenate([weight_ref[q : q + 1, :] for q in range(4)], axis=1)
    src_col = jnp.broadcast_to(src & 127, (128, 4 * OV))
    pick = jnp.where(lax.broadcasted_iota(jnp.int32, (128, 4 * OV), 0) == src_col, 1.0, 0.0).astype(BF16)
    src_row = jnp.broadcast_to(src >> 7, (8, 4 * OV))
    wgt = jnp.broadcast_to(wgt, (8, 4 * OV))
    cells = cells_ref[...]
    cell_col = jnp.broadcast_to(cells & 127, (128, OV))
    place = jnp.where(lax.broadcasted_iota(jnp.int32, (128, OV), 0) == cell_col, 1.0, 0.0).astype(BF16)
    cell_row = jnp.broadcast_to(cells >> 7, (128, OV))
    in_row = (lax.broadcasted_iota(jnp.int32, (128, OV), 0) >> 3) == cell_row
    nt = (((1,), (1,)), ((), ()))
    covered = lax.dot_general(jnp.where(in_row, 1.0, 0.0).astype(BF16), place, nt, preferred_element_type=F32) > 0.5
    joined = []
    for lb in range(G):
        cols = jnp.dot(both_ref[other, lb], pick, preferred_element_type=F32)
        rep = jnp.zeros((8, 4 * OV), F32)
        for r in range(ROWS):
            rep = rep + jnp.where(src_row == r, wgt, 0.0) * cols[8 * r : 8 * r + 8, :]
        rep = rep[:, :OV] + rep[:, OV : 2 * OV] + rep[:, 2 * OV : 3 * OV] + rep[:, 3 * OV :]
        spread = jnp.where(in_row, jnp.concatenate([rep] * ROWS, axis=0), 0.0)
        values = None
        for part in split3(spread):
            value = lax.dot_general(part, place, nt, preferred_element_type=F32)
            values = value if values is None else values + value
        joined.append(jnp.where(covered, values, rhs_ref[lb]))
    levels = jnp.concatenate(
        [jnp.concatenate([joined[lb][8 * r : 8 * r + 8] for lb in range(G)], axis=0) for r in range(ROWS)], axis=1
    )
    modal = jnp.dot(proj_ref[...], levels, precision=lax.Precision.HIGHEST, preferred_element_type=F32)
    for lb in range(G):
        for r in range(ROWS):
            tile = modal[8 * lb : 8 * lb + 8, COLS * r : COLS * r + COLS]
            b_ref[lb, 8 * r : 8 * r + 8, :] = tile
            if r < 3:
                top_ref[lb, 8 * r : 8 * r + 8, :] = tile
            if r >= ROWS - 3:
                s = r - (ROWS - 3)
                bottom_ref[lb, 8 * s : 8 * s + 8, :] = tile


def margin(rhs, both, cells, source, weight, proj):
    return pl.pallas_call(
        margin_kernel,
        out_shape=[
            jax.ShapeDtypeStruct((G, 128, COLS), F32),
            jax.ShapeDtypeStruct((G, 24, COLS), F32),
            jax.ShapeDtypeStruct((G, 24, COLS), F32),
        ],
        compiler_params=params(),
        name="margin",
    )(rhs, both, cells, source, weight, proj)


def pack_columns_kernel(b_ref, north_ref, south_ref, out_ref):
    lane = lane_iota((8, COLS))
    for lb in range(G):
        acc = jnp.zeros((8, COLS), F32)
        for i in range(20):
            j = i - 2
            if j < 0:
                row = north_ref[lb, 8 * (j + 3) : 8 * (j + 3) + 8, :]
            elif j >= ROWS:
                row = south_ref[lb, 8 * (j - ROWS) : 8 * (j - ROWS) + 8, :]
            else:
                row = b_ref[lb, 8 * j : 8 * j + 8, :]
            here = ((lane - 6 * i + 3) & 127) < 6
            acc = jnp.where(here, roll_lanes(row, 6 * i), acc)
        out_ref[lb] = acc


def pack_columns(b, north, south):
    return pl.pallas_call(
        pack_columns_kernel,
        out_shape=jax.ShapeDtypeStruct((G, 8, COLS), F32),
        compiler_params=params(),
        name="pack_columns",
    )(b, north, south)


def images_kernel(shift_ref, b_ref, north_ref, south_ref, fwest_ref, feast_ref, c_ref, u1_ref, u2_ref, s_ref):
    lat, lon = lax.axis_index("lat"), lax.axis_index("lon")
    one = jnp.float32(1.0)
    zero = jnp.float32(0.0)
    has_n = jnp.where(lat > 0, one, zero)
    has_s = jnp.where(lat < lax.axis_size("lat") - 1, one, zero)
    has_w = jnp.where(lon > 0, one, zero)
    has_e = jnp.where(lon < lax.axis_size("lon") - 1, one, zero)
    lane = lane_iota((8, COLS))
    first, last = lane == 0, lane == COLS - 1
    side = jnp.where(lane < 64, has_e, has_w)
    from_east = ((lane % 6) < 3) & (lane < 120)

    def line(main, ext):
        return roll_lanes(jnp.where(last, ext, main), 1) + roll_lanes(jnp.where(first, ext, main), -1)

    def row_scale(j):
        return has_n if j < 0 else has_s if j >= ROWS else None

    sums_out = jnp.zeros((8, COLS), F32)
    for lb in range(G):
        diag = lane_iota((8, LEV)) == (lax.broadcasted_iota(jnp.int32, (8, LEV), 0) + 8 * lb)
        a = 4.0 + jnp.sum(jnp.where(diag, jnp.broadcast_to(shift_ref[...], (8, LEV)), 0.0), axis=1, keepdims=True)
        a = jnp.broadcast_to(a, (8, COLS))
        packed = jnp.where(from_east, feast_ref[lb], fwest_ref[lb])

        def b_main(j):
            if j < 0:
                return north_ref[lb, 8 * (j + 3) : 8 * (j + 3) + 8, :]
            if j >= ROWS:
                return south_ref[lb, 8 * (j - ROWS) : 8 * (j - ROWS) + 8, :]
            return b_ref[lb, 8 * j : 8 * j + 8, :]

        bm = {j: b_main(j) for j in (-3, -2)}
        bx = {-2: packed}
        cm, cx, um, ux = {}, {}, {}, {}
        sums = [jnp.zeros((8, COLS), F32) for _ in range(8)]
        for j in range(-2, ROWS + 4):
            if j <= ROWS + 1:
                bm[j + 1] = b_main(j + 1)
                if j + 1 <= ROWS + 1:
                    bx[j + 1] = roll_lanes(packed, -6 * (j + 3))
                value = a * bm[j] - (bm[j - 1] + bm[j + 1] + line(bm[j], bx[j]))
                scale = row_scale(j)
                cm[j] = value if scale is None else value * scale
                if -1 <= j <= ROWS:
                    value = (a * bx[j] - (bx[j - 1] + bx[j + 1] + line(bx[j], bm[j]))) * side
                    cx[j] = value if scale is None else value * scale
                if 0 <= j < ROWS:
                    c_ref[lb, 8 * j : 8 * j + 8, :] = cm[j]
            i = j - 1
            if -1 <= i <= ROWS:
                value = 0.25 * (cm[i - 1] + cm[i + 1] + line(cm[i], cx[i]))
                scale = row_scale(i)
                um[i] = value if scale is None else value * scale
                if 0 <= i < ROWS:
                    ux[i] = 0.25 * (cx[i - 1] + cx[i + 1] + line(cx[i], cm[i])) * side
                    u1_ref[lb, 8 * i : 8 * i + 8, :] = um[i]
            i = j - 2
            if 0 <= i < ROWS:
                u2 = 0.5 * (um[i - 1] + um[i + 1] + line(um[i], ux[i])) - cm[i]
                u2_ref[lb, 8 * i : 8 * i + 8, :] = u2
                b, c, u1 = b_main(i), cm[i], um[i]
                pairs = ((b, c), (b, u1), (b, u2), (c, c), (c, u1), (u1, u1), (u1, u2), (u2, u2))
                sums = [s + x * y for s, (x, y) in zip(sums, pairs)]
        for q in range(8):
            total = jnp.sum(sums[q], axis=1, keepdims=True)
            sums_out = jnp.where(lane == 8 * lb + q, total, sums_out)
    s_ref[...] = sums_out


def images(mode_shift, b, north, south, from_west, from_east):
    full = jax.ShapeDtypeStruct((G, 128, COLS), F32)
    return pl.pallas_call(
        images_kernel,
        out_shape=[full, full, full, jax.ShapeDtypeStruct((8, COLS), F32)],
        compiler_params=params(),
        name="images",
    )(mode_shift, b, north, south, from_west, from_east)


def iterate_kernel(shift_ref, s_ref, b_ref, c_ref, u1_ref, u2_ref, sol_ref, res_ref):
    lane = lane_iota((8, COLS))
    sums = s_ref[...]
    for lb in range(G):
        diag = lane_iota((8, LEV)) == (lax.broadcasted_iota(jnp.int32, (8, LEV), 0) + 8 * lb)
        a = 4.0 + jnp.sum(jnp.where(diag, jnp.broadcast_to(shift_ref[...], (8, LEV)), 0.0), axis=1, keepdims=True)
        a = jnp.broadcast_to(a, (8, COLS))

        def inner(q):
            value = jnp.sum(jnp.where(lane == 8 * lb + q, sums, 0.0), axis=1, keepdims=True)
            return jnp.broadcast_to(value, (8, COLS))

        bc, bu1, bu2, cc, cu1, u1u1, u1u2, u2u2 = [inner(q) for q in range(8)]
        cu2 = 2.0 * u1u1 - cc
        l10 = cu1 / cc
        l20 = cu2 / cc
        d1 = u1u1 - l10 * cu1
        e1 = u1u2 - l10 * cu2
        l21 = e1 / d1
        d2 = u2u2 - l20 * cu2 - l21 * e1
        z0 = bc
        z1 = bu1 - l10 * z0
        z2 = bu2 - l20 * z0 - l21 * z1
        y2 = z2 / d2
        y1 = z1 / d1 - l21 * y2
        y0 = z0 / cc - l10 * y1 - l20 * y2
        for r in range(ROWS):
            rows = slice(8 * r, 8 * r + 8)
            b, c, u1, u2 = b_ref[lb, rows, :], c_ref[lb, rows, :], u1_ref[lb, rows, :], u2_ref[lb, rows, :]
            v1 = 0.25 * (a * b - c)
            v2 = 0.5 * (a * v1 - u1) - b
            at = pl.ds(lb * 128 + r, 8, stride=ROWS)
            sol_ref[at, :] = y0 * b + y1 * v1 + y2 * v2
            res_ref[at, :] = b - y0 * c - y1 * u1 - y2 * u2


def iterate(mode_shift, sums, b, c, u1, u2):
    out = jax.ShapeDtypeStruct((LEV * ROWS, COLS), F32)
    return pl.pallas_call(
        iterate_kernel,
        out_shape=[out, out],
        compiler_params=params(),
        name="iterate",
    )(mode_shift, sums, b, c, u1, u2)


def send(block, axis, by):
    count = lax.axis_size(axis)
    return lax.ppermute(block, axis, [(i, i + by) for i in range(count) if 0 <= i + by < count])


def groups_of_lon(count):
    along_x = [[4 * z + x for x in range(4)] for z in range(count // 4)]
    along_z = [[4 * z + x for z in range(count // 4)] for x in range(4)]
    return along_x, along_z


def reduced(sums):
    along_x, along_z = groups_of_lon(lax.axis_size("lon"))
    sums = lax.psum(sums, "panel")
    sums = lax.psum(sums, "lon", axis_index_groups=along_x)
    sums = lax.psum(sums, "lat")
    return lax.psum(sums, "lon", axis_index_groups=along_z)


def per_device(fields, frac, shift, mix, proj, mode_shift, cells, source, weight):
    fields = fields[0]
    west = send(fields, "lon", 1)
    east = send(pack_east(fields), "lon", -1)
    adv, rhs, half = advect(mix, shift[0], frac[0], fields, west, east)
    both = lax.all_gather(half, "panel")
    b, top, bottom = margin(rhs, both, cells[0], source[0, 0].T, weight[0, 0].T, proj)
    north = send(bottom, "lat", 1)
    south = send(top, "lat", -1)
    columns = pack_columns(b, north, south)
    from_west = send(columns, "lon", 1)
    from_east = send(columns, "lon", -1)
    shifts = mode_shift.reshape(1, LEV)
    c, u1, u2, sums = images(shifts, b, north, south, from_west, from_east)
    sol, res = iterate(shifts, reduced(sums), b, c, u1, u2)
    shape = (1, LEV, ROWS, COLS)
    return adv[None], sol.reshape(shape), res.reshape(shape)


def solution(mesh):
    wide = P("panel", None, None, "lat", "lon")
    flat = P("panel", None, "lat", "lon")
    table = P("panel", "lat", "lon", None)
    in_specs = (wide, flat, P("panel", "lat", None), P(), P(), P(), P("panel", "lat", "lon"), table, table)
    return jax.shard_map(per_device, mesh=mesh, in_specs=in_specs, out_specs=(wide, flat, flat), check_vma=False)
```

```python
import jax
import jax.numpy as jnp
from jax import lax
from jax.experimental import pallas as pl
from jax.experimental.pallas import tpu as pltpu
from jax.sharding import PartitionSpec as P

F32 = jnp.float32
BF16 = jnp.bfloat16
NF = 6
LEV = 24
ROWS = 16
COLS = 128
G = 3
OV = 256
VMEM_LIMIT = 48 * 1024 * 1024


def lane_iota(shape):
    return lax.broadcasted_iota(jnp.int32, shape, len(shape) - 1)


def roll_lanes(x, by):
    by = by % COLS
    if by == 0:
        return x
    return pltpu.roll(x, by, x.ndim - 1)


def params():
    return pltpu.CompilerParams(vmem_limit_bytes=VMEM_LIMIT)


def pack_east_kernel(fields_ref, out_ref):
    lane = lane_iota((ROWS, COLS))
    acc = jnp.zeros((ROWS, COLS), F32)
    for f in range(NF):
        for l8 in range(8):
            i = f * 8 + l8
            x = roll_lanes(fields_ref[f, l8].astype(F32), 2 * i)
            acc = jnp.where((lane >> 1) == i, x, acc)
    out_ref[0] = acc.astype(BF16)


def pack_east(fields):
    return pl.pallas_call(
        pack_east_kernel,
        grid=(G,),
        in_specs=[pl.BlockSpec((NF, 8, ROWS, COLS), lambda g: (0, g, 0, 0))],
        out_specs=pl.BlockSpec((1, ROWS, COLS), lambda g: (g, 0, 0)),
        out_shape=jax.ShapeDtypeStruct((G, ROWS, COLS), BF16),
        compiler_params=params(),
        name="pack_east",
    )(fields)


def half_mask(mask):
    return jnp.where(mask, 1, 0).astype(jnp.int16) == jnp.int16(1)


def advect_kernel(mix_ref, shift_ref, frac_ref, fields_ref, west_ref, east_ref, adv_ref, rhs_ref, half_ref):
    g = pl.program_id(0)
    lon = lax.axis_index("lon")
    table = shift_ref[...]
    own = jnp.sum(jnp.where(lane_iota(table.shape) == lon, table, 0), axis=1, keepdims=True)
    shift = jnp.broadcast_to(own, (ROWS, COLS))
    lane = lane_iota((ROWS, COLS))
    odd, two = (shift & 1) == 1, (shift & 2) == 2
    odd16, two16 = half_mask(odd), half_mask(two)
    edge16 = half_mask(lane < 2)

    def turn(x, sign, odd, two):
        x = jnp.where(odd, roll_lanes(x, 32 * sign), x)
        return jnp.where(two, roll_lanes(x, 64), x)

    def beyond(j):
        at = ((lane - j + 32 * shift) & (COLS - 1)) - 32 * shift + j
        return (at < 0) | (at >= COLS)

    taps = (-1, 0, 1, 2)
    masks = [half_mask(beyond(j)) for j in taps]
    source = lax.broadcasted_iota(jnp.int32, (COLS, COLS), 0)
    target = lax.broadcasted_iota(jnp.int32, (COLS, COLS), 1)
    shifts = [jnp.where(source == ((target + j) & (COLS - 1)), 1.0, 0.0).astype(BF16) for j in taps]
    east = east_ref[0]
    for l8 in range(8):
        t = turn(frac_ref[l8], -1, odd, two)
        tm1, tm2, tp1 = t - 1.0, t - 2.0, t + 1.0
        weights = (
            -t * tm1 * tm2 * (1.0 / 6.0),
            tp1 * tm1 * tm2 * 0.5,
            -tp1 * t * tm2 * 0.5,
            tp1 * t * tm1 * (1.0 / 6.0),
        )
        chosen = [[] for _ in taps]
        for f in range(NF):
            other = jnp.where(edge16, roll_lanes(east, -2 * (f * 8 + l8)), west_ref[f, l8])
            for n, mask in enumerate(masks):
                chosen[n].append(jnp.where(mask, other, fields_ref[f, l8]))
        moved = []
        for j, parts, matrix in zip(taps, chosen, shifts):
            if j == 0:
                moved.append([part.astype(F32) for part in parts])
            else:
                wide = jnp.dot(jnp.concatenate(parts, axis=0), matrix, preferred_element_type=F32)
                moved.append([wide[ROWS * f : ROWS * f + ROWS] for f in range(NF)])
        total = jnp.zeros((ROWS, COLS), F32)
        for f in range(NF):
            acc = weights[0] * moved[0][f]
            for n in range(1, 4):
                acc = acc + weights[n] * moved[n][f]
            rounded = acc.astype(BF16)
            adv_ref[f, l8] = turn(rounded, 1, odd16, two16)
            total = total + mix_ref[f, g * 8 + l8] * rounded.astype(F32)
        rhs_ref[0, pl.ds(l8, ROWS, stride=8), :] = turn(total, 1, odd, two)
    half_ref[0] = rhs_ref[0].astype(BF16)


def advect(mix, shift, frac, fields, west, east):
    block = pl.BlockSpec((NF, 8, ROWS, COLS), lambda g: (0, g, 0, 0))
    group = pl.BlockSpec((1, 128, COLS), lambda g: (g, 0, 0))
    return pl.pallas_call(
        advect_kernel,
        grid=(G,),
        in_specs=[
            pl.BlockSpec(memory_space=pltpu.SMEM),
            pl.BlockSpec((ROWS, 32), lambda g: (0, 0)),
            pl.BlockSpec((8, ROWS, COLS), lambda g: (g, 0, 0)),
            block,
            block,
            pl.BlockSpec((1, ROWS, COLS), lambda g: (g, 0, 0)),
        ],
        out_specs=[block, group, group],
        out_shape=[
            jax.ShapeDtypeStruct((NF, LEV, ROWS, COLS), BF16),
            jax.ShapeDtypeStruct((G, 128, COLS), F32),
            jax.ShapeDtypeStruct((G, 128, COLS), BF16),
        ],
        compiler_params=params(),
        name="advect",
    )(mix, shift, frac, fields, west, east)


def split3(x):
    a = x.astype(BF16)
    rest = x - a.astype(F32)
    b = rest.astype(BF16)
    c = (rest - b.astype(F32)).astype(BF16)
    return a, b, c


def margin_kernel(rhs_ref, both_ref, cells_ref, source_ref, weight_ref, proj_ref, b_ref, top_ref, bottom_ref):
    other = 1 - lax.axis_index("panel")
    src = jnp.concatenate([source_ref[q : q + 1, :] for q in range(4)], axis=1)
    wgt = jnp.concatenate([weight_ref[q : q + 1, :] for q in range(4)], axis=1)
    src_col = jnp.broadcast_to(src & 127, (128, 4 * OV))
    pick = jnp.where(lax.broadcasted_iota(jnp.int32, (128, 4 * OV), 0) == src_col, 1.0, 0.0).astype(BF16)
    src_row = jnp.broadcast_to(src >> 7, (8, 4 * OV))
    wgt = jnp.broadcast_to(wgt, (8, 4 * OV))
    cells = cells_ref[...]
    cell_col = jnp.broadcast_to(cells & 127, (128, OV))
    place = jnp.where(lax.broadcasted_iota(jnp.int32, (128, OV), 0) == cell_col, 1.0, 0.0).astype(BF16)
    cell_row = jnp.broadcast_to(cells >> 7, (128, OV))
    in_row = (lax.broadcasted_iota(jnp.int32, (128, OV), 0) >> 3) == cell_row
    nt = (((1,), (1,)), ((), ()))
    covered = lax.dot_general(jnp.where(in_row, 1.0, 0.0).astype(BF16), place, nt, preferred_element_type=F32) > 0.5
    joined = []
    for lb in range(G):
        cols = jnp.dot(both_ref[other, lb], pick, preferred_element_type=F32)
        rep = jnp.zeros((8, 4 * OV), F32)
        for r in range(ROWS):
            rep = rep + jnp.where(src_row == r, wgt, 0.0) * cols[8 * r : 8 * r + 8, :]
        rep = rep[:, :OV] + rep[:, OV : 2 * OV] + rep[:, 2 * OV : 3 * OV] + rep[:, 3 * OV :]
        spread = jnp.where(in_row, jnp.concatenate([rep] * ROWS, axis=0), 0.0)
        values = None
        for part in split3(spread):
            value = lax.dot_general(part, place, nt, preferred_element_type=F32)
            values = value if values is None else values + value
        joined.append(jnp.where(covered, values, rhs_ref[lb]))
    levels = jnp.concatenate(
        [jnp.concatenate([joined[lb][8 * r : 8 * r + 8] for lb in range(G)], axis=0) for r in range(ROWS)], axis=1
    )
    modal = jnp.dot(proj_ref[...], levels, precision=lax.Precision.HIGHEST, preferred_element_type=F32)
    for lb in range(G):
        for r in range(ROWS):
            tile = modal[8 * lb : 8 * lb + 8, COLS * r : COLS * r + COLS]
            b_ref[lb, 8 * r : 8 * r + 8, :] = tile
            if r < 3:
                top_ref[lb, 8 * r : 8 * r + 8, :] = tile
            if r >= ROWS - 3:
                s = r - (ROWS - 3)
                bottom_ref[lb, 8 * s : 8 * s + 8, :] = tile


def margin(rhs, both, cells, source, weight, proj):
    return pl.pallas_call(
        margin_kernel,
        out_shape=[
            jax.ShapeDtypeStruct((G, 128, COLS), F32),
            jax.ShapeDtypeStruct((G, 24, COLS), F32),
            jax.ShapeDtypeStruct((G, 24, COLS), F32),
        ],
        compiler_params=params(),
        name="margin",
    )(rhs, both, cells, source, weight, proj)


def pack_columns_kernel(b_ref, north_ref, south_ref, out_ref):
    lane = lane_iota((8, COLS))
    for lb in range(G):
        acc = jnp.zeros((8, COLS), F32)
        for i in range(20):
            j = i - 2
            if j < 0:
                row = north_ref[lb, 8 * (j + 3) : 8 * (j + 3) + 8, :]
            elif j >= ROWS:
                row = south_ref[lb, 8 * (j - ROWS) : 8 * (j - ROWS) + 8, :]
            else:
                row = b_ref[lb, 8 * j : 8 * j + 8, :]
            here = ((lane - 6 * i + 3) & 127) < 6
            acc = jnp.where(here, roll_lanes(row, 6 * i), acc)
        out_ref[lb] = acc


def pack_columns(b, north, south):
    return pl.pallas_call(
        pack_columns_kernel,
        out_shape=jax.ShapeDtypeStruct((G, 8, COLS), F32),
        compiler_params=params(),
        name="pack_columns",
    )(b, north, south)


def images_kernel(shift_ref, b_ref, north_ref, south_ref, fwest_ref, feast_ref, c_ref, u1_ref, u2_ref, s_ref):
    lat, lon = lax.axis_index("lat"), lax.axis_index("lon")
    one = jnp.float32(1.0)
    zero = jnp.float32(0.0)
    has_n = jnp.where(lat > 0, one, zero)
    has_s = jnp.where(lat < lax.axis_size("lat") - 1, one, zero)
    has_w = jnp.where(lon > 0, one, zero)
    has_e = jnp.where(lon < lax.axis_size("lon") - 1, one, zero)
    lane = lane_iota((8, COLS))
    first, last = lane == 0, lane == COLS - 1
    side = jnp.where(lane < 64, has_e, has_w)
    from_east = ((lane % 6) < 3) & (lane < 120)

    def line(main, ext):
        return roll_lanes(jnp.where(last, ext, main), 1) + roll_lanes(jnp.where(first, ext, main), -1)

    def row_scale(j):
        return has_n if j < 0 else has_s if j >= ROWS else None

    sums_out = jnp.zeros((8, COLS), F32)
    for lb in range(G):
        diag = lane_iota((8, LEV)) == (lax.broadcasted_iota(jnp.int32, (8, LEV), 0) + 8 * lb)
        a = 4.0 + jnp.sum(jnp.where(diag, jnp.broadcast_to(shift_ref[...], (8, LEV)), 0.0), axis=1, keepdims=True)
        a = jnp.broadcast_to(a, (8, COLS))
        packed = jnp.where(from_east, feast_ref[lb], fwest_ref[lb])

        def b_main(j):
            if j < 0:
                return north_ref[lb, 8 * (j + 3) : 8 * (j + 3) + 8, :]
            if j >= ROWS:
                return south_ref[lb, 8 * (j - ROWS) : 8 * (j - ROWS) + 8, :]
            return b_ref[lb, 8 * j : 8 * j + 8, :]

        bm = {j: b_main(j) for j in (-3, -2)}
        bx = {-2: packed}
        cm, cx, um, ux = {}, {}, {}, {}
        sums = [jnp.zeros((8, COLS), F32) for _ in range(8)]
        for j in range(-2, ROWS + 4):
            if j <= ROWS + 1:
                bm[j + 1] = b_main(j + 1)
                if j + 1 <= ROWS + 1:
                    bx[j + 1] = roll_lanes(packed, -6 * (j + 3))
                value = a * bm[j] - (bm[j - 1] + bm[j + 1] + line(bm[j], bx[j]))
                scale = row_scale(j)
                cm[j] = value if scale is None else value * scale
                if -1 <= j <= ROWS:
                    value = (a * bx[j] - (bx[j - 1] + bx[j + 1] + line(bx[j], bm[j]))) * side
                    cx[j] = value if scale is None else value * scale
                if 0 <= j < ROWS:
                    c_ref[lb, 8 * j : 8 * j + 8, :] = cm[j]
            i = j - 1
            if -1 <= i <= ROWS:
                value = 0.25 * (cm[i - 1] + cm[i + 1] + line(cm[i], cx[i]))
                scale = row_scale(i)
                um[i] = value if scale is None else value * scale
                if 0 <= i < ROWS:
                    ux[i] = 0.25 * (cx[i - 1] + cx[i + 1] + line(cx[i], cm[i])) * side
                    u1_ref[lb, 8 * i : 8 * i + 8, :] = um[i]
            i = j - 2
            if 0 <= i < ROWS:
                u2 = 0.5 * (um[i - 1] + um[i + 1] + line(um[i], ux[i])) - cm[i]
                u2_ref[lb, 8 * i : 8 * i + 8, :] = u2
                b, c, u1 = b_main(i), cm[i], um[i]
                pairs = ((b, c), (b, u1), (b, u2), (c, c), (c, u1), (u1, u1), (u1, u2), (u2, u2))
                sums = [s + x * y for s, (x, y) in zip(sums, pairs)]
        for q in range(8):
            total = jnp.sum(sums[q], axis=1, keepdims=True)
            sums_out = jnp.where(lane == 8 * lb + q, total, sums_out)
    for n in range(s_ref.shape[0]):
        s_ref[n] = sums_out


def images(mode_shift, b, north, south, from_west, from_east, copies):
    full = jax.ShapeDtypeStruct((G, 128, COLS), F32)
    return pl.pallas_call(
        images_kernel,
        out_shape=[full, full, full, jax.ShapeDtypeStruct((copies, 8, COLS), F32)],
        compiler_params=params(),
        name="images",
    )(mode_shift, b, north, south, from_west, from_east)


def sum_copies(ref):
    parts = [ref[n] for n in range(ref.shape[0])]
    while len(parts) > 1:
        parts = [parts[n] + parts[n + 1] for n in range(0, len(parts), 2)]
    return parts[0]


def iterate_kernel(shift_ref, s_ref, b_ref, c_ref, u1_ref, u2_ref, sol_ref, res_ref):
    lane = lane_iota((8, COLS))
    sums = sum_copies(s_ref)
    for lb in range(G):
        diag = lane_iota((8, LEV)) == (lax.broadcasted_iota(jnp.int32, (8, LEV), 0) + 8 * lb)
        a = 4.0 + jnp.sum(jnp.where(diag, jnp.broadcast_to(shift_ref[...], (8, LEV)), 0.0), axis=1, keepdims=True)
        a = jnp.broadcast_to(a, (8, COLS))

        def inner(q):
            value = jnp.sum(jnp.where(lane == 8 * lb + q, sums, 0.0), axis=1, keepdims=True)
            return jnp.broadcast_to(value, (8, COLS))

        bc, bu1, bu2, cc, cu1, u1u1, u1u2, u2u2 = [inner(q) for q in range(8)]
        cu2 = 2.0 * u1u1 - cc
        l10 = cu1 / cc
        l20 = cu2 / cc
        d1 = u1u1 - l10 * cu1
        e1 = u1u2 - l10 * cu2
        l21 = e1 / d1
        d2 = u2u2 - l20 * cu2 - l21 * e1
        z0 = bc
        z1 = bu1 - l10 * z0
        z2 = bu2 - l20 * z0 - l21 * z1
        y2 = z2 / d2
        y1 = z1 / d1 - l21 * y2
        y0 = z0 / cc - l10 * y1 - l20 * y2
        for r in range(ROWS):
            rows = slice(8 * r, 8 * r + 8)
            b, c, u1, u2 = b_ref[lb, rows, :], c_ref[lb, rows, :], u1_ref[lb, rows, :], u2_ref[lb, rows, :]
            v1 = 0.25 * (a * b - c)
            v2 = 0.5 * (a * v1 - u1) - b
            at = pl.ds(lb * 128 + r, 8, stride=ROWS)
            sol_ref[at, :] = y0 * b + y1 * v1 + y2 * v2
            res_ref[at, :] = b - y0 * c - y1 * u1 - y2 * u2


def iterate(mode_shift, sums, b, c, u1, u2):
    out = jax.ShapeDtypeStruct((LEV * ROWS, COLS), F32)
    return pl.pallas_call(
        iterate_kernel,
        out_shape=[out, out],
        compiler_params=params(),
        name="iterate",
    )(mode_shift, sums, b, c, u1, u2)


def send(block, axis, by):
    count = lax.axis_size(axis)
    return lax.ppermute(block, axis, [(i, i + by) for i in range(count) if 0 <= i + by < count])


def relay_kernel(in_ref, out_ref):
    total = sum_copies(in_ref)
    for n in range(out_ref.shape[0]):
        out_ref[n] = total


def relay(parts, copies):
    return pl.pallas_call(
        relay_kernel,
        out_shape=jax.ShapeDtypeStruct((copies, 8, COLS), F32),
        compiler_params=params(),
        name="relay",
    )(parts)


def per_device(fields, frac, shift, mix, proj, mode_shift, cells, source, weight):
    fields = fields[0]
    west = send(fields, "lon", 1)
    east = send(pack_east(fields), "lon", -1)
    adv, rhs, half = advect(mix, shift[0], frac[0], fields, west, east)
    both = lax.all_gather(half, "panel")
    b, top, bottom = margin(rhs, both, cells[0], source[0, 0].T, weight[0, 0].T, proj)
    north = send(bottom, "lat", 1)
    south = send(top, "lat", -1)
    columns = pack_columns(b, north, south)
    from_west = send(columns, "lon", 1)
    from_east = send(columns, "lon", -1)
    shifts = mode_shift.reshape(1, LEV)
    count = lax.axis_size("lon")
    rest = lax.axis_size("panel") * lax.axis_size("lat")
    c, u1, u2, sums = images(shifts, b, north, south, from_west, from_east, count)
    sums = relay(lax.all_to_all(sums, "lon", 0, 0), rest)
    sums = lax.all_to_all(sums, ("panel", "lat"), 0, 0)
    sol, res = iterate(shifts, sums, b, c, u1, u2)
    shape = (1, LEV, ROWS, COLS)
    return adv[None], sol.reshape(shape), res.reshape(shape)


def solution(mesh):
    wide = P("panel", None, None, "lat", "lon")
    flat = P("panel", None, "lat", "lon")
    table = P("panel", "lat", "lon", None)
    in_specs = (wide, flat, P("panel", "lat", None), P(), P(), P(), P("panel", "lat", "lon"), table, table)
    return jax.shard_map(per_device, mesh=mesh, in_specs=in_specs, out_specs=(wide, flat, flat), check_vma=False)
```

```python
import jax
import jax.numpy as jnp
from jax import lax
from jax.experimental import pallas as pl
from jax.experimental.pallas import tpu as pltpu
from jax.sharding import PartitionSpec as P

F32 = jnp.float32
BF16 = jnp.bfloat16
NF = 6
LEV = 24
ROWS = 16
COLS = 128
G = 3
OV = 256
VMEM_LIMIT = 48 * 1024 * 1024


def lane_iota(shape):
    return lax.broadcasted_iota(jnp.int32, shape, len(shape) - 1)


def roll_lanes(x, by):
    by = by % COLS
    if by == 0:
        return x
    return pltpu.roll(x, by, x.ndim - 1)


def params():
    return pltpu.CompilerParams(vmem_limit_bytes=VMEM_LIMIT)


def own_shift(shift_ref, lon):
    table = shift_ref[...]
    own = jnp.sum(jnp.where(lane_iota(table.shape) == lon, table, 0), axis=1, keepdims=True)
    return jnp.broadcast_to(own, (ROWS, COLS))


def half_mask(mask):
    return jnp.where(mask, 1, 0).astype(jnp.int16) == jnp.int16(1)


def lane_matrix(rule):
    source = lax.broadcasted_iota(jnp.int32, (COLS, COLS), 0)
    target = lax.broadcasted_iota(jnp.int32, (COLS, COLS), 1)
    return jnp.where(rule(source, target), 1.0, 0.0).astype(BF16)


def mirrored(source, target):
    return (target >= 32) & (source == jnp.where((target >> 5) == 2, target, (target + 64) & (COLS - 1)))


def pack_kernel(shift_ref, fields_ref, west_ref, east_ref, scratch):
    shift = own_shift(shift_ref, lax.axis_index("lon") + 1)
    lane = lane_iota((ROWS, COLS))
    low = (lax.broadcasted_iota(jnp.int32, (ROWS, COLS), 0) & 1) == 0
    block = lane >= COLS - 32 * shift
    single = lane == COLS - 1 - 32 * shift
    masks = [half_mask(m & row) for row in (low, ~low) for m in (block, single)]
    matrix = jnp.concatenate(
        [
            lane_matrix(lambda s, t: s == t),
            lane_matrix(lambda s, t: ((s & 31) == 31) & (t == 31)),
            lane_matrix(mirrored),
            lane_matrix(lambda s, t: ((s & 31) == 31) & (t == 30)),
        ],
        axis=0,
    )
    zero = jnp.zeros((ROWS, COLS), BF16)
    acc = jnp.zeros((ROWS, COLS), F32)
    for l8 in range(8):
        parts = [
            jnp.concatenate([jnp.where(m, fields_ref[f, l8], zero) for m in masks], axis=1) for f in range(NF)
        ]
        scratch[l8] = jnp.dot(jnp.concatenate(parts, axis=0), matrix, preferred_element_type=F32)
        pairs = scratch[l8, pl.ds(0, 8 * NF, stride=2), :] + scratch[l8, pl.ds(1, 8 * NF, stride=2), :]
        pairs = pairs.astype(BF16)
        for n in range(NF // 2):
            west_ref[n, l8] = pairs[ROWS * n : ROWS * n + ROWS]
        for f in range(NF):
            i = f * 8 + l8
            x = roll_lanes(fields_ref[f, l8].astype(F32), 2 * i)
            acc = jnp.where((lane >> 1) == i, x, acc)
    east_ref[0] = acc.astype(BF16)


def pack(shift, fields):
    return pl.pallas_call(
        pack_kernel,
        grid=(G,),
        in_specs=[
            pl.BlockSpec((ROWS, 32), lambda g: (0, 0)),
            pl.BlockSpec((NF, 8, ROWS, COLS), lambda g: (0, g, 0, 0)),
        ],
        out_specs=[
            pl.BlockSpec((NF // 2, 8, ROWS, COLS), lambda g: (0, g, 0, 0)),
            pl.BlockSpec((1, ROWS, COLS), lambda g: (g, 0, 0)),
        ],
        out_shape=[
            jax.ShapeDtypeStruct((NF // 2, LEV, ROWS, COLS), BF16),
            jax.ShapeDtypeStruct((G, ROWS, COLS), BF16),
        ],
        scratch_shapes=[pltpu.VMEM((8, NF * ROWS, COLS), F32)],
        compiler_params=params(),
        name="pack",
    )(shift, fields)


def advect_kernel(mix_ref, shift_ref, frac_ref, fields_ref, west_ref, east_ref, adv_ref, rhs_ref, half_ref, scratch):
    g = pl.program_id(0)
    shift = own_shift(shift_ref, lax.axis_index("lon"))
    lane = lane_iota((ROWS, COLS))
    low = (lax.broadcasted_iota(jnp.int32, (ROWS, COLS), 0) & 1) == 0
    swap16 = half_mask(~low & ((lane >> 5) != 2))
    single16 = half_mask(lane == jnp.where(low, 31, 30))
    single_at = jnp.concatenate([lane == ((COLS - 32 * shift) & (COLS - 1))] * NF, axis=0)
    single_to = lane_matrix(lambda s, t: ((s == 30) | (s == 31)) & ((t & 31) == 0))
    zero = jnp.zeros((ROWS, COLS), BF16)
    odd, two = (shift & 1) == 1, (shift & 2) == 2
    odd16, two16 = half_mask(odd), half_mask(two)
    edge16 = half_mask(lane < 2)

    def turn(x, sign, odd, two):
        x = jnp.where(odd, roll_lanes(x, 32 * sign), x)
        return jnp.where(two, roll_lanes(x, 64), x)

    def beyond(j):
        at = ((lane - j + 32 * shift) & (COLS - 1)) - 32 * shift + j
        return (at < 0) | (at >= COLS)

    taps = (-1, 0, 1, 2)
    masks = [half_mask(beyond(j)) for j in taps]
    shifts = [lane_matrix(lambda s, t, j=j: s == ((t + j) & (COLS - 1))) for j in taps]
    east = east_ref[0]
    for l8 in range(8):
        t = turn(frac_ref[l8], -1, odd, two)
        tm1, tm2, tp1 = t - 1.0, t - 2.0, t + 1.0
        weights = (
            -t * tm1 * tm2 * (1.0 / 6.0),
            tp1 * tm1 * tm2 * 0.5,
            -tp1 * t * tm2 * 0.5,
            tp1 * t * tm1 * (1.0 / 6.0),
        )
        shared = jnp.concatenate([west_ref[n, l8] for n in range(NF // 2)], axis=0).astype(F32)
        scratch[l8, pl.ds(0, 8 * NF, stride=2), :] = shared
        scratch[l8, pl.ds(1, 8 * NF, stride=2), :] = shared
        west = scratch[l8].astype(BF16)
        chosen = [[] for _ in taps]
        singles = []
        for f in range(NF):
            other = west[ROWS * f : ROWS * f + ROWS]
            singles.append(jnp.where(single16, other, zero))
            other = jnp.where(swap16, roll_lanes(other, 64), other)
            other = jnp.where(edge16, roll_lanes(east, -2 * (f * 8 + l8)), other)
            for n, mask in enumerate(masks):
                chosen[n].append(jnp.where(mask, other, fields_ref[f, l8]))
        moved = []
        for j, parts, matrix in zip(taps, chosen, shifts):
            if j == 0:
                moved.append([part.astype(F32) for part in parts])
            else:
                wide = jnp.dot(jnp.concatenate(parts, axis=0), matrix, preferred_element_type=F32)
                if j == -1:
                    column = jnp.dot(jnp.concatenate(singles, axis=0), single_to, preferred_element_type=F32)
                    wide = jnp.where(single_at, column, wide)
                moved.append([wide[ROWS * f : ROWS * f + ROWS] for f in range(NF)])
        total = jnp.zeros((ROWS, COLS), F32)
        for f in range(NF):
            acc = weights[0] * moved[0][f]
            for n in range(1, 4):
                acc = acc + weights[n] * moved[n][f]
            rounded = acc.astype(BF16)
            adv_ref[f, l8] = turn(rounded, 1, odd16, two16)
            total = total + mix_ref[f, g * 8 + l8] * rounded.astype(F32)
        rhs_ref[0, pl.ds(l8, ROWS, stride=8), :] = turn(total, 1, odd, two)
    half_ref[0] = rhs_ref[0].astype(BF16)


def advect(mix, shift, frac, fields, west, east):
    block = pl.BlockSpec((NF, 8, ROWS, COLS), lambda g: (0, g, 0, 0))
    group = pl.BlockSpec((1, 128, COLS), lambda g: (g, 0, 0))
    return pl.pallas_call(
        advect_kernel,
        grid=(G,),
        in_specs=[
            pl.BlockSpec(memory_space=pltpu.SMEM),
            pl.BlockSpec((ROWS, 32), lambda g: (0, 0)),
            pl.BlockSpec((8, ROWS, COLS), lambda g: (g, 0, 0)),
            block,
            pl.BlockSpec((NF // 2, 8, ROWS, COLS), lambda g: (0, g, 0, 0)),
            pl.BlockSpec((1, ROWS, COLS), lambda g: (g, 0, 0)),
        ],
        out_specs=[block, group, group],
        out_shape=[
            jax.ShapeDtypeStruct((NF, LEV, ROWS, COLS), BF16),
            jax.ShapeDtypeStruct((G, 128, COLS), F32),
            jax.ShapeDtypeStruct((G, 128, COLS), BF16),
        ],
        scratch_shapes=[pltpu.VMEM((8, NF * ROWS, COLS), F32)],
        compiler_params=params(),
        name="advect",
    )(mix, shift, frac, fields, west, east)


def split3(x):
    a = x.astype(BF16)
    rest = x - a.astype(F32)
    b = rest.astype(BF16)
    c = (rest - b.astype(F32)).astype(BF16)
    return a, b, c


def margin_kernel(rhs_ref, both_ref, cells_ref, source_ref, weight_ref, proj_ref, b_ref, top_ref, bottom_ref):
    other = 1 - lax.axis_index("panel")
    src = jnp.concatenate([source_ref[q : q + 1, :] for q in range(4)], axis=1)
    wgt = jnp.concatenate([weight_ref[q : q + 1, :] for q in range(4)], axis=1)
    src_col = jnp.broadcast_to(src & 127, (128, 4 * OV))
    pick = jnp.where(lax.broadcasted_iota(jnp.int32, (128, 4 * OV), 0) == src_col, 1.0, 0.0).astype(BF16)
    src_row = jnp.broadcast_to(src >> 7, (8, 4 * OV))
    wgt = jnp.broadcast_to(wgt, (8, 4 * OV))
    cells = cells_ref[...]
    cell_col = jnp.broadcast_to(cells & 127, (128, OV))
    place = jnp.where(lax.broadcasted_iota(jnp.int32, (128, OV), 0) == cell_col, 1.0, 0.0).astype(BF16)
    cell_row = jnp.broadcast_to(cells >> 7, (128, OV))
    in_row = (lax.broadcasted_iota(jnp.int32, (128, OV), 0) >> 3) == cell_row
    nt = (((1,), (1,)), ((), ()))
    covered = lax.dot_general(jnp.where(in_row, 1.0, 0.0).astype(BF16), place, nt, preferred_element_type=F32) > 0.5
    joined = []
    for lb in range(G):
        cols = jnp.dot(both_ref[other, lb], pick, preferred_element_type=F32)
        rep = jnp.zeros((8, 4 * OV), F32)
        for r in range(ROWS):
            rep = rep + jnp.where(src_row == r, wgt, 0.0) * cols[8 * r : 8 * r + 8, :]
        rep = rep[:, :OV] + rep[:, OV : 2 * OV] + rep[:, 2 * OV : 3 * OV] + rep[:, 3 * OV :]
        spread = jnp.where(in_row, jnp.concatenate([rep] * ROWS, axis=0), 0.0)
        values = None
        for part in split3(spread):
            value = lax.dot_general(part, place, nt, preferred_element_type=F32)
            values = value if values is None else values + value
        joined.append(jnp.where(covered, values, rhs_ref[lb]))
    levels = jnp.concatenate(
        [jnp.concatenate([joined[lb][8 * r : 8 * r + 8] for lb in range(G)], axis=0) for r in range(ROWS)], axis=1
    )
    modal = jnp.dot(proj_ref[...], levels, precision=lax.Precision.HIGHEST, preferred_element_type=F32)
    for lb in range(G):
        for r in range(ROWS):
            tile = modal[8 * lb : 8 * lb + 8, COLS * r : COLS * r + COLS]
            b_ref[lb, 8 * r : 8 * r + 8, :] = tile
            if r < 3:
                top_ref[lb, 8 * r : 8 * r + 8, :] = tile
            if r >= ROWS - 3:
                s = r - (ROWS - 3)
                bottom_ref[lb, 8 * s : 8 * s + 8, :] = tile


def margin(rhs, both, cells, source, weight, proj):
    return pl.pallas_call(
        margin_kernel,
        out_shape=[
            jax.ShapeDtypeStruct((G, 128, COLS), F32),
            jax.ShapeDtypeStruct((G, 24, COLS), F32),
            jax.ShapeDtypeStruct((G, 24, COLS), F32),
        ],
        compiler_params=params(),
        name="margin",
    )(rhs, both, cells, source, weight, proj)


def pack_columns_kernel(b_ref, north_ref, south_ref, out_ref):
    lane = lane_iota((8, COLS))
    for lb in range(G):
        acc = jnp.zeros((8, COLS), F32)
        for i in range(20):
            j = i - 2
            if j < 0:
                row = north_ref[lb, 8 * (j + 3) : 8 * (j + 3) + 8, :]
            elif j >= ROWS:
                row = south_ref[lb, 8 * (j - ROWS) : 8 * (j - ROWS) + 8, :]
            else:
                row = b_ref[lb, 8 * j : 8 * j + 8, :]
            here = ((lane - 6 * i + 3) & 127) < 6
            acc = jnp.where(here, roll_lanes(row, 6 * i), acc)
        out_ref[lb] = acc


def pack_columns(b, north, south):
    return pl.pallas_call(
        pack_columns_kernel,
        out_shape=jax.ShapeDtypeStruct((G, 8, COLS), F32),
        compiler_params=params(),
        name="pack_columns",
    )(b, north, south)


def images_kernel(shift_ref, b_ref, north_ref, south_ref, fwest_ref, feast_ref, c_ref, u1_ref, u2_ref, s_ref):
    lat, lon = lax.axis_index("lat"), lax.axis_index("lon")
    one = jnp.float32(1.0)
    zero = jnp.float32(0.0)
    has_n = jnp.where(lat > 0, one, zero)
    has_s = jnp.where(lat < lax.axis_size("lat") - 1, one, zero)
    has_w = jnp.where(lon > 0, one, zero)
    has_e = jnp.where(lon < lax.axis_size("lon") - 1, one, zero)
    lane = lane_iota((8, COLS))
    first, last = lane == 0, lane == COLS - 1
    side = jnp.where(lane < 64, has_e, has_w)
    from_east = ((lane % 6) < 3) & (lane < 120)

    def line(main, ext):
        return roll_lanes(jnp.where(last, ext, main), 1) + roll_lanes(jnp.where(first, ext, main), -1)

    def row_scale(j):
        return has_n if j < 0 else has_s if j >= ROWS else None

    sums_out = jnp.zeros((8, COLS), F32)
    for lb in range(G):
        diag = lane_iota((8, LEV)) == (lax.broadcasted_iota(jnp.int32, (8, LEV), 0) + 8 * lb)
        a = 4.0 + jnp.sum(jnp.where(diag, jnp.broadcast_to(shift_ref[...], (8, LEV)), 0.0), axis=1, keepdims=True)
        a = jnp.broadcast_to(a, (8, COLS))
        packed = jnp.where(from_east, feast_ref[lb], fwest_ref[lb])

        def b_main(j):
            if j < 0:
                return north_ref[lb, 8 * (j + 3) : 8 * (j + 3) + 8, :]
            if j >= ROWS:
                return south_ref[lb, 8 * (j - ROWS) : 8 * (j - ROWS) + 8, :]
            return b_ref[lb, 8 * j : 8 * j + 8, :]

        bm = {j: b_main(j) for j in (-3, -2)}
        bx = {-2: packed}
        cm, cx, um, ux = {}, {}, {}, {}
        sums = [jnp.zeros((8, COLS), F32) for _ in range(8)]
        for j in range(-2, ROWS + 4):
            if j <= ROWS + 1:
                bm[j + 1] = b_main(j + 1)
                if j + 1 <= ROWS + 1:
                    bx[j + 1] = roll_lanes(packed, -6 * (j + 3))
                value = a * bm[j] - (bm[j - 1] + bm[j + 1] + line(bm[j], bx[j]))
                scale = row_scale(j)
                cm[j] = value if scale is None else value * scale
                if -1 <= j <= ROWS:
                    value = (a * bx[j] - (bx[j - 1] + bx[j + 1] + line(bx[j], bm[j]))) * side
                    cx[j] = value if scale is None else value * scale
                if 0 <= j < ROWS:
                    c_ref[lb, 8 * j : 8 * j + 8, :] = cm[j]
            i = j - 1
            if -1 <= i <= ROWS:
                value = 0.25 * (cm[i - 1] + cm[i + 1] + line(cm[i], cx[i]))
                scale = row_scale(i)
                um[i] = value if scale is None else value * scale
                if 0 <= i < ROWS:
                    ux[i] = 0.25 * (cx[i - 1] + cx[i + 1] + line(cx[i], cm[i])) * side
                    u1_ref[lb, 8 * i : 8 * i + 8, :] = um[i]
            i = j - 2
            if 0 <= i < ROWS:
                u2 = 0.5 * (um[i - 1] + um[i + 1] + line(um[i], ux[i])) - cm[i]
                u2_ref[lb, 8 * i : 8 * i + 8, :] = u2
                b, c, u1 = b_main(i), cm[i], um[i]
                pairs = ((b, c), (b, u1), (b, u2), (c, c), (c, u1), (u1, u1), (u1, u2), (u2, u2))
                sums = [s + x * y for s, (x, y) in zip(sums, pairs)]
        for q in range(8):
            total = jnp.sum(sums[q], axis=1, keepdims=True)
            sums_out = jnp.where(lane == 8 * lb + q, total, sums_out)
    for n in range(s_ref.shape[0]):
        s_ref[n] = sums_out


def images(mode_shift, b, north, south, from_west, from_east, copies):
    full = jax.ShapeDtypeStruct((G, 128, COLS), F32)
    return pl.pallas_call(
        images_kernel,
        out_shape=[full, full, full, jax.ShapeDtypeStruct((copies, 8, COLS), F32)],
        compiler_params=params(),
        name="images",
    )(mode_shift, b, north, south, from_west, from_east)


def sum_copies(ref):
    parts = [ref[n] for n in range(ref.shape[0])]
    while len(parts) > 1:
        parts = [parts[n] + parts[n + 1] for n in range(0, len(parts), 2)]
    return parts[0]


def iterate_kernel(shift_ref, s_ref, b_ref, c_ref, u1_ref, u2_ref, sol_ref, res_ref):
    lane = lane_iota((8, COLS))
    sums = sum_copies(s_ref)
    for lb in range(G):
        diag = lane_iota((8, LEV)) == (lax.broadcasted_iota(jnp.int32, (8, LEV), 0) + 8 * lb)
        a = 4.0 + jnp.sum(jnp.where(diag, jnp.broadcast_to(shift_ref[...], (8, LEV)), 0.0), axis=1, keepdims=True)
        a = jnp.broadcast_to(a, (8, COLS))

        def inner(q):
            value = jnp.sum(jnp.where(lane == 8 * lb + q, sums, 0.0), axis=1, keepdims=True)
            return jnp.broadcast_to(value, (8, COLS))

        bc, bu1, bu2, cc, cu1, u1u1, u1u2, u2u2 = [inner(q) for q in range(8)]
        cu2 = 2.0 * u1u1 - cc
        l10 = cu1 / cc
        l20 = cu2 / cc
        d1 = u1u1 - l10 * cu1
        e1 = u1u2 - l10 * cu2
        l21 = e1 / d1
        d2 = u2u2 - l20 * cu2 - l21 * e1
        z0 = bc
        z1 = bu1 - l10 * z0
        z2 = bu2 - l20 * z0 - l21 * z1
        y2 = z2 / d2
        y1 = z1 / d1 - l21 * y2
        y0 = z0 / cc - l10 * y1 - l20 * y2
        for r in range(ROWS):
            rows = slice(8 * r, 8 * r + 8)
            b, c, u1, u2 = b_ref[lb, rows, :], c_ref[lb, rows, :], u1_ref[lb, rows, :], u2_ref[lb, rows, :]
            v1 = 0.25 * (a * b - c)
            v2 = 0.5 * (a * v1 - u1) - b
            at = pl.ds(lb * 128 + r, 8, stride=ROWS)
            sol_ref[at, :] = y0 * b + y1 * v1 + y2 * v2
            res_ref[at, :] = b - y0 * c - y1 * u1 - y2 * u2


def iterate(mode_shift, sums, b, c, u1, u2):
    out = jax.ShapeDtypeStruct((LEV * ROWS, COLS), F32)
    return pl.pallas_call(
        iterate_kernel,
        out_shape=[out, out],
        compiler_params=params(),
        name="iterate",
    )(mode_shift, sums, b, c, u1, u2)


def send(block, axis, by):
    count = lax.axis_size(axis)
    return lax.ppermute(block, axis, [(i, i + by) for i in range(count) if 0 <= i + by < count])


def relay_kernel(in_ref, out_ref):
    total = sum_copies(in_ref)
    for n in range(out_ref.shape[0]):
        out_ref[n] = total


def relay(parts, copies):
    return pl.pallas_call(
        relay_kernel,
        out_shape=jax.ShapeDtypeStruct((copies, 8, COLS), F32),
        compiler_params=params(),
        name="relay",
    )(parts)


def per_device(fields, frac, shift, mix, proj, mode_shift, cells, source, weight):
    fields = fields[0]
    west, east = pack(shift[0], fields)
    west = send(west, "lon", 1)
    east = send(east, "lon", -1)
    adv, rhs, half = advect(mix, shift[0], frac[0], fields, west, east)
    both = lax.all_gather(half, "panel")
    b, top, bottom = margin(rhs, both, cells[0], source[0, 0].T, weight[0, 0].T, proj)
    north = send(bottom, "lat", 1)
    south = send(top, "lat", -1)
    columns = pack_columns(b, north, south)
    from_west = send(columns, "lon", 1)
    from_east = send(columns, "lon", -1)
    shifts = mode_shift.reshape(1, LEV)
    count = lax.axis_size("lon")
    rest = lax.axis_size("panel") * lax.axis_size("lat")
    c, u1, u2, sums = images(shifts, b, north, south, from_west, from_east, count)
    sums = relay(lax.all_to_all(sums, "lon", 0, 0), rest)
    sums = lax.all_to_all(sums, ("panel", "lat"), 0, 0)
    sol, res = iterate(shifts, sums, b, c, u1, u2)
    shape = (1, LEV, ROWS, COLS)
    return adv[None], sol.reshape(shape), res.reshape(shape)


def solution(mesh):
    wide = P("panel", None, None, "lat", "lon")
    flat = P("panel", None, "lat", "lon")
    table = P("panel", "lat", "lon", None)
    in_specs = (wide, flat, P("panel", "lat", None), P(), P(), P(), P("panel", "lat", "lon"), table, table)
    return jax.shard_map(per_device, mesh=mesh, in_specs=in_specs, out_specs=(wide, flat, flat), check_vma=False)
```

```python
import jax
import jax.numpy as jnp
from jax import lax
from jax.experimental import pallas as pl
from jax.experimental.pallas import tpu as pltpu
from jax.sharding import PartitionSpec as P

F32 = jnp.float32
BF16 = jnp.bfloat16
NF = 6
LEV = 24
ROWS = 16
COLS = 128
G = 3
OV = 256
VMEM_LIMIT = 48 * 1024 * 1024


def lane_iota(shape):
    return lax.broadcasted_iota(jnp.int32, shape, len(shape) - 1)


def roll_lanes(x, by):
    by = by % COLS
    if by == 0:
        return x
    return pltpu.roll(x, by, x.ndim - 1)


def params():
    return pltpu.CompilerParams(vmem_limit_bytes=VMEM_LIMIT)


def own_shift(shift_ref, lon):
    table = shift_ref[...]
    own = jnp.sum(jnp.where(lane_iota(table.shape) == lon, table, 0), axis=1, keepdims=True)
    return jnp.broadcast_to(own, (ROWS, COLS))


def half_mask(mask):
    return jnp.where(mask, 1, 0).astype(jnp.int16) == jnp.int16(1)


def lane_matrix(rule):
    source = lax.broadcasted_iota(jnp.int32, (COLS, COLS), 0)
    target = lax.broadcasted_iota(jnp.int32, (COLS, COLS), 1)
    return jnp.where(rule(source, target), 1.0, 0.0).astype(BF16)


def mirrored(source, target):
    return (target >= 32) & (source == jnp.where((target >> 5) == 2, target, (target + 64) & (COLS - 1)))


def pack_east_kernel(fields_ref, out_ref):
    lane = lane_iota((ROWS, COLS))
    acc = jnp.zeros((ROWS, COLS), F32)
    for f in range(NF):
        for l8 in range(8):
            i = f * 8 + l8
            x = roll_lanes(fields_ref[f, l8].astype(F32), 2 * i)
            acc = jnp.where((lane >> 1) == i, x, acc)
    out_ref[0] = acc.astype(BF16)


def pack_east(fields):
    return pl.pallas_call(
        pack_east_kernel,
        grid=(G,),
        in_specs=[pl.BlockSpec((NF, 8, ROWS, COLS), lambda g: (0, g, 0, 0))],
        out_specs=pl.BlockSpec((1, ROWS, COLS), lambda g: (g, 0, 0)),
        out_shape=jax.ShapeDtypeStruct((G, ROWS, COLS), BF16),
        compiler_params=params(),
        name="pack_east",
    )(fields)


def pack_kernel(shift_ref, fields_ref, west_ref, scratch):
    shift = own_shift(shift_ref, lax.axis_index("lon") + 1)
    lane = lane_iota((ROWS, COLS))
    low = (lax.broadcasted_iota(jnp.int32, (ROWS, COLS), 0) & 1) == 0
    block = lane >= COLS - 32 * shift
    single = lane == COLS - 1 - 32 * shift
    masks = [half_mask(m & row) for row in (low, ~low) for m in (block, single)]
    matrix = jnp.concatenate(
        [
            lane_matrix(lambda s, t: s == t),
            lane_matrix(lambda s, t: ((s & 31) == 31) & (t == 31)),
            lane_matrix(mirrored),
            lane_matrix(lambda s, t: ((s & 31) == 31) & (t == 30)),
        ],
        axis=0,
    )
    zero = jnp.zeros((ROWS, COLS), BF16)
    for l8 in range(8):
        parts = [
            jnp.concatenate([jnp.where(m, fields_ref[f, l8], zero) for m in masks], axis=1) for f in range(NF)
        ]
        scratch[l8] = jnp.dot(jnp.concatenate(parts, axis=0), matrix, preferred_element_type=F32)
        pairs = scratch[l8, pl.ds(0, 8 * NF, stride=2), :] + scratch[l8, pl.ds(1, 8 * NF, stride=2), :]
        pairs = pairs.astype(BF16)
        for n in range(NF // 2):
            west_ref[n, l8] = pairs[ROWS * n : ROWS * n + ROWS]


def pack(shift, fields):
    return pl.pallas_call(
        pack_kernel,
        grid=(G,),
        in_specs=[
            pl.BlockSpec((ROWS, 32), lambda g: (0, 0)),
            pl.BlockSpec((NF, 8, ROWS, COLS), lambda g: (0, g, 0, 0)),
        ],
        out_specs=pl.BlockSpec((NF // 2, 8, ROWS, COLS), lambda g: (0, g, 0, 0)),
        out_shape=jax.ShapeDtypeStruct((NF // 2, LEV, ROWS, COLS), BF16),
        scratch_shapes=[pltpu.VMEM((8, NF * ROWS, COLS), F32)],
        compiler_params=params(),
        name="pack",
    )(shift, fields)


def advect_kernel(mix_ref, shift_ref, frac_ref, fields_ref, west_ref, east_ref, adv_ref, rhs_ref, half_ref, scratch):
    g = pl.program_id(0)
    shift = own_shift(shift_ref, lax.axis_index("lon"))
    lane = lane_iota((ROWS, COLS))
    low = (lax.broadcasted_iota(jnp.int32, (ROWS, COLS), 0) & 1) == 0
    swap16 = half_mask(~low & ((lane >> 5) != 2))
    single16 = half_mask(lane == jnp.where(low, 31, 30))
    single_at = jnp.concatenate([lane == ((COLS - 32 * shift) & (COLS - 1))] * NF, axis=0)
    single_to = lane_matrix(lambda s, t: ((s == 30) | (s == 31)) & ((t & 31) == 0))
    zero = jnp.zeros((ROWS, COLS), BF16)
    odd, two = (shift & 1) == 1, (shift & 2) == 2
    odd16, two16 = half_mask(odd), half_mask(two)
    edge16 = half_mask(lane < 2)

    def turn(x, sign, odd, two):
        x = jnp.where(odd, roll_lanes(x, 32 * sign), x)
        return jnp.where(two, roll_lanes(x, 64), x)

    def beyond(j):
        at = ((lane - j + 32 * shift) & (COLS - 1)) - 32 * shift + j
        return (at < 0) | (at >= COLS)

    taps = (-1, 0, 1, 2)
    masks = [half_mask(beyond(j)) for j in taps]
    shifts = [lane_matrix(lambda s, t, j=j: s == ((t + j) & (COLS - 1))) for j in taps]
    east = east_ref[0]
    for l8 in range(8):
        t = turn(frac_ref[l8], -1, odd, two)
        tm1, tm2, tp1 = t - 1.0, t - 2.0, t + 1.0
        weights = (
            -t * tm1 * tm2 * (1.0 / 6.0),
            tp1 * tm1 * tm2 * 0.5,
            -tp1 * t * tm2 * 0.5,
            tp1 * t * tm1 * (1.0 / 6.0),
        )
        shared = jnp.concatenate([west_ref[n, l8] for n in range(NF // 2)], axis=0).astype(F32)
        scratch[l8, pl.ds(0, 8 * NF, stride=2), :] = shared
        scratch[l8, pl.ds(1, 8 * NF, stride=2), :] = shared
        west = scratch[l8].astype(BF16)
        chosen = [[] for _ in taps]
        singles = []
        for f in range(NF):
            other = west[ROWS * f : ROWS * f + ROWS]
            singles.append(jnp.where(single16, other, zero))
            other = jnp.where(swap16, roll_lanes(other, 64), other)
            other = jnp.where(edge16, roll_lanes(east, -2 * (f * 8 + l8)), other)
            for n, mask in enumerate(masks):
                chosen[n].append(jnp.where(mask, other, fields_ref[f, l8]))
        moved = []
        for j, parts, matrix in zip(taps, chosen, shifts):
            if j == 0:
                moved.append([part.astype(F32) for part in parts])
            else:
                wide = jnp.dot(jnp.concatenate(parts, axis=0), matrix, preferred_element_type=F32)
                if j == -1:
                    column = jnp.dot(jnp.concatenate(singles, axis=0), single_to, preferred_element_type=F32)
                    wide = jnp.where(single_at, column, wide)
                moved.append([wide[ROWS * f : ROWS * f + ROWS] for f in range(NF)])
        total = jnp.zeros((ROWS, COLS), F32)
        for f in range(NF):
            acc = weights[0] * moved[0][f]
            for n in range(1, 4):
                acc = acc + weights[n] * moved[n][f]
            rounded = acc.astype(BF16)
            adv_ref[f, l8] = turn(rounded, 1, odd16, two16)
            total = total + mix_ref[f, g * 8 + l8] * rounded.astype(F32)
        rhs_ref[0, pl.ds(l8, ROWS, stride=8), :] = turn(total, 1, odd, two)
    half_ref[0] = rhs_ref[0].astype(BF16)


def advect(mix, shift, frac, fields, west, east):
    block = pl.BlockSpec((NF, 8, ROWS, COLS), lambda g: (0, g, 0, 0))
    group = pl.BlockSpec((1, 128, COLS), lambda g: (g, 0, 0))
    return pl.pallas_call(
        advect_kernel,
        grid=(G,),
        in_specs=[
            pl.BlockSpec(memory_space=pltpu.SMEM),
            pl.BlockSpec((ROWS, 32), lambda g: (0, 0)),
            pl.BlockSpec((8, ROWS, COLS), lambda g: (g, 0, 0)),
            block,
            pl.BlockSpec((NF // 2, 8, ROWS, COLS), lambda g: (0, g, 0, 0)),
            pl.BlockSpec((1, ROWS, COLS), lambda g: (g, 0, 0)),
        ],
        out_specs=[block, group, group],
        out_shape=[
            jax.ShapeDtypeStruct((NF, LEV, ROWS, COLS), BF16),
            jax.ShapeDtypeStruct((G, 128, COLS), F32),
            jax.ShapeDtypeStruct((G, 128, COLS), BF16),
        ],
        scratch_shapes=[pltpu.VMEM((8, NF * ROWS, COLS), F32)],
        compiler_params=params(),
        name="advect",
    )(mix, shift, frac, fields, west, east)


SLOTS = 20


def slot_of_lane():
    return ((lane_iota((8, COLS)) + 3) & (COLS - 1)) // 6


def split3(x):
    a = x.astype(BF16)
    rest = x - a.astype(F32)
    b = rest.astype(BF16)
    c = (rest - b.astype(F32)).astype(BF16)
    return a, b, c


def tables_kernel(
    cells_ref, source_ref, weight_ref, proj_ref, pick_ref, place_ref, in_row_ref, covered_ref, src_row_ref, wgt_ref, proj_out_ref
):
    proj_out_ref[...] = proj_ref[...]
    src = jnp.concatenate([source_ref[q : q + 1, :] for q in range(4)], axis=1)
    wgt = jnp.concatenate([weight_ref[q : q + 1, :] for q in range(4)], axis=1)
    wide = (COLS, 4 * OV)
    col = jnp.broadcast_to(src & (COLS - 1), wide)
    pick_ref[...] = jnp.where(lax.broadcasted_iota(jnp.int32, wide, 0) == col, 1.0, 0.0).astype(BF16)
    src_row_ref[...] = jnp.broadcast_to(src >> 7, (8, 4 * OV))
    wgt_ref[...] = jnp.broadcast_to(wgt, (8, 4 * OV))
    cells = cells_ref[...]
    sub = lax.broadcasted_iota(jnp.int32, (128, OV), 0)
    place = jnp.where(sub == jnp.broadcast_to(cells & (COLS - 1), (128, OV)), 1.0, 0.0).astype(BF16)
    place_ref[...] = place
    in_row = jnp.where((sub >> 3) == jnp.broadcast_to(cells >> 7, (128, OV)), 1.0, 0.0).astype(BF16)
    in_row_ref[...] = in_row
    nt = (((1,), (1,)), ((), ()))
    covered_ref[...] = lax.dot_general(in_row, place, nt, preferred_element_type=F32)


def tables(cells, source, weight, proj):
    return pl.pallas_call(
        tables_kernel,
        out_shape=[
            jax.ShapeDtypeStruct((COLS, 4 * OV), BF16),
            jax.ShapeDtypeStruct((128, OV), BF16),
            jax.ShapeDtypeStruct((128, OV), BF16),
            jax.ShapeDtypeStruct((128, COLS), F32),
            jax.ShapeDtypeStruct((8, 4 * OV), jnp.int32),
            jax.ShapeDtypeStruct((8, 4 * OV), F32),
            jax.ShapeDtypeStruct((LEV, LEV), F32),
        ],
        compiler_params=params(),
        cost_estimate=pl.CostEstimate(flops=4_000_000, bytes_accessed=500_000, transcendentals=0),
        name="tables",
    )(cells, source, weight, proj)


def margin_kernel(
    rhs_ref, both_ref, pick_ref, place_ref, in_row_ref, covered_ref, src_row_ref, wgt_ref, proj_ref, b_ref, slots_ref
):
    other = 1 - lax.axis_index("panel")
    pick, place = pick_ref[...], place_ref[...]
    src_row, wgt = src_row_ref[...], wgt_ref[...]
    in_row = in_row_ref[...].astype(F32)
    covered = covered_ref[...] > 0.5
    nt = (((1,), (1,)), ((), ()))
    joined = []
    for lb in range(G):
        cols = jnp.dot(both_ref[other, lb], pick, preferred_element_type=F32)
        rep = jnp.zeros((8, 4 * OV), F32)
        for r in range(ROWS):
            rep = rep + jnp.where(src_row == r, wgt, 0.0) * cols[8 * r : 8 * r + 8, :]
        rep = rep[:, :OV] + rep[:, OV : 2 * OV] + rep[:, 2 * OV : 3 * OV] + rep[:, 3 * OV :]
        spread = in_row * jnp.concatenate([rep] * ROWS, axis=0)
        values = None
        for part in split3(spread):
            value = lax.dot_general(part, place, nt, preferred_element_type=F32)
            values = value if values is None else values + value
        joined.append(jnp.where(covered, values, rhs_ref[lb]))
    levels = jnp.concatenate(
        [jnp.concatenate([joined[lb][8 * r : 8 * r + 8] for lb in range(G)], axis=0) for r in range(ROWS)], axis=1
    )
    modal = jnp.dot(proj_ref[...], levels, precision=lax.Precision.HIGHEST, preferred_element_type=F32)
    for lb in range(G):
        for r in range(ROWS):
            tile = modal[8 * lb : 8 * lb + 8, COLS * r : COLS * r + COLS]
            b_ref[lb, 8 * r : 8 * r + 8, :] = tile
    lat, lon = lax.axis_index("lat"), lax.axis_index("lon")
    place_in_square = 2 * (lat & 1) + (lon & 1)
    for lb in range(G):
        slots_ref[place_in_square ^ 2, lb] = b_ref[lb, pl.ds(pl.multiple_of(8 * 13 * (1 - (lat & 1)), 8), 24), :]
        acc = jnp.zeros((8, COLS), F32)
        for i in range(SLOTS):
            r = (i - 2) % ROWS
            acc = jnp.where(slot_of_lane() == i, roll_lanes(b_ref[lb, 8 * r : 8 * r + 8, :], 6 * i), acc)
        slots_ref[place_in_square ^ 1, lb, 0:8, :] = acc
        slots_ref[place_in_square ^ 3, lb, 0:8, :] = acc


def margin(rhs, both, lists):
    return pl.pallas_call(
        margin_kernel,
        out_shape=[
            jax.ShapeDtypeStruct((G, 128, COLS), F32),
            jax.ShapeDtypeStruct((4, G, 24, COLS), F32),
        ],
        compiler_params=params(),
        name="margin",
    )(rhs, both, *lists)


def second_kernel(b_ref, first_ref, got_ref, out_ref):
    lat, lon = lax.axis_index("lat"), lax.axis_index("lon")
    here = 2 * (lat & 1) + (lon & 1)
    there = 3 - here
    even = jnp.broadcast_to(lat & 1, (8, COLS)) == 0
    slot = slot_of_lane()
    for lb in range(G):
        out_ref[there ^ 2, lb, 0:24, :] = b_ref[lb, pl.ds(pl.multiple_of(8 * 13 * (lat & 1), 8), 24), :]
        out_ref[there ^ 2, lb, 24:32, :] = got_ref[here ^ 1, lb, 0:8, :]
        own = first_ref[here ^ 1, lb, 0:8, :]
        out_ref[there ^ 3, lb, 24:32, :] = own
        row = [got_ref[here ^ 2, lb, 8 * n : 8 * n + 8, :] for n in range(3)]
        with_south = jnp.where(slot == 18, roll_lanes(row[0], 6 * 18), jnp.where(slot == 19, roll_lanes(row[1], 6 * 19), own))
        with_north = jnp.where(slot == 0, row[1], jnp.where(slot == 1, roll_lanes(row[2], 6), own))
        out_ref[there ^ 1, lb, 24:32, :] = jnp.where(even, with_south, with_north)


def second(b, first, got):
    return pl.pallas_call(
        second_kernel,
        out_shape=jax.ShapeDtypeStruct((4, G, 32, COLS), F32),
        compiler_params=params(),
        name="second",
    )(b, first, got)


def images_kernel(shift_ref, b_ref, first_ref, second_ref, c_ref, u1_ref, u2_ref, s_ref):
    lat, lon = lax.axis_index("lat"), lax.axis_index("lon")
    one = jnp.float32(1.0)
    zero = jnp.float32(0.0)
    has_n = jnp.where(lat > 0, one, zero)
    has_s = jnp.where(lat < lax.axis_size("lat") - 1, one, zero)
    has_w = jnp.where(lon > 0, one, zero)
    has_e = jnp.where(lon < lax.axis_size("lon") - 1, one, zero)
    lane = lane_iota((8, COLS))
    first, last = lane == 0, lane == COLS - 1
    side = jnp.where(lane < 64, has_e, has_w)
    here = 2 * (lat & 1) + (lon & 1)
    there = 3 - here
    lat_even = jnp.broadcast_to(lat & 1, (8, COLS)) == 0
    slot = slot_of_lane()
    from_east = ((lane % 6) < 3) & (lane < 120)
    north_slot, south_slot = slot < 2, (slot == 18) | (slot == 19)
    inside = jnp.where(from_east, has_e, has_w)
    inside = jnp.where(north_slot, inside * has_n, jnp.where(south_slot, inside * has_s, inside)) > 0.5
    first_side = (lat_even & south_slot) | (~lat_even & north_slot)
    second_side = (lat_even & north_slot) | (~lat_even & south_slot)
    east_first = jnp.where(from_east, 1, 0) == jnp.broadcast_to(1 - (lon & 1), (8, COLS))

    def line(main, ext):
        return roll_lanes(jnp.where(last, ext, main), 1) + roll_lanes(jnp.where(first, ext, main), -1)

    def row_scale(j):
        return has_n if j < 0 else has_s if j >= ROWS else None

    sums_out = jnp.zeros((8, COLS), F32)
    for lb in range(G):
        diag = lane_iota((8, LEV)) == (lax.broadcasted_iota(jnp.int32, (8, LEV), 0) + 8 * lb)
        a = 4.0 + jnp.sum(jnp.where(diag, jnp.broadcast_to(shift_ref[...], (8, LEV)), 0.0), axis=1, keepdims=True)
        a = jnp.broadcast_to(a, (8, COLS))
        near = jnp.where(first_side, first_ref[here ^ 3, lb, 0:8, :], first_ref[here ^ 1, lb, 0:8, :])
        near = jnp.where(second_side, second_ref[there ^ 2, lb, 24:32, :], near)
        far = jnp.where(second_side, second_ref[there ^ 3, lb, 24:32, :], second_ref[there ^ 1, lb, 24:32, :])
        packed = jnp.where(inside, jnp.where(east_first, near, far), 0.0)

        def b_main(j):
            if 0 <= j < ROWS:
                return b_ref[lb, 8 * j : 8 * j + 8, :]
            n = j + 3 if j < 0 else j - ROWS
            rows = slice(8 * n, 8 * n + 8)
            one, two = first_ref[here ^ 2, lb, rows, :], second_ref[there ^ 2, lb, rows, :]
            if j < 0:
                return jnp.where(has_n > 0.5, jnp.where(lat_even, two, one), 0.0)
            return jnp.where(has_s > 0.5, jnp.where(lat_even, one, two), 0.0)

        bm = {j: b_main(j) for j in (-3, -2)}
        bx = {-2: packed}
        cm, cx, um, ux = {}, {}, {}, {}
        sums = [jnp.zeros((8, COLS), F32) for _ in range(8)]
        for j in range(-2, ROWS + 4):
            if j <= ROWS + 1:
                bm[j + 1] = b_main(j + 1)
                if j + 1 <= ROWS + 1:
                    bx[j + 1] = roll_lanes(packed, -6 * (j + 3))
                value = a * bm[j] - (bm[j - 1] + bm[j + 1] + line(bm[j], bx[j]))
                scale = row_scale(j)
                cm[j] = value if scale is None else value * scale
                if -1 <= j <= ROWS:
                    value = (a * bx[j] - (bx[j - 1] + bx[j + 1] + line(bx[j], bm[j]))) * side
                    cx[j] = value if scale is None else value * scale
                if 0 <= j < ROWS:
                    c_ref[lb, 8 * j : 8 * j + 8, :] = cm[j]
            i = j - 1
            if -1 <= i <= ROWS:
                value = 0.25 * (cm[i - 1] + cm[i + 1] + line(cm[i], cx[i]))
                scale = row_scale(i)
                um[i] = value if scale is None else value * scale
                if 0 <= i < ROWS:
                    ux[i] = 0.25 * (cx[i - 1] + cx[i + 1] + line(cx[i], cm[i])) * side
                    u1_ref[lb, 8 * i : 8 * i + 8, :] = um[i]
            i = j - 2
            if 0 <= i < ROWS:
                u2 = 0.5 * (um[i - 1] + um[i + 1] + line(um[i], ux[i])) - cm[i]
                u2_ref[lb, 8 * i : 8 * i + 8, :] = u2
                b, c, u1 = b_main(i), cm[i], um[i]
                pairs = ((b, c), (b, u1), (b, u2), (c, c), (c, u1), (u1, u1), (u1, u2), (u2, u2))
                sums = [s + x * y for s, (x, y) in zip(sums, pairs)]
        for q in range(8):
            total = jnp.sum(sums[q], axis=1, keepdims=True)
            sums_out = jnp.where(lane == 8 * lb + q, total, sums_out)
    sub = lax.broadcasted_iota(jnp.int32, (8, COLS), 0)
    spread = jnp.zeros((8, COLS), F32)
    for m in range(4):
        spread = jnp.where((sub & 3) == m, roll_lanes(sums_out, 32 * m), spread)
    folded = jnp.concatenate([jnp.sum(spread[4 * h : 4 * h + 4], axis=0, keepdims=True) for h in range(2)], axis=0)
    for n in range(s_ref.shape[0]):
        s_ref[n] = folded


def images(mode_shift, b, got_first, got_second, copies):
    full = jax.ShapeDtypeStruct((G, 128, COLS), F32)
    return pl.pallas_call(
        images_kernel,
        out_shape=[full, full, full, jax.ShapeDtypeStruct((copies, 2, COLS), F32)],
        compiler_params=params(),
        name="images",
    )(mode_shift, b, got_first, got_second)


def sum_copies(ref):
    parts = [ref[n] for n in range(ref.shape[0])]
    while len(parts) > 1:
        parts = [parts[n] + parts[n + 1] for n in range(0, len(parts), 2)]
    return parts[0]


def iterate_kernel(shift_ref, s_ref, b_ref, c_ref, u1_ref, u2_ref, sol_ref, res_ref):
    lane = lane_iota((8, COLS))
    total = sum_copies(s_ref)
    sub = lax.broadcasted_iota(jnp.int32, (8, COLS), 0)
    rows = jnp.where(sub < 4, jnp.broadcast_to(total[0:1], (8, COLS)), jnp.broadcast_to(total[1:2], (8, COLS)))
    sums = rows
    for m in range(1, 4):
        sums = jnp.where((sub & 3) == m, roll_lanes(rows, -32 * m), sums)
    for lb in range(G):
        diag = lane_iota((8, LEV)) == (lax.broadcasted_iota(jnp.int32, (8, LEV), 0) + 8 * lb)
        a = 4.0 + jnp.sum(jnp.where(diag, jnp.broadcast_to(shift_ref[...], (8, LEV)), 0.0), axis=1, keepdims=True)
        a = jnp.broadcast_to(a, (8, COLS))

        def inner(q):
            value = jnp.sum(jnp.where(lane == 8 * lb + q, sums, 0.0), axis=1, keepdims=True)
            return jnp.broadcast_to(value, (8, COLS))

        bc, bu1, bu2, cc, cu1, u1u1, u1u2, u2u2 = [inner(q) for q in range(8)]
        cu2 = 2.0 * u1u1 - cc
        l10 = cu1 / cc
        l20 = cu2 / cc
        d1 = u1u1 - l10 * cu1
        e1 = u1u2 - l10 * cu2
        l21 = e1 / d1
        d2 = u2u2 - l20 * cu2 - l21 * e1
        z0 = bc
        z1 = bu1 - l10 * z0
        z2 = bu2 - l20 * z0 - l21 * z1
        y2 = z2 / d2
        y1 = z1 / d1 - l21 * y2
        y0 = z0 / cc - l10 * y1 - l20 * y2
        for r in range(ROWS):
            rows = slice(8 * r, 8 * r + 8)
            b, c, u1, u2 = b_ref[lb, rows, :], c_ref[lb, rows, :], u1_ref[lb, rows, :], u2_ref[lb, rows, :]
            v1 = 0.25 * (a * b - c)
            v2 = 0.5 * (a * v1 - u1) - b
            at = pl.ds(lb * 128 + r, 8, stride=ROWS)
            sol_ref[at, :] = y0 * b + y1 * v1 + y2 * v2
            res_ref[at, :] = b - y0 * c - y1 * u1 - y2 * u2


def iterate(mode_shift, sums, b, c, u1, u2):
    out = jax.ShapeDtypeStruct((LEV * ROWS, COLS), F32)
    return pl.pallas_call(
        iterate_kernel,
        out_shape=[out, out],
        compiler_params=params(),
        name="iterate",
    )(mode_shift, sums, b, c, u1, u2)


def send(block, axis, by):
    count = lax.axis_size(axis)
    return lax.ppermute(block, axis, [(i, i + by) for i in range(count) if 0 <= i + by < count])


def relay_kernel(in_ref, out_ref):
    total = sum_copies(in_ref)
    for n in range(out_ref.shape[0]):
        out_ref[n] = total


def relay(parts, copies):
    return pl.pallas_call(
        relay_kernel,
        out_shape=jax.ShapeDtypeStruct((copies, 2, COLS), F32),
        compiler_params=params(),
        name="relay",
    )(parts)


def in_squares(slots, begin):
    lats, lons = lax.axis_size("lat"), lax.axis_size("lon")
    groups = [
        [((i + a) % lats) * lons + (j + b) % lons for a in (0, 1) for b in (0, 1)]
        for i in range(begin, lats, 2)
        for j in range(begin, lons, 2)
    ]
    return lax.all_to_all(slots, ("lat", "lon"), 0, 0, axis_index_groups=groups)


def per_device(fields, frac, shift, mix, proj, mode_shift, cells, source, weight):
    fields = fields[0]
    lists = tables(cells[0], source[0, 0].T, weight[0, 0].T, proj)
    east = send(pack_east(fields), "lon", -1)
    west = send(pack(shift[0], fields), "lon", 1)
    adv, rhs, half = advect(mix, shift[0], frac[0], fields, west, east)
    both = lax.all_gather(half, "panel")
    b, first = margin(rhs, both, lists)
    got_first = in_squares(first, 0)
    got_second = in_squares(second(b, first, got_first), 1)
    shifts = mode_shift.reshape(1, LEV)
    count = lax.axis_size("lon")
    rest = lax.axis_size("panel") * lax.axis_size("lat")
    c, u1, u2, sums = images(shifts, b, got_first, got_second, count)
    sums = relay(lax.all_to_all(sums, "lon", 0, 0), rest)
    sums = lax.all_to_all(sums, ("panel", "lat"), 0, 0)
    sol, res = iterate(shifts, sums, b, c, u1, u2)
    shape = (1, LEV, ROWS, COLS)
    return adv[None], sol.reshape(shape), res.reshape(shape)


def solution(mesh):
    wide = P("panel", None, None, "lat", "lon")
    flat = P("panel", None, "lat", "lon")
    table = P("panel", "lat", "lon", None)
    in_specs = (wide, flat, P("panel", "lat", None), P(), P(), P(), P("panel", "lat", "lon"), table, table)
    return jax.shard_map(per_device, mesh=mesh, in_specs=in_specs, out_specs=(wide, flat, flat), check_vma=False)
```

```python
import jax
import jax.numpy as jnp
from jax import lax
from jax.experimental import pallas as pl
from jax.experimental.pallas import tpu as pltpu
from jax.sharding import PartitionSpec as P

F32 = jnp.float32
BF16 = jnp.bfloat16
NF = 6
LEV = 24
ROWS = 16
COLS = 128
G = 3
OV = 256
VMEM_LIMIT = 48 * 1024 * 1024


def lane_iota(shape):
    return lax.broadcasted_iota(jnp.int32, shape, len(shape) - 1)


def roll_lanes(x, by):
    by = by % COLS
    if by == 0:
        return x
    return pltpu.roll(x, by, x.ndim - 1)


def params():
    return pltpu.CompilerParams(vmem_limit_bytes=VMEM_LIMIT)


def own_shift(shift_ref, lon):
    table = shift_ref[...]
    own = jnp.sum(jnp.where(lane_iota(table.shape) == lon, table, 0), axis=1, keepdims=True)
    return jnp.broadcast_to(own, (ROWS, COLS))


def half_bits(mask):
    return jnp.where(mask, 1, 0).astype(jnp.int16)


def lane_matrix(rule):
    source = lax.broadcasted_iota(jnp.int32, (COLS, COLS), 0)
    target = lax.broadcasted_iota(jnp.int32, (COLS, COLS), 1)
    return jnp.where(rule(source, target), 1.0, 0.0).astype(BF16)


def mirrored(source, target):
    return (target >= 32) & (source == jnp.where((target >> 5) == 2, target, (target + 64) & (COLS - 1)))


def pack_east_kernel(fields_ref, out_ref):
    lane = lane_iota((ROWS, COLS))
    acc = jnp.zeros((ROWS, COLS), F32)
    for f in range(NF):
        for l8 in range(8):
            i = f * 8 + l8
            x = roll_lanes(fields_ref[f, l8].astype(F32), 2 * i)
            acc = jnp.where((lane >> 1) == i, x, acc)
    out_ref[0] = acc.astype(BF16)


def pack_east(fields):
    return pl.pallas_call(
        pack_east_kernel,
        grid=(G,),
        in_specs=[pl.BlockSpec((NF, 8, ROWS, COLS), lambda g: (0, g, 0, 0))],
        out_specs=pl.BlockSpec((1, ROWS, COLS), lambda g: (g, 0, 0)),
        out_shape=jax.ShapeDtypeStruct((G, ROWS, COLS), BF16),
        compiler_params=params(),
        name="pack_east",
    )(fields)


def pack_kernel(shift_hbm, fields_hbm, west_ref, kept_ref, shift_ref, scratch, mask_ref, matrix_ref, sems):
    table = pltpu.make_async_copy(shift_hbm, shift_ref, sems.at[G])
    table.start()
    copies = []
    for g in range(G):
        part = (slice(None), pl.ds(8 * g, 8))
        copies.append(pltpu.make_async_copy(fields_hbm.at[part], kept_ref.at[part], sems.at[g]))
        copies[-1].start()
    table.wait()
    pack_plan(shift_ref, mask_ref, matrix_ref)
    masks = [mask_ref[n] == 1 for n in range(4)]
    zero = jnp.zeros((ROWS, COLS), BF16)
    for g in range(G):
        copies[g].wait()
        for l8 in range(8):
            level = 8 * g + l8
            parts = [
                jnp.concatenate([jnp.where(m, kept_ref[f, level], zero) for m in masks], axis=1) for f in range(NF)
            ]
            wide = jnp.dot(jnp.concatenate(parts, axis=0), matrix_ref[...], preferred_element_type=F32)
            scratch[l8] = wide
            pairs = scratch[l8, pl.ds(0, 8 * NF, stride=2), :] + scratch[l8, pl.ds(1, 8 * NF, stride=2), :]
            pairs = pairs.astype(BF16)
            for n in range(NF // 2):
                west_ref[n, level] = pairs[ROWS * n : ROWS * n + ROWS]


def pack_plan(shift_ref, mask_ref, matrix_ref):
    shift = own_shift(shift_ref, lax.axis_index("lon") + 1)
    lane = lane_iota((ROWS, COLS))
    low = (lax.broadcasted_iota(jnp.int32, (ROWS, COLS), 0) & 1) == 0
    block = lane >= COLS - 32 * shift
    single = lane == COLS - 1 - 32 * shift
    for n, mask in enumerate([m & row for row in (low, ~low) for m in (block, single)]):
        mask_ref[n] = half_bits(mask)
    rules = (
        lambda s, t: s == t,
        lambda s, t: ((s & 31) == 31) & (t == 31),
        mirrored,
        lambda s, t: ((s & 31) == 31) & (t == 30),
    )
    for n, rule in enumerate(rules):
        matrix_ref[COLS * n : COLS * n + COLS, :] = lane_matrix(rule)


def pack(shift, fields):
    return pl.pallas_call(
        pack_kernel,
        in_specs=[pl.BlockSpec(memory_space=pltpu.HBM)] * 2,
        out_specs=[pl.BlockSpec(memory_space=pltpu.VMEM)] * 2,
        out_shape=[
            jax.ShapeDtypeStruct((NF // 2, LEV, ROWS, COLS), BF16),
            jax.ShapeDtypeStruct((NF, LEV, ROWS, COLS), BF16),
        ],
        scratch_shapes=[
            pltpu.VMEM((ROWS, 32), jnp.int32),
            pltpu.VMEM((8, NF * ROWS, COLS), F32),
            pltpu.VMEM((4, ROWS, COLS), jnp.int16),
            pltpu.VMEM((4 * COLS, COLS), BF16),
            pltpu.SemaphoreType.DMA((G + 1,)),
        ],
        compiler_params=params(),
        name="pack",
    )(*(pltpu.with_memory_space_constraint(x, pltpu.HBM) for x in (shift, fields)))


TAPS = (-1, 0, 1, 2)


def turn(x, sign, odd, two):
    x = jnp.where(odd, roll_lanes(x, 32 * sign), x)
    return jnp.where(two, roll_lanes(x, 64), x)


def advect_plan(mix_ref, shift_ref, frac_ref, mix_out_ref, mask_ref, shift_out_ref, matrix_ref, weight_ref):
    for f in range(NF):
        for level in range(LEV):
            mix_out_ref[f, level] = jnp.full((8, COLS), mix_ref[f, level], F32)
    shift = own_shift(shift_ref, lax.axis_index("lon"))
    shift_out_ref[...] = shift
    lane = lane_iota((ROWS, COLS))
    low = (lax.broadcasted_iota(jnp.int32, (ROWS, COLS), 0) & 1) == 0
    odd, two = (shift & 1) == 1, (shift & 2) == 2

    def beyond(j):
        at = ((lane - j + 32 * shift) & (COLS - 1)) - 32 * shift + j
        return (at < 0) | (at >= COLS)

    masks = [beyond(j) for j in TAPS]
    masks += [odd, two, lane < 2, ~low & ((lane >> 5) != 2), lane == jnp.where(low, 31, 30)]
    for n, mask in enumerate(masks):
        mask_ref[n] = half_bits(mask)
    rules = [lambda s, t, j=j: s == ((t + j) & (COLS - 1)) for j in TAPS if j]
    rules.append(lambda s, t: ((s == 30) | (s == 31)) & ((t & 31) == 0))
    for n, rule in enumerate(rules):
        matrix_ref[n] = lane_matrix(rule)
    for level in range(LEV):
        t = turn(frac_ref[level], -1, odd, two)
        tm1, tm2, tp1 = t - 1.0, t - 2.0, t + 1.0
        weight_ref[0, level] = -t * tm1 * tm2 * (1.0 / 6.0)
        weight_ref[1, level] = tp1 * tm1 * tm2 * 0.5
        weight_ref[2, level] = -tp1 * t * tm2 * 0.5
        weight_ref[3, level] = tp1 * t * tm1 * (1.0 / 6.0)


def advect_kernel(
    mix_ref, mask_ref, shift_ref, matrix_ref, weight_ref, fields_ref, west_ref, east_ref, adv_ref, rhs_ref, half_ref, scratch
):
    shift = shift_ref[...]
    lane = lane_iota((ROWS, COLS))
    odd, two = (shift & 1) == 1, (shift & 2) == 2
    bits = [mask_ref[n] == 1 for n in range(9)]
    masks, (odd16, two16, edge16, swap16, single16) = bits[:4], bits[4:]
    single_at = jnp.concatenate([lane == ((COLS - 32 * shift) & (COLS - 1))] * NF, axis=0)
    zero = jnp.zeros((ROWS, COLS), BF16)

    @pl.loop(0, G)
    def _(g):
        east = east_ref[g]
        for l8 in range(8):
            level = g * 8 + l8
            shared = jnp.concatenate([west_ref[n, level] for n in range(NF // 2)], axis=0).astype(F32)
            scratch[l8, pl.ds(0, 8 * NF, stride=2), :] = shared
            scratch[l8, pl.ds(1, 8 * NF, stride=2), :] = shared
            west = scratch[l8].astype(BF16)
            chosen = [[] for _ in TAPS]
            singles = []
            for f in range(NF):
                other = west[ROWS * f : ROWS * f + ROWS]
                singles.append(jnp.where(single16, other, zero))
                other = jnp.where(swap16, roll_lanes(other, 64), other)
                other = jnp.where(edge16, roll_lanes(east, -2 * (f * 8 + l8)), other)
                own = fields_ref[f, level]
                for n, mask in enumerate(masks):
                    chosen[n].append(jnp.where(mask, other, own))
            moved = [None] * 4
            moved[1] = [part.astype(F32) for part in chosen[1]]
            for n, tap in ((0, 0), (1, 2), (2, 3)):
                wide = jnp.dot(jnp.concatenate(chosen[tap], axis=0), matrix_ref[n], preferred_element_type=F32)
                if tap == 0:
                    column = jnp.dot(jnp.concatenate(singles, axis=0), matrix_ref[3], preferred_element_type=F32)
                    wide = jnp.where(single_at, column, wide)
                moved[tap] = [wide[ROWS * f : ROWS * f + ROWS] for f in range(NF)]
            weights = [weight_ref[n, level] for n in range(4)]
            total = jnp.zeros((ROWS, COLS), F32)
            for f in range(NF):
                acc = weights[0] * moved[0][f]
                for n in range(1, 4):
                    acc = acc + weights[n] * moved[n][f]
                rounded = acc.astype(BF16)
                adv_ref[f, level] = turn(rounded, 1, odd16, two16)
                mix = mix_ref[f, level]
                total = total + jnp.concatenate([mix, mix], axis=0) * rounded.astype(F32)
            rhs_ref[g, pl.ds(l8, ROWS, stride=8), :] = turn(total, 1, odd, two)
        half_ref[g] = rhs_ref[g].astype(BF16)


def advect(plan, fields, west, east):
    whole = pl.BlockSpec(memory_space=pltpu.VMEM)
    return pl.pallas_call(
        advect_kernel,
        in_specs=[whole] * 8,
        out_specs=[whole] * 3,
        out_shape=[
            jax.ShapeDtypeStruct((NF, LEV, ROWS, COLS), BF16),
            jax.ShapeDtypeStruct((G, 128, COLS), F32),
            jax.ShapeDtypeStruct((G, 128, COLS), BF16),
        ],
        scratch_shapes=[pltpu.VMEM((8, NF * ROWS, COLS), F32)],
        compiler_params=params(),
        name="advect",
    )(*plan, fields, west, east)


SLOTS = 20


def slot_of_lane():
    return ((lane_iota((8, COLS)) + 3) & (COLS - 1)) // 6


def split3(x):
    a = x.astype(BF16)
    rest = x - a.astype(F32)
    b = rest.astype(BF16)
    c = (rest - b.astype(F32)).astype(BF16)
    return a, b, c


def prepare_kernel(
    mix_ref, shift_ref, frac_ref, mode_ref, cells_ref, source_ref, weight_ref, proj_ref,
    mix_out_ref, mask_ref, own_ref, matrix_ref, taps_ref, mode_out_ref,
    pick_ref, place_ref, in_row_ref, covered_ref, src_row_ref, wgt_ref, proj_out_ref,
):
    advect_plan(mix_ref, shift_ref, frac_ref, mix_out_ref, mask_ref, own_ref, matrix_ref, taps_ref)
    mode_out_ref[...] = mode_ref[...]
    proj_out_ref[...] = proj_ref[...]
    src = jnp.concatenate([source_ref[q : q + 1, :] for q in range(4)], axis=1)
    wgt = jnp.concatenate([weight_ref[q : q + 1, :] for q in range(4)], axis=1)
    wide = (COLS, 4 * OV)
    col = jnp.broadcast_to(src & (COLS - 1), wide)
    pick_ref[...] = jnp.where(lax.broadcasted_iota(jnp.int32, wide, 0) == col, 1.0, 0.0).astype(BF16)
    src_row_ref[...] = jnp.broadcast_to(src >> 7, (8, 4 * OV))
    wgt_ref[...] = jnp.broadcast_to(wgt, (8, 4 * OV))
    cells = cells_ref[...]
    sub = lax.broadcasted_iota(jnp.int32, (128, OV), 0)
    place = jnp.where(sub == jnp.broadcast_to(cells & (COLS - 1), (128, OV)), 1.0, 0.0).astype(BF16)
    place_ref[...] = place
    in_row = jnp.where((sub >> 3) == jnp.broadcast_to(cells >> 7, (128, OV)), 1.0, 0.0).astype(BF16)
    in_row_ref[...] = in_row
    nt = (((1,), (1,)), ((), ()))
    covered_ref[...] = lax.dot_general(in_row, place, nt, preferred_element_type=F32)


def prepare(*args):
    shapes = [
        ((NF, LEV, 8, COLS), F32),
        ((9, ROWS, COLS), jnp.int16),
        ((ROWS, COLS), jnp.int32),
        ((4, COLS, COLS), BF16),
        ((4, LEV, ROWS, COLS), F32),
        ((1, LEV), F32),
        ((COLS, 4 * OV), BF16),
        ((128, OV), BF16),
        ((128, OV), BF16),
        ((128, COLS), F32),
        ((8, 4 * OV), jnp.int32),
        ((8, 4 * OV), F32),
        ((LEV, LEV), F32),
    ]
    made = pl.pallas_call(
        prepare_kernel,
        in_specs=[pl.BlockSpec(memory_space=pltpu.SMEM)] + [pl.BlockSpec(memory_space=pltpu.VMEM)] * 7,
        out_shape=[jax.ShapeDtypeStruct(shape, dtype) for shape, dtype in shapes],
        compiler_params=params(),
        cost_estimate=pl.CostEstimate(flops=4_000_000, bytes_accessed=2_000_000, transcendentals=0),
        name="prepare",
    )(*args)
    return made[:5], made[5], made[6:]


def margin_kernel(
    rhs_ref, both_ref, pick_ref, place_ref, in_row_ref, covered_ref, src_row_ref, wgt_ref, proj_ref, b_ref, slots_ref
):
    other = 1 - lax.axis_index("panel")
    pick, place = pick_ref[...], place_ref[...]
    src_row, wgt = src_row_ref[...], wgt_ref[...]
    in_row = in_row_ref[...].astype(F32)
    covered = covered_ref[...] > 0.5
    nt = (((1,), (1,)), ((), ()))
    joined = []
    for lb in range(G):
        cols = jnp.dot(both_ref[other, lb], pick, preferred_element_type=F32)
        rep = jnp.zeros((8, 4 * OV), F32)
        for r in range(ROWS):
            rep = rep + jnp.where(src_row == r, wgt, 0.0) * cols[8 * r : 8 * r + 8, :]
        rep = rep[:, :OV] + rep[:, OV : 2 * OV] + rep[:, 2 * OV : 3 * OV] + rep[:, 3 * OV :]
        spread = in_row * jnp.concatenate([rep] * ROWS, axis=0)
        values = None
        for part in split3(spread):
            value = lax.dot_general(part, place, nt, preferred_element_type=F32)
            values = value if values is None else values + value
        joined.append(jnp.where(covered, values, rhs_ref[lb]))
    levels = jnp.concatenate(
        [jnp.concatenate([joined[lb][8 * r : 8 * r + 8] for lb in range(G)], axis=0) for r in range(ROWS)], axis=1
    )
    modal = jnp.dot(proj_ref[...], levels, precision=lax.Precision.HIGHEST, preferred_element_type=F32)
    for lb in range(G):
        for r in range(ROWS):
            tile = modal[8 * lb : 8 * lb + 8, COLS * r : COLS * r + COLS]
            b_ref[lb, 8 * r : 8 * r + 8, :] = tile
    lat, lon = lax.axis_index("lat"), lax.axis_index("lon")
    place_in_square = 2 * (lat & 1) + (lon & 1)
    for lb in range(G):
        slots_ref[place_in_square ^ 2, lb] = b_ref[lb, pl.ds(pl.multiple_of(8 * 13 * (1 - (lat & 1)), 8), 24), :]
        acc = jnp.zeros((8, COLS), F32)
        for i in range(SLOTS):
            r = (i - 2) % ROWS
            acc = jnp.where(slot_of_lane() == i, roll_lanes(b_ref[lb, 8 * r : 8 * r + 8, :], 6 * i), acc)
        slots_ref[place_in_square ^ 1, lb, 0:8, :] = acc
        slots_ref[place_in_square ^ 3, lb, 0:8, :] = acc


def margin(rhs, both, lists):
    return pl.pallas_call(
        margin_kernel,
        out_shape=[
            jax.ShapeDtypeStruct((G, 128, COLS), F32),
            jax.ShapeDtypeStruct((4, G, 24, COLS), F32),
        ],
        compiler_params=params(),
        name="margin",
    )(rhs, both, *lists)


def second_kernel(b_ref, first_ref, got_ref, out_ref):
    lat, lon = lax.axis_index("lat"), lax.axis_index("lon")
    here = 2 * (lat & 1) + (lon & 1)
    there = 3 - here
    even = jnp.broadcast_to(lat & 1, (8, COLS)) == 0
    slot = slot_of_lane()
    for lb in range(G):
        out_ref[there ^ 2, lb, 0:24, :] = b_ref[lb, pl.ds(pl.multiple_of(8 * 13 * (lat & 1), 8), 24), :]
        out_ref[there ^ 2, lb, 24:32, :] = got_ref[here ^ 1, lb, 0:8, :]
        own = first_ref[here ^ 1, lb, 0:8, :]
        out_ref[there ^ 3, lb, 24:32, :] = own
        row = [got_ref[here ^ 2, lb, 8 * n : 8 * n + 8, :] for n in range(3)]
        with_south = jnp.where(slot == 18, roll_lanes(row[0], 6 * 18), jnp.where(slot == 19, roll_lanes(row[1], 6 * 19), own))
        with_north = jnp.where(slot == 0, row[1], jnp.where(slot == 1, roll_lanes(row[2], 6), own))
        out_ref[there ^ 1, lb, 24:32, :] = jnp.where(even, with_south, with_north)


def second(b, first, got):
    return pl.pallas_call(
        second_kernel,
        out_shape=jax.ShapeDtypeStruct((4, G, 32, COLS), F32),
        compiler_params=params(),
        name="second",
    )(b, first, got)


def images_kernel(shift_ref, b_ref, first_ref, second_ref, adv_ref, c_ref, u1_ref, u2_ref, s_ref, adv_hbm, sem):
    leaving = pltpu.make_async_copy(adv_ref, adv_hbm, sem)
    leaving.start()
    lat, lon = lax.axis_index("lat"), lax.axis_index("lon")
    one = jnp.float32(1.0)
    zero = jnp.float32(0.0)
    has_n = jnp.where(lat > 0, one, zero)
    has_s = jnp.where(lat < lax.axis_size("lat") - 1, one, zero)
    has_w = jnp.where(lon > 0, one, zero)
    has_e = jnp.where(lon < lax.axis_size("lon") - 1, one, zero)
    lane = lane_iota((8, COLS))
    first, last = lane == 0, lane == COLS - 1
    side = jnp.where(lane < 64, has_e, has_w)
    here = 2 * (lat & 1) + (lon & 1)
    there = 3 - here
    lat_even = jnp.broadcast_to(lat & 1, (8, COLS)) == 0
    slot = slot_of_lane()
    from_east = ((lane % 6) < 3) & (lane < 120)
    north_slot, south_slot = slot < 2, (slot == 18) | (slot == 19)
    inside = jnp.where(from_east, has_e, has_w)
    inside = jnp.where(north_slot, inside * has_n, jnp.where(south_slot, inside * has_s, inside)) > 0.5
    first_side = (lat_even & south_slot) | (~lat_even & north_slot)
    second_side = (lat_even & north_slot) | (~lat_even & south_slot)
    east_first = jnp.where(from_east, 1, 0) == jnp.broadcast_to(1 - (lon & 1), (8, COLS))

    def line(main, ext):
        return roll_lanes(jnp.where(last, ext, main), 1) + roll_lanes(jnp.where(first, ext, main), -1)

    def row_scale(j):
        return has_n if j < 0 else has_s if j >= ROWS else None

    sums_out = jnp.zeros((8, COLS), F32)
    for lb in range(G):
        diag = lane_iota((8, LEV)) == (lax.broadcasted_iota(jnp.int32, (8, LEV), 0) + 8 * lb)
        a = 4.0 + jnp.sum(jnp.where(diag, jnp.broadcast_to(shift_ref[...], (8, LEV)), 0.0), axis=1, keepdims=True)
        a = jnp.broadcast_to(a, (8, COLS))
        near = jnp.where(first_side, first_ref[here ^ 3, lb, 0:8, :], first_ref[here ^ 1, lb, 0:8, :])
        near = jnp.where(second_side, second_ref[there ^ 2, lb, 24:32, :], near)
        far = jnp.where(second_side, second_ref[there ^ 3, lb, 24:32, :], second_ref[there ^ 1, lb, 24:32, :])
        packed = jnp.where(inside, jnp.where(east_first, near, far), 0.0)

        def b_main(j):
            if 0 <= j < ROWS:
                return b_ref[lb, 8 * j : 8 * j + 8, :]
            n = j + 3 if j < 0 else j - ROWS
            rows = slice(8 * n, 8 * n + 8)
            one, two = first_ref[here ^ 2, lb, rows, :], second_ref[there ^ 2, lb, rows, :]
            if j < 0:
                return jnp.where(has_n > 0.5, jnp.where(lat_even, two, one), 0.0)
            return jnp.where(has_s > 0.5, jnp.where(lat_even, one, two), 0.0)

        bm = {j: b_main(j) for j in (-3, -2)}
        bx = {-2: packed}
        cm, cx, um, ux = {}, {}, {}, {}
        sums = [jnp.zeros((8, COLS), F32) for _ in range(8)]
        for j in range(-2, ROWS + 4):
            if j <= ROWS + 1:
                bm[j + 1] = b_main(j + 1)
                if j + 1 <= ROWS + 1:
                    bx[j + 1] = roll_lanes(packed, -6 * (j + 3))
                value = a * bm[j] - (bm[j - 1] + bm[j + 1] + line(bm[j], bx[j]))
                scale = row_scale(j)
                cm[j] = value if scale is None else value * scale
                if -1 <= j <= ROWS:
                    value = (a * bx[j] - (bx[j - 1] + bx[j + 1] + line(bx[j], bm[j]))) * side
                    cx[j] = value if scale is None else value * scale
                if 0 <= j < ROWS:
                    c_ref[lb, 8 * j : 8 * j + 8, :] = cm[j]
            i = j - 1
            if -1 <= i <= ROWS:
                value = 0.25 * (cm[i - 1] + cm[i + 1] + line(cm[i], cx[i]))
                scale = row_scale(i)
                um[i] = value if scale is None else value * scale
                if 0 <= i < ROWS:
                    ux[i] = 0.25 * (cx[i - 1] + cx[i + 1] + line(cx[i], cm[i])) * side
                    u1_ref[lb, 8 * i : 8 * i + 8, :] = um[i]
            i = j - 2
            if 0 <= i < ROWS:
                u2 = 0.5 * (um[i - 1] + um[i + 1] + line(um[i], ux[i])) - cm[i]
                u2_ref[lb, 8 * i : 8 * i + 8, :] = u2
                b, c, u1 = b_main(i), cm[i], um[i]
                pairs = ((b, c), (b, u1), (b, u2), (c, c), (c, u1), (u1, u1), (u1, u2), (u2, u2))
                sums = [s + x * y for s, (x, y) in zip(sums, pairs)]
        for q in range(8):
            total = jnp.sum(sums[q], axis=1, keepdims=True)
            sums_out = jnp.where(lane == 8 * lb + q, total, sums_out)
    sub = lax.broadcasted_iota(jnp.int32, (8, COLS), 0)
    spread = jnp.zeros((8, COLS), F32)
    for m in range(4):
        spread = jnp.where((sub & 3) == m, roll_lanes(sums_out, 32 * m), spread)
    folded = jnp.concatenate([jnp.sum(spread[4 * h : 4 * h + 4], axis=0, keepdims=True) for h in range(2)], axis=0)
    for n in range(s_ref.shape[0]):
        s_ref[n] = folded
    leaving.wait()


def images(mode_shift, b, got_first, got_second, adv, copies):
    full = jax.ShapeDtypeStruct((G, 128, COLS), F32)
    return pl.pallas_call(
        images_kernel,
        in_specs=[pl.BlockSpec(memory_space=pltpu.VMEM)] * 5,
        out_specs=[pl.BlockSpec(memory_space=pltpu.VMEM)] * 4 + [pl.BlockSpec(memory_space=pltpu.HBM)],
        out_shape=[
            full,
            full,
            full,
            jax.ShapeDtypeStruct((copies, 2, COLS), F32),
            jax.ShapeDtypeStruct(adv.shape, adv.dtype),
        ],
        scratch_shapes=[pltpu.SemaphoreType.DMA(())],
        compiler_params=params(),
        name="images",
    )(mode_shift, b, got_first, got_second, adv)


def sum_copies(ref):
    parts = [ref[n] for n in range(ref.shape[0])]
    while len(parts) > 1:
        parts = [parts[n] + parts[n + 1] for n in range(0, len(parts), 2)]
    return parts[0]


def iterate_kernel(shift_ref, s_ref, b_ref, c_ref, u1_ref, u2_ref, sol_ref, res_ref):
    lane = lane_iota((8, COLS))
    total = sum_copies(s_ref)
    sub = lax.broadcasted_iota(jnp.int32, (8, COLS), 0)
    rows = jnp.where(sub < 4, jnp.broadcast_to(total[0:1], (8, COLS)), jnp.broadcast_to(total[1:2], (8, COLS)))
    sums = rows
    for m in range(1, 4):
        sums = jnp.where((sub & 3) == m, roll_lanes(rows, -32 * m), sums)
    for lb in range(G):
        diag = lane_iota((8, LEV)) == (lax.broadcasted_iota(jnp.int32, (8, LEV), 0) + 8 * lb)
        a = 4.0 + jnp.sum(jnp.where(diag, jnp.broadcast_to(shift_ref[...], (8, LEV)), 0.0), axis=1, keepdims=True)
        a = jnp.broadcast_to(a, (8, COLS))

        def inner(q):
            value = jnp.sum(jnp.where(lane == 8 * lb + q, sums, 0.0), axis=1, keepdims=True)
            return jnp.broadcast_to(value, (8, COLS))

        bc, bu1, bu2, cc, cu1, u1u1, u1u2, u2u2 = [inner(q) for q in range(8)]
        cu2 = 2.0 * u1u1 - cc
        l10 = cu1 / cc
        l20 = cu2 / cc
        d1 = u1u1 - l10 * cu1
        e1 = u1u2 - l10 * cu2
        l21 = e1 / d1
        d2 = u2u2 - l20 * cu2 - l21 * e1
        z0 = bc
        z1 = bu1 - l10 * z0
        z2 = bu2 - l20 * z0 - l21 * z1
        y2 = z2 / d2
        y1 = z1 / d1 - l21 * y2
        y0 = z0 / cc - l10 * y1 - l20 * y2
        for r in range(ROWS):
            rows = slice(8 * r, 8 * r + 8)
            b, c, u1, u2 = b_ref[lb, rows, :], c_ref[lb, rows, :], u1_ref[lb, rows, :], u2_ref[lb, rows, :]
            v1 = 0.25 * (a * b - c)
            v2 = 0.5 * (a * v1 - u1) - b
            at = pl.ds(lb * 128 + r, 8, stride=ROWS)
            sol_ref[at, :] = y0 * b + y1 * v1 + y2 * v2
            res_ref[at, :] = b - y0 * c - y1 * u1 - y2 * u2


def iterate(mode_shift, sums, b, c, u1, u2):
    out = jax.ShapeDtypeStruct((LEV * ROWS, COLS), F32)
    return pl.pallas_call(
        iterate_kernel,
        out_shape=[out, out],
        compiler_params=params(),
        name="iterate",
    )(mode_shift, sums, b, c, u1, u2)


def send(block, axis, by):
    count = lax.axis_size(axis)
    return lax.ppermute(block, axis, [(i, i + by) for i in range(count) if 0 <= i + by < count])


def relay_kernel(in_ref, out_ref):
    total = sum_copies(in_ref)
    for n in range(out_ref.shape[0]):
        out_ref[n] = total


def relay(parts, copies):
    return pl.pallas_call(
        relay_kernel,
        out_shape=jax.ShapeDtypeStruct((copies, 2, COLS), F32),
        compiler_params=params(),
        name="relay",
    )(parts)


def in_squares(slots, begin):
    lats, lons = lax.axis_size("lat"), lax.axis_size("lon")
    groups = [
        [((i + a) % lats) * lons + (j + b) % lons for a in (0, 1) for b in (0, 1)]
        for i in range(begin, lats, 2)
        for j in range(begin, lons, 2)
    ]
    return lax.all_to_all(slots, ("lat", "lon"), 0, 0, axis_index_groups=groups)


def per_device(fields, frac, shift, mix, proj, mode_shift, cells, source, weight):
    fields = fields[0]
    table = shift[0]
    plan, modes, lists = prepare(
        mix, table, frac[0], mode_shift.reshape(1, LEV), cells[0], source[0, 0].T, weight[0, 0].T, proj
    )
    packed, fields = pack(table, fields)
    west = send(packed, "lon", 1)
    east = send(pack_east(fields), "lon", -1)
    adv, rhs, half = advect(plan, fields, west, east)
    both = lax.all_gather(half, "panel")
    b, first = margin(rhs, both, lists)
    got_first = in_squares(first, 0)
    got_second = in_squares(second(b, first, got_first), 1)
    count = lax.axis_size("lon")
    rest = lax.axis_size("panel") * lax.axis_size("lat")
    c, u1, u2, sums, adv = images(modes, b, got_first, got_second, adv, count)
    sums = relay(lax.all_to_all(sums, "lon", 0, 0), rest)
    sums = lax.all_to_all(sums, ("panel", "lat"), 0, 0)
    sol, res = iterate(modes, sums, b, c, u1, u2)
    shape = (1, LEV, ROWS, COLS)
    return adv[None], sol.reshape(shape), res.reshape(shape)


def solution(mesh):
    wide = P("panel", None, None, "lat", "lon")
    flat = P("panel", None, "lat", "lon")
    table = P("panel", "lat", "lon", None)
    in_specs = (wide, flat, P("panel", "lat", None), P(), P(), P(), P("panel", "lat", "lon"), table, table)
    return jax.shard_map(per_device, mesh=mesh, in_specs=in_specs, out_specs=(wide, flat, flat), check_vma=False)
```

```python
import jax
import jax.numpy as jnp
from jax import lax
from jax.experimental import pallas as pl
from jax.experimental.pallas import tpu as pltpu
from jax.sharding import PartitionSpec as P

F32 = jnp.float32
BF16 = jnp.bfloat16
NF = 6
LEV = 24
ROWS = 16
COLS = 128
G = 3
OV = 256
VMEM_LIMIT = 48 * 1024 * 1024


def lane_iota(shape):
    return lax.broadcasted_iota(jnp.int32, shape, len(shape) - 1)


def roll_lanes(x, by):
    by = by % COLS
    if by == 0:
        return x
    return pltpu.roll(x, by, x.ndim - 1)


def params():
    return pltpu.CompilerParams(vmem_limit_bytes=VMEM_LIMIT)


def own_shift(shift_ref, lon):
    table = shift_ref[...]
    own = jnp.sum(jnp.where(lane_iota(table.shape) == lon, table, 0), axis=1, keepdims=True)
    return jnp.broadcast_to(own, (ROWS, COLS))


def half_bits(mask):
    return jnp.where(mask, 1, 0).astype(jnp.int16)


def lane_matrix(rule):
    source = lax.broadcasted_iota(jnp.int32, (COLS, COLS), 0)
    target = lax.broadcasted_iota(jnp.int32, (COLS, COLS), 1)
    return jnp.where(rule(source, target), 1.0, 0.0).astype(BF16)


def mirrored(source, target):
    return (target >= 32) & (source == jnp.where((target >> 5) == 2, target, (target + 64) & (COLS - 1)))


def pack_east_kernel(fields_ref, out_ref):
    pair = (lane_iota((ROWS, COLS)) >> 1).astype(jnp.int16)
    for g in range(G):
        acc = jnp.zeros((ROWS, COLS), BF16)
        for f in range(NF):
            for l8 in range(8):
                i = f * 8 + l8
                acc = jnp.where(pair == jnp.int16(i), roll_lanes(fields_ref[f, 8 * g + l8], 2 * i), acc)
        out_ref[g] = acc


def pack_east(fields):
    return pl.pallas_call(
        pack_east_kernel,
        in_specs=[pl.BlockSpec(memory_space=pltpu.VMEM)],
        out_specs=pl.BlockSpec(memory_space=pltpu.VMEM),
        out_shape=jax.ShapeDtypeStruct((G, ROWS, COLS), BF16),
        compiler_params=params(),
        name="pack_east",
    )(fields)


def pack_kernel(shift_hbm, fields_hbm, west_ref, kept_ref, shift_ref, scratch, mask_ref, matrix_ref, sems):
    table = pltpu.make_async_copy(shift_hbm, shift_ref, sems.at[G])
    table.start()
    copies = []
    for g in range(G):
        part = (slice(None), pl.ds(8 * g, 8))
        copies.append(pltpu.make_async_copy(fields_hbm.at[part], kept_ref.at[part], sems.at[g]))
        copies[-1].start()
    table.wait()
    pack_plan(shift_ref, mask_ref, matrix_ref)
    masks = [mask_ref[n] == 1 for n in range(2)]
    zero = jnp.zeros((ROWS, COLS), BF16)
    for g in range(G):
        copies[g].wait()
        for l8 in range(8):
            level = 8 * g + l8
            parts = [
                jnp.concatenate([jnp.where(m, kept_ref[f, level], zero) for m in masks], axis=1) for f in range(NF)
            ]
            wide = jnp.dot(jnp.concatenate(parts, axis=0), matrix_ref[...], preferred_element_type=F32)
            scratch[l8, 0] = wide[:, :COLS]
            scratch[l8, 1] = wide[:, COLS:]
            pairs = scratch[l8, 0, pl.ds(0, 8 * NF, stride=2), :] + scratch[l8, 1, pl.ds(1, 8 * NF, stride=2), :]
            pairs = pairs.astype(BF16)
            for n in range(NF // 2):
                west_ref[n, level] = pairs[ROWS * n : ROWS * n + ROWS]


def pack_plan(shift_ref, mask_ref, matrix_ref):
    shift = own_shift(shift_ref, lax.axis_index("lon") + 1)
    lane = lane_iota((ROWS, COLS))
    mask_ref[0] = half_bits(lane >= COLS - 32 * shift)
    mask_ref[1] = half_bits(lane == COLS - 1 - 32 * shift)
    rules = (
        (lambda s, t: s == t, mirrored),
        (lambda s, t: ((s & 31) == 31) & (t == 31), lambda s, t: ((s & 31) == 31) & (t == 30)),
    )
    for m, pair in enumerate(rules):
        for n, rule in enumerate(pair):
            matrix_ref[COLS * m : COLS * m + COLS, COLS * n : COLS * n + COLS] = lane_matrix(rule)


def pack(shift, fields):
    return pl.pallas_call(
        pack_kernel,
        in_specs=[pl.BlockSpec(memory_space=pltpu.HBM)] * 2,
        out_specs=[pl.BlockSpec(memory_space=pltpu.VMEM)] * 2,
        out_shape=[
            jax.ShapeDtypeStruct((NF // 2, LEV, ROWS, COLS), BF16),
            jax.ShapeDtypeStruct((NF, LEV, ROWS, COLS), BF16),
        ],
        scratch_shapes=[
            pltpu.VMEM((ROWS, 32), jnp.int32),
            pltpu.VMEM((8, 2, NF * ROWS, COLS), F32),
            pltpu.VMEM((2, ROWS, COLS), jnp.int16),
            pltpu.VMEM((2 * COLS, 2 * COLS), BF16),
            pltpu.SemaphoreType.DMA((G + 1,)),
        ],
        compiler_params=params(),
        name="pack",
    )(*(pltpu.with_memory_space_constraint(x, pltpu.HBM) for x in (shift, fields)))


TAPS = (-1, 0, 1, 2)


def turn(x, sign, odd, two):
    x = jnp.where(odd, roll_lanes(x, 32 * sign), x)
    return jnp.where(two, roll_lanes(x, 64), x)


def advect_plan(mix_ref, shift_ref, frac_ref, mix_out_ref, mask_ref, shift_out_ref, matrix_ref, weight_ref):
    for f in range(NF):
        for level in range(LEV):
            mix_out_ref[f, level] = jnp.full((8, COLS), mix_ref[f, level], F32)
    shift = own_shift(shift_ref, lax.axis_index("lon"))
    shift_out_ref[...] = shift
    lane = lane_iota((ROWS, COLS))
    low = (lax.broadcasted_iota(jnp.int32, (ROWS, COLS), 0) & 1) == 0
    odd, two = (shift & 1) == 1, (shift & 2) == 2

    def beyond(j):
        at = ((lane - j + 32 * shift) & (COLS - 1)) - 32 * shift + j
        return (at < 0) | (at >= COLS)

    masks = [beyond(j) for j in TAPS]
    masks += [odd, two, lane < 2, ~low & ((lane >> 5) != 2), lane == jnp.where(low, 31, 30)]
    for n, mask in enumerate(masks):
        mask_ref[n] = half_bits(mask)
    rules = [lambda s, t, j=j: s == ((t + j) & (COLS - 1)) for j in TAPS if j]
    rules.append(lambda s, t: ((s == 30) | (s == 31)) & ((t & 31) == 0))
    for n, rule in enumerate(rules):
        matrix_ref[n] = lane_matrix(rule)
    for level in range(LEV):
        t = turn(frac_ref[level], -1, odd, two)
        tm1, tm2, tp1 = t - 1.0, t - 2.0, t + 1.0
        weight_ref[0, level] = -t * tm1 * tm2 * (1.0 / 6.0)
        weight_ref[1, level] = tp1 * tm1 * tm2 * 0.5
        weight_ref[2, level] = -tp1 * t * tm2 * 0.5
        weight_ref[3, level] = tp1 * t * tm1 * (1.0 / 6.0)


def advect_kernel(
    mix_ref, mask_ref, shift_ref, matrix_ref, weight_ref, fields_ref, west_ref, east_ref, adv_ref, rhs_ref, half_ref, scratch
):
    shift = shift_ref[...]
    lane = lane_iota((ROWS, COLS))
    odd, two = (shift & 1) == 1, (shift & 2) == 2
    bits = [mask_ref[n] == 1 for n in range(9)]
    masks, (odd16, two16, edge16, swap16, single16) = bits[:4], bits[4:]
    single_at = jnp.concatenate([lane == ((COLS - 32 * shift) & (COLS - 1))] * NF, axis=0)
    zero = jnp.zeros((ROWS, COLS), BF16)

    @pl.loop(0, G)
    def _(g):
        east = east_ref[g]
        for l8 in range(8):
            level = g * 8 + l8
            shared = jnp.concatenate([west_ref[n, level] for n in range(NF // 2)], axis=0).astype(F32)
            scratch[l8, pl.ds(0, 8 * NF, stride=2), :] = shared
            scratch[l8, pl.ds(1, 8 * NF, stride=2), :] = shared
            west = scratch[l8].astype(BF16)
            chosen = [[] for _ in TAPS]
            singles = []
            for f in range(NF):
                other = west[ROWS * f : ROWS * f + ROWS]
                singles.append(jnp.where(single16, other, zero))
                other = jnp.where(swap16, roll_lanes(other, 64), other)
                other = jnp.where(edge16, roll_lanes(east, -2 * (f * 8 + l8)), other)
                own = fields_ref[f, level]
                for n, mask in enumerate(masks):
                    chosen[n].append(jnp.where(mask, other, own))
            moved = [None] * 4
            moved[1] = [part.astype(F32) for part in chosen[1]]
            for n, tap in ((0, 0), (1, 2), (2, 3)):
                wide = jnp.dot(jnp.concatenate(chosen[tap], axis=0), matrix_ref[n], preferred_element_type=F32)
                if tap == 0:
                    column = jnp.dot(jnp.concatenate(singles, axis=0), matrix_ref[3], preferred_element_type=F32)
                    wide = jnp.where(single_at, column, wide)
                moved[tap] = [wide[ROWS * f : ROWS * f + ROWS] for f in range(NF)]
            weights = [weight_ref[n, level] for n in range(4)]
            total = jnp.zeros((ROWS, COLS), F32)
            for f in range(NF):
                acc = weights[0] * moved[0][f]
                for n in range(1, 4):
                    acc = acc + weights[n] * moved[n][f]
                rounded = acc.astype(BF16)
                adv_ref[f, level] = turn(rounded, 1, odd16, two16)
                mix = mix_ref[f, level]
                total = total + jnp.concatenate([mix, mix], axis=0) * rounded.astype(F32)
            rhs_ref[g, pl.ds(l8, ROWS, stride=8), :] = turn(total, 1, odd, two)
        half_ref[g] = rhs_ref[g].astype(BF16)


def advect(plan, fields, west, east):
    whole = pl.BlockSpec(memory_space=pltpu.VMEM)
    return pl.pallas_call(
        advect_kernel,
        in_specs=[whole] * 8,
        out_specs=[whole] * 3,
        out_shape=[
            jax.ShapeDtypeStruct((NF, LEV, ROWS, COLS), BF16),
            jax.ShapeDtypeStruct((G, 128, COLS), F32),
            jax.ShapeDtypeStruct((G, 128, COLS), BF16),
        ],
        scratch_shapes=[pltpu.VMEM((8, NF * ROWS, COLS), F32)],
        compiler_params=params(),
        name="advect",
    )(*plan, fields, west, east)


SLOTS = 20


def slot_of_lane(shape=(8, COLS)):
    return ((lane_iota(shape) + 3) & (COLS - 1)) // 6


def split3(x):
    a = x.astype(BF16)
    rest = x - a.astype(F32)
    b = rest.astype(BF16)
    c = (rest - b.astype(F32)).astype(BF16)
    return a, b, c


def prepare_kernel(
    mix_ref, shift_ref, frac_ref, mode_ref, cells_ref, source_ref, weight_ref, proj_ref,
    mix_out_ref, mask_ref, own_ref, matrix_ref, taps_ref, mode_out_ref,
    pick_ref, place_ref, in_row_ref, covered_ref, src_row_ref, wgt_ref, proj_out_ref,
):
    advect_plan(mix_ref, shift_ref, frac_ref, mix_out_ref, mask_ref, own_ref, matrix_ref, taps_ref)
    mode_out_ref[...] = mode_ref[...]
    proj_out_ref[...] = proj_ref[...]
    src = jnp.concatenate([source_ref[q : q + 1, :] for q in range(4)], axis=1)
    wgt = jnp.concatenate([weight_ref[q : q + 1, :] for q in range(4)], axis=1)
    wide = (COLS, 4 * OV)
    col = jnp.broadcast_to(src & (COLS - 1), wide)
    pick_ref[...] = jnp.where(lax.broadcasted_iota(jnp.int32, wide, 0) == col, 1.0, 0.0).astype(BF16)
    src_row_ref[...] = jnp.broadcast_to(src >> 7, (8, 4 * OV))
    wgt_ref[...] = jnp.broadcast_to(wgt, (8, 4 * OV))
    cells = cells_ref[...]
    sub = lax.broadcasted_iota(jnp.int32, (128, OV), 0)
    place = jnp.where(sub == jnp.broadcast_to(cells & (COLS - 1), (128, OV)), 1.0, 0.0).astype(BF16)
    place_ref[...] = place
    in_row = jnp.where((sub >> 3) == jnp.broadcast_to(cells >> 7, (128, OV)), 1.0, 0.0).astype(BF16)
    in_row_ref[...] = in_row
    nt = (((1,), (1,)), ((), ()))
    covered_ref[...] = lax.dot_general(in_row, place, nt, preferred_element_type=F32)


def prepare(*args):
    shapes = [
        ((NF, LEV, 8, COLS), F32),
        ((9, ROWS, COLS), jnp.int16),
        ((ROWS, COLS), jnp.int32),
        ((4, COLS, COLS), BF16),
        ((4, LEV, ROWS, COLS), F32),
        ((1, LEV), F32),
        ((COLS, 4 * OV), BF16),
        ((128, OV), BF16),
        ((128, OV), BF16),
        ((128, COLS), F32),
        ((8, 4 * OV), jnp.int32),
        ((8, 4 * OV), F32),
        ((LEV, LEV), F32),
    ]
    made = pl.pallas_call(
        prepare_kernel,
        in_specs=[pl.BlockSpec(memory_space=pltpu.SMEM)] + [pl.BlockSpec(memory_space=pltpu.VMEM)] * 7,
        out_shape=[jax.ShapeDtypeStruct(shape, dtype) for shape, dtype in shapes],
        compiler_params=params(),
        cost_estimate=pl.CostEstimate(flops=4_000_000, bytes_accessed=2_000_000, transcendentals=0),
        name="prepare",
    )(*args)
    return made[:5], made[5], made[6:]


def margin_kernel(
    rhs_ref, both_ref, pick_ref, place_ref, in_row_ref, covered_ref, src_row_ref, wgt_ref, proj_ref, b_ref, slots_ref
):
    other = 1 - lax.axis_index("panel")
    pick, place = pick_ref[...], place_ref[...]
    src_row, wgt = src_row_ref[...], wgt_ref[...]
    in_row = in_row_ref[...].astype(F32)
    covered = covered_ref[...] > 0.5
    nt = (((1,), (1,)), ((), ()))
    halves = jnp.concatenate([both_ref[other, lb] for lb in range(G)], axis=0)
    cols = jnp.dot(halves, pick, preferred_element_type=F32)
    rep = jnp.zeros((8 * G, 4 * OV), F32)
    for r in range(ROWS):
        weight = jnp.where(src_row == r, wgt, 0.0)
        rows = [cols[128 * lb + 8 * r : 128 * lb + 8 * r + 8] for lb in range(G)]
        rep = rep + jnp.concatenate([weight] * G, axis=0) * jnp.concatenate(rows, axis=0)
    rep = rep[:, :OV] + rep[:, OV : 2 * OV] + rep[:, 2 * OV : 3 * OV] + rep[:, 3 * OV :]
    spread = jnp.concatenate([in_row * jnp.concatenate([rep[8 * lb : 8 * lb + 8]] * ROWS, axis=0) for lb in range(G)], axis=0)
    placed = lax.dot_general(jnp.concatenate(split3(spread), axis=0), place, nt, preferred_element_type=F32)
    placed = placed[:384] + placed[384:768] + placed[768:]
    joined = [jnp.where(covered, placed[128 * lb : 128 * lb + 128], rhs_ref[lb]) for lb in range(G)]
    levels = jnp.concatenate(
        [jnp.concatenate([joined[lb][8 * r : 8 * r + 8] for lb in range(G)], axis=0) for r in range(ROWS)], axis=1
    )
    modal = jnp.dot(proj_ref[...], levels, precision=lax.Precision.HIGHEST, preferred_element_type=F32)
    for lb in range(G):
        for r in range(ROWS):
            b_ref[lb, 8 * r : 8 * r + 8, :] = modal[8 * lb : 8 * lb + 8, COLS * r : COLS * r + COLS]
    lat, lon = lax.axis_index("lat"), lax.axis_index("lon")
    place_in_square = 2 * (lat & 1) + (lon & 1)
    for lb in range(G):
        slots_ref[place_in_square ^ 2, lb] = b_ref[lb, pl.ds(pl.multiple_of(8 * 13 * (1 - (lat & 1)), 8), 24), :]
        acc = jnp.zeros((8, COLS), F32)
        for i in range(SLOTS):
            r = (i - 2) % ROWS
            acc = jnp.where(slot_of_lane() == i, roll_lanes(b_ref[lb, 8 * r : 8 * r + 8, :], 6 * i), acc)
        slots_ref[place_in_square ^ 1, lb, 0:8, :] = acc
        slots_ref[place_in_square ^ 3, lb, 0:8, :] = acc


def margin(rhs, both, lists):
    return pl.pallas_call(
        margin_kernel,
        out_shape=[
            jax.ShapeDtypeStruct((G, 128, COLS), F32),
            jax.ShapeDtypeStruct((4, G, 24, COLS), F32),
        ],
        compiler_params=params(),
        name="margin",
    )(rhs, both, *lists)


def second_kernel(b_ref, first_ref, got_ref, out_ref):
    lat, lon = lax.axis_index("lat"), lax.axis_index("lon")
    here = 2 * (lat & 1) + (lon & 1)
    there = 3 - here
    even = jnp.broadcast_to(lat & 1, (8, COLS)) == 0
    slot = slot_of_lane()
    for lb in range(G):
        out_ref[there ^ 2, lb, 0:24, :] = b_ref[lb, pl.ds(pl.multiple_of(8 * 13 * (lat & 1), 8), 24), :]
        out_ref[there ^ 2, lb, 24:32, :] = got_ref[here ^ 1, lb, 0:8, :]
        own = first_ref[here ^ 1, lb, 0:8, :]
        out_ref[there ^ 3, lb, 24:32, :] = own
        row = [got_ref[here ^ 2, lb, 8 * n : 8 * n + 8, :] for n in range(3)]
        with_south = jnp.where(slot == 18, roll_lanes(row[0], 6 * 18), jnp.where(slot == 19, roll_lanes(row[1], 6 * 19), own))
        with_north = jnp.where(slot == 0, row[1], jnp.where(slot == 1, roll_lanes(row[2], 6), own))
        out_ref[there ^ 1, lb, 24:32, :] = jnp.where(even, with_south, with_north)


def second(b, first, got):
    return pl.pallas_call(
        second_kernel,
        out_shape=jax.ShapeDtypeStruct((4, G, 32, COLS), F32),
        compiler_params=params(),
        name="second",
    )(b, first, got)


def images_kernel(shift_ref, b_ref, first_ref, second_ref, adv_ref, c_ref, u1_ref, u2_ref, s_ref, adv_hbm, sem):
    leaving = pltpu.make_async_copy(adv_ref, adv_hbm, sem)
    leaving.start()
    lat, lon = lax.axis_index("lat"), lax.axis_index("lon")
    one = jnp.float32(1.0)
    zero = jnp.float32(0.0)
    has_n = jnp.where(lat > 0, one, zero)
    has_s = jnp.where(lat < lax.axis_size("lat") - 1, one, zero)
    has_w = jnp.where(lon > 0, one, zero)
    has_e = jnp.where(lon < lax.axis_size("lon") - 1, one, zero)
    shape = (8 * G, COLS)
    lane = lane_iota(shape)
    first, last = lane == 0, lane == COLS - 1
    side = jnp.where(lane < 64, has_e, has_w)
    here = 2 * (lat & 1) + (lon & 1)
    there = 3 - here
    lat_even = jnp.broadcast_to(lat & 1, shape) == 0
    slot = slot_of_lane(shape)
    from_east = ((lane % 6) < 3) & (lane < 120)
    north_slot, south_slot = slot < 2, (slot == 18) | (slot == 19)
    inside = jnp.where(from_east, has_e, has_w)
    inside = jnp.where(north_slot, inside * has_n, jnp.where(south_slot, inside * has_s, inside)) > 0.5
    first_side = (lat_even & south_slot) | (~lat_even & north_slot)
    second_side = (lat_even & north_slot) | (~lat_even & south_slot)
    east_first = jnp.where(from_east, 1, 0) == jnp.broadcast_to(1 - (lon & 1), shape)

    def rows_of(ref, *at):
        return jnp.concatenate([ref[(*at[:-1], lb, at[-1])] for lb in range(G)], axis=0)

    def store(ref, j, value):
        for lb in range(G):
            ref[lb, 8 * j : 8 * j + 8, :] = value[8 * lb : 8 * lb + 8]

    def line(main, ext):
        return roll_lanes(jnp.where(last, ext, main), 1) + roll_lanes(jnp.where(first, ext, main), -1)

    def row_scale(j):
        return has_n if j < 0 else has_s if j >= ROWS else None

    modes = jnp.broadcast_to(shift_ref[...], (8 * G, LEV))
    diag = lane_iota((8 * G, LEV)) == lax.broadcasted_iota(jnp.int32, (8 * G, LEV), 0)
    a = jnp.broadcast_to(4.0 + jnp.sum(jnp.where(diag, modes, 0.0), axis=1, keepdims=True), shape)
    columns, forwarded = slice(0, 8), slice(24, 32)
    near = jnp.where(first_side, rows_of(first_ref, here ^ 3, columns), rows_of(first_ref, here ^ 1, columns))
    near = jnp.where(second_side, rows_of(second_ref, there ^ 2, forwarded), near)
    far = jnp.where(second_side, rows_of(second_ref, there ^ 3, forwarded), rows_of(second_ref, there ^ 1, forwarded))
    packed = jnp.where(inside, jnp.where(east_first, near, far), 0.0)

    def b_main(j):
        if 0 <= j < ROWS:
            return rows_of(b_ref, slice(8 * j, 8 * j + 8))
        n = j + 3 if j < 0 else j - ROWS
        rows = slice(8 * n, 8 * n + 8)
        one, two = rows_of(first_ref, here ^ 2, rows), rows_of(second_ref, there ^ 2, rows)
        if j < 0:
            return jnp.where(has_n > 0.5, jnp.where(lat_even, two, one), 0.0)
        return jnp.where(has_s > 0.5, jnp.where(lat_even, one, two), 0.0)

    bm = {j: b_main(j) for j in (-3, -2)}
    bx = {-2: packed}
    cm, cx, um, ux = {}, {}, {}, {}
    sums = [jnp.zeros(shape, F32) for _ in range(8)]
    for j in range(-2, ROWS + 4):
        if j <= ROWS + 1:
            bm[j + 1] = b_main(j + 1)
            if j + 1 <= ROWS + 1:
                bx[j + 1] = roll_lanes(packed, -6 * (j + 3))
            value = a * bm[j] - (bm[j - 1] + bm[j + 1] + line(bm[j], bx[j]))
            scale = row_scale(j)
            cm[j] = value if scale is None else value * scale
            if -1 <= j <= ROWS:
                value = (a * bx[j] - (bx[j - 1] + bx[j + 1] + line(bx[j], bm[j]))) * side
                cx[j] = value if scale is None else value * scale
            if 0 <= j < ROWS:
                store(c_ref, j, cm[j])
        i = j - 1
        if -1 <= i <= ROWS:
            value = 0.25 * (cm[i - 1] + cm[i + 1] + line(cm[i], cx[i]))
            scale = row_scale(i)
            um[i] = value if scale is None else value * scale
            if 0 <= i < ROWS:
                ux[i] = 0.25 * (cx[i - 1] + cx[i + 1] + line(cx[i], cm[i])) * side
                store(u1_ref, i, um[i])
        i = j - 2
        if 0 <= i < ROWS:
            u2 = 0.5 * (um[i - 1] + um[i + 1] + line(um[i], ux[i])) - cm[i]
            store(u2_ref, i, u2)
            b, c, u1 = b_main(i), cm[i], um[i]
            pairs = ((b, c), (b, u1), (b, u2), (c, c), (c, u1), (u1, u1), (u1, u2), (u2, u2))
            sums = [s + x * y for s, (x, y) in zip(sums, pairs)]
    lane, sub = lane_iota((8, COLS)), lax.broadcasted_iota(jnp.int32, (8, COLS), 0)
    sums_out = jnp.zeros((8, COLS), F32)
    for q in range(8):
        total = jnp.sum(sums[q], axis=1, keepdims=True)
        for lb in range(G):
            sums_out = jnp.where(lane == 8 * lb + q, total[8 * lb : 8 * lb + 8], sums_out)
    spread = jnp.zeros((8, COLS), F32)
    for m in range(4):
        spread = jnp.where((sub & 3) == m, roll_lanes(sums_out, 32 * m), spread)
    folded = jnp.concatenate([jnp.sum(spread[4 * h : 4 * h + 4], axis=0, keepdims=True) for h in range(2)], axis=0)
    for n in range(s_ref.shape[0]):
        s_ref[n] = folded
    leaving.wait()


def images(mode_shift, b, got_first, got_second, adv, copies):
    full = jax.ShapeDtypeStruct((G, 128, COLS), F32)
    return pl.pallas_call(
        images_kernel,
        in_specs=[pl.BlockSpec(memory_space=pltpu.VMEM)] * 5,
        out_specs=[pl.BlockSpec(memory_space=pltpu.VMEM)] * 4 + [pl.BlockSpec(memory_space=pltpu.HBM)],
        out_shape=[
            full,
            full,
            full,
            jax.ShapeDtypeStruct((copies, 2, COLS), F32),
            jax.ShapeDtypeStruct(adv.shape, adv.dtype),
        ],
        scratch_shapes=[pltpu.SemaphoreType.DMA(())],
        compiler_params=params(),
        name="images",
    )(mode_shift, b, got_first, got_second, adv)


def sum_copies(ref):
    parts = [ref[n] for n in range(ref.shape[0])]
    while len(parts) > 1:
        parts = [parts[n] + parts[n + 1] for n in range(0, len(parts), 2)]
    return parts[0]


def iterate_kernel(shift_ref, s_ref, b_ref, c_ref, u1_ref, u2_ref, sol_ref, res_ref):
    lane = lane_iota((8, COLS))
    total = sum_copies(s_ref)
    sub = lax.broadcasted_iota(jnp.int32, (8, COLS), 0)
    rows = jnp.where(sub < 4, jnp.broadcast_to(total[0:1], (8, COLS)), jnp.broadcast_to(total[1:2], (8, COLS)))
    sums = rows
    for m in range(1, 4):
        sums = jnp.where((sub & 3) == m, roll_lanes(rows, -32 * m), sums)
    for lb in range(G):
        diag = lane_iota((8, LEV)) == (lax.broadcasted_iota(jnp.int32, (8, LEV), 0) + 8 * lb)
        a = 4.0 + jnp.sum(jnp.where(diag, jnp.broadcast_to(shift_ref[...], (8, LEV)), 0.0), axis=1, keepdims=True)
        a = jnp.broadcast_to(a, (8, COLS))

        def inner(q):
            value = jnp.sum(jnp.where(lane == 8 * lb + q, sums, 0.0), axis=1, keepdims=True)
            return jnp.broadcast_to(value, (8, COLS))

        bc, bu1, bu2, cc, cu1, u1u1, u1u2, u2u2 = [inner(q) for q in range(8)]
        cu2 = 2.0 * u1u1 - cc
        l10 = cu1 / cc
        l20 = cu2 / cc
        d1 = u1u1 - l10 * cu1
        e1 = u1u2 - l10 * cu2
        l21 = e1 / d1
        d2 = u2u2 - l20 * cu2 - l21 * e1
        z0 = bc
        z1 = bu1 - l10 * z0
        z2 = bu2 - l20 * z0 - l21 * z1
        y2 = z2 / d2
        y1 = z1 / d1 - l21 * y2
        y0 = z0 / cc - l10 * y1 - l20 * y2
        for r in range(ROWS):
            rows = slice(8 * r, 8 * r + 8)
            b, c, u1, u2 = b_ref[lb, rows, :], c_ref[lb, rows, :], u1_ref[lb, rows, :], u2_ref[lb, rows, :]
            v1 = 0.25 * (a * b - c)
            v2 = 0.5 * (a * v1 - u1) - b
            at = pl.ds(lb * 128 + r, 8, stride=ROWS)
            sol_ref[at, :] = y0 * b + y1 * v1 + y2 * v2
            res_ref[at, :] = b - y0 * c - y1 * u1 - y2 * u2


def iterate(mode_shift, sums, b, c, u1, u2):
    out = jax.ShapeDtypeStruct((LEV * ROWS, COLS), F32)
    return pl.pallas_call(
        iterate_kernel,
        out_shape=[out, out],
        compiler_params=params(),
        name="iterate",
    )(mode_shift, sums, b, c, u1, u2)


def send(block, axis, by):
    count = lax.axis_size(axis)
    return lax.ppermute(block, axis, [(i, i + by) for i in range(count) if 0 <= i + by < count])


def relay_kernel(in_ref, out_ref):
    total = sum_copies(in_ref)
    for n in range(out_ref.shape[0]):
        out_ref[n] = total


def relay(parts, copies):
    return pl.pallas_call(
        relay_kernel,
        out_shape=jax.ShapeDtypeStruct((copies, 2, COLS), F32),
        compiler_params=params(),
        name="relay",
    )(parts)


def in_squares(slots, begin):
    lats, lons = lax.axis_size("lat"), lax.axis_size("lon")
    groups = [
        [((i + a) % lats) * lons + (j + b) % lons for a in (0, 1) for b in (0, 1)]
        for i in range(begin, lats, 2)
        for j in range(begin, lons, 2)
    ]
    return lax.all_to_all(slots, ("lat", "lon"), 0, 0, axis_index_groups=groups)


def per_device(fields, frac, shift, mix, proj, mode_shift, cells, source, weight):
    fields = fields[0]
    table = shift[0]
    plan, modes, lists = prepare(
        mix, table, frac[0], mode_shift.reshape(1, LEV), cells[0], source[0, 0].T, weight[0, 0].T, proj
    )
    packed, fields = pack(table, fields)
    west = send(packed, "lon", 1)
    east = send(pack_east(fields), "lon", -1)
    adv, rhs, half = advect(plan, fields, west, east)
    both = lax.all_gather(half, "panel")
    b, first = margin(rhs, both, lists)
    got_first = in_squares(first, 0)
    got_second = in_squares(second(b, first, got_first), 1)
    count = lax.axis_size("lon")
    rest = lax.axis_size("panel") * lax.axis_size("lat")
    c, u1, u2, sums, adv = images(modes, b, got_first, got_second, adv, count)
    sums = relay(lax.all_to_all(sums, "lon", 0, 0), rest)
    sums = lax.all_to_all(sums, ("panel", "lat"), 0, 0)
    sol, res = iterate(modes, sums, b, c, u1, u2)
    shape = (1, LEV, ROWS, COLS)
    return adv[None], sol.reshape(shape), res.reshape(shape)


def solution(mesh):
    wide = P("panel", None, None, "lat", "lon")
    flat = P("panel", None, "lat", "lon")
    table = P("panel", "lat", "lon", None)
    in_specs = (wide, flat, P("panel", "lat", None), P(), P(), P(), P("panel", "lat", "lon"), table, table)
    return jax.shard_map(per_device, mesh=mesh, in_specs=in_specs, out_specs=(wide, flat, flat), check_vma=False)
```

```python
import jax
import jax.numpy as jnp
from jax import lax
from jax.experimental import pallas as pl
from jax.experimental.pallas import tpu as pltpu
from jax.sharding import PartitionSpec as P

F32 = jnp.float32
BF16 = jnp.bfloat16
NF = 6
LEV = 24
ROWS = 16
COLS = 128
G = 3
OV = 256
VMEM_LIMIT = 48 * 1024 * 1024


def lane_iota(shape):
    return lax.broadcasted_iota(jnp.int32, shape, len(shape) - 1)


def roll_lanes(x, by):
    by = by % COLS
    if by == 0:
        return x
    return pltpu.roll(x, by, x.ndim - 1)


def params():
    return pltpu.CompilerParams(vmem_limit_bytes=VMEM_LIMIT)


def own_shift(shift_ref, lon):
    table = shift_ref[...]
    own = jnp.sum(jnp.where(lane_iota(table.shape) == lon, table, 0), axis=1, keepdims=True)
    return jnp.broadcast_to(own, (ROWS, COLS))


def half_bits(mask):
    return jnp.where(mask, 1, 0).astype(jnp.int16)


def lane_matrix(rule):
    source = lax.broadcasted_iota(jnp.int32, (COLS, COLS), 0)
    target = lax.broadcasted_iota(jnp.int32, (COLS, COLS), 1)
    return jnp.where(rule(source, target), 1.0, 0.0).astype(BF16)


def mirrored(source, target):
    return (target >= 32) & (source == jnp.where((target >> 5) == 2, target, (target + 64) & (COLS - 1)))


def pack_east_kernel(fields_ref, out_ref):
    pair = (lane_iota((ROWS, COLS)) >> 1).astype(jnp.int16)
    for g in range(G):
        acc = jnp.zeros((ROWS, COLS), BF16)
        for f in range(NF):
            for l8 in range(8):
                i = f * 8 + l8
                acc = jnp.where(pair == jnp.int16(i), roll_lanes(fields_ref[f, 8 * g + l8], 2 * i), acc)
        out_ref[g] = acc


def pack_east(fields):
    return pl.pallas_call(
        pack_east_kernel,
        in_specs=[pl.BlockSpec(memory_space=pltpu.VMEM)],
        out_specs=pl.BlockSpec(memory_space=pltpu.VMEM),
        out_shape=jax.ShapeDtypeStruct((G, ROWS, COLS), BF16),
        compiler_params=params(),
        name="pack_east",
    )(fields)


CHUNKS = 1
PER_CHUNK = LEV // CHUNKS


def pack_kernel(shift_hbm, fields_hbm, west_ref, kept_ref, shift_ref, scratch, mask_ref, matrix_ref, sems):
    table = pltpu.make_async_copy(shift_hbm, shift_ref, sems.at[CHUNKS])
    table.start()
    copies = []
    for n in range(CHUNKS):
        part = (slice(None), pl.ds(PER_CHUNK * n, PER_CHUNK))
        copies.append(pltpu.make_async_copy(fields_hbm.at[part], kept_ref.at[part], sems.at[n]))
        copies[-1].start()
    table.wait()
    pack_plan(shift_ref, mask_ref, matrix_ref)
    masks = [mask_ref[n] == 1 for n in range(2)]
    zero = jnp.zeros((ROWS, COLS), BF16)
    low = (lax.broadcasted_iota(jnp.int32, (NF * ROWS, COLS), 0) & 1) == 0
    for n in range(CHUNKS):
        copies[n].wait()
        for level in range(PER_CHUNK * n, PER_CHUNK * n + PER_CHUNK):
            parts = [
                jnp.concatenate([jnp.where(m, kept_ref[f, level], zero) for m in masks], axis=1) for f in range(NF)
            ]
            wide = jnp.dot(jnp.concatenate(parts, axis=0), matrix_ref[...], preferred_element_type=F32)
            scratch[level % 8] = jnp.where(low, wide[:, :COLS], wide[:, COLS:])
            pairs = scratch[level % 8, pl.ds(0, 8 * NF, stride=2), :] + scratch[level % 8, pl.ds(1, 8 * NF, stride=2), :]
            pairs = pairs.astype(BF16)
            for m in range(NF // 2):
                west_ref[m, level] = pairs[ROWS * m : ROWS * m + ROWS]


def pack_plan(shift_ref, mask_ref, matrix_ref):
    shift = own_shift(shift_ref, lax.axis_index("lon") + 1)
    lane = lane_iota((ROWS, COLS))
    mask_ref[0] = half_bits(lane >= COLS - 32 * shift)
    mask_ref[1] = half_bits(lane == COLS - 1 - 32 * shift)
    rules = (
        (lambda s, t: s == t, mirrored),
        (lambda s, t: ((s & 31) == 31) & (t == 31), lambda s, t: ((s & 31) == 31) & (t == 30)),
    )
    for m, pair in enumerate(rules):
        for n, rule in enumerate(pair):
            matrix_ref[COLS * m : COLS * m + COLS, COLS * n : COLS * n + COLS] = lane_matrix(rule)


def pack(shift, fields):
    return pl.pallas_call(
        pack_kernel,
        in_specs=[pl.BlockSpec(memory_space=pltpu.HBM)] * 2,
        out_specs=[pl.BlockSpec(memory_space=pltpu.VMEM)] * 2,
        out_shape=[
            jax.ShapeDtypeStruct((NF // 2, LEV, ROWS, COLS), BF16),
            jax.ShapeDtypeStruct((NF, LEV, ROWS, COLS), BF16),
        ],
        scratch_shapes=[
            pltpu.VMEM((ROWS, 32), jnp.int32),
            pltpu.VMEM((8, NF * ROWS, COLS), F32),
            pltpu.VMEM((2, ROWS, COLS), jnp.int16),
            pltpu.VMEM((2 * COLS, 2 * COLS), BF16),
            pltpu.SemaphoreType.DMA((CHUNKS + 1,)),
        ],
        compiler_params=params(),
        name="pack",
    )(*(pltpu.with_memory_space_constraint(x, pltpu.HBM) for x in (shift, fields)))


TAPS = (-1, 0, 1, 2)


def turn(x, sign, odd, two):
    x = jnp.where(odd, roll_lanes(x, 32 * sign), x)
    return jnp.where(two, roll_lanes(x, 64), x)


def advect_plan(mix_ref, shift_ref, frac_ref, mix_out_ref, mask_ref, shift_out_ref, matrix_ref, weight_ref):
    for f in range(NF):
        for level in range(LEV):
            mix_out_ref[f, level] = jnp.full((8, COLS), mix_ref[f, level], F32)
    shift = own_shift(shift_ref, lax.axis_index("lon"))
    shift_out_ref[...] = shift
    lane = lane_iota((ROWS, COLS))
    low = (lax.broadcasted_iota(jnp.int32, (ROWS, COLS), 0) & 1) == 0
    odd, two = (shift & 1) == 1, (shift & 2) == 2

    def beyond(j):
        at = ((lane - j + 32 * shift) & (COLS - 1)) - 32 * shift + j
        return (at < 0) | (at >= COLS)

    masks = [beyond(j) for j in TAPS]
    masks += [odd, two, lane < 2, ~low & ((lane >> 5) != 2), lane == jnp.where(low, 31, 30)]
    for n, mask in enumerate(masks):
        mask_ref[n] = half_bits(mask)
    rules = [lambda s, t, j=j: s == ((t + j) & (COLS - 1)) for j in TAPS if j]
    rules.append(lambda s, t: ((s == 30) | (s == 31)) & ((t & 31) == 0))
    for n, rule in enumerate(rules):
        matrix_ref[n] = lane_matrix(rule)
    for level in range(LEV):
        t = turn(frac_ref[level], -1, odd, two)
        tm1, tm2, tp1 = t - 1.0, t - 2.0, t + 1.0
        weight_ref[0, level] = -t * tm1 * tm2 * (1.0 / 6.0)
        weight_ref[1, level] = tp1 * tm1 * tm2 * 0.5
        weight_ref[2, level] = -tp1 * t * tm2 * 0.5
        weight_ref[3, level] = tp1 * t * tm1 * (1.0 / 6.0)


def advect_kernel(
    mix_ref, mask_ref, shift_ref, matrix_ref, weight_ref, fields_ref, west_ref, east_ref, adv_ref, rhs_ref, half_ref, scratch
):
    shift = shift_ref[...]
    lane = lane_iota((ROWS, COLS))
    odd, two = (shift & 1) == 1, (shift & 2) == 2
    bits = [mask_ref[n] == 1 for n in range(9)]
    masks, (odd16, two16, edge16, swap16, single16) = bits[:4], bits[4:]
    single_at = lane == ((COLS - 32 * shift) & (COLS - 1))
    zero = jnp.zeros((ROWS, COLS), BF16)

    @pl.loop(0, G)
    def _(g):
        east = east_ref[g]
        for batch in (range(8),):
            chosen = [[] for _ in TAPS]
            singles = []
            for l8 in batch:
                level = g * 8 + l8
                shared = jnp.concatenate([west_ref[n, level] for n in range(NF // 2)], axis=0).astype(F32)
                scratch[l8, pl.ds(0, 8 * NF, stride=2), :] = shared
                scratch[l8, pl.ds(1, 8 * NF, stride=2), :] = shared
            for l8 in batch:
                level = g * 8 + l8
                west = scratch[l8].astype(BF16)
                for f in range(NF):
                    other = west[ROWS * f : ROWS * f + ROWS]
                    singles.append(jnp.where(single16, other, zero))
                    other = jnp.where(swap16, roll_lanes(other, 64), other)
                    other = jnp.where(edge16, roll_lanes(east, -2 * (f * 8 + l8)), other)
                    own = fields_ref[f, level]
                    for n, mask in enumerate(masks):
                        chosen[n].append(jnp.where(mask, other, own))
            wide = [
                jnp.dot(jnp.concatenate(chosen[tap], axis=0), matrix_ref[n], preferred_element_type=F32)
                for n, tap in ((0, 0), (1, 2), (2, 3))
            ]
            column = jnp.dot(jnp.concatenate(singles, axis=0), matrix_ref[3], preferred_element_type=F32)
            for k, l8 in enumerate(batch):
                level = g * 8 + l8
                weights = [weight_ref[n, level] for n in range(4)]
                total = jnp.zeros((ROWS, COLS), F32)
                for f in range(NF):
                    i = k * NF + f
                    at = slice(ROWS * i, ROWS * i + ROWS)
                    acc = weights[0] * jnp.where(single_at, column[at], wide[0][at])
                    acc = acc + weights[1] * chosen[1][i].astype(F32)
                    acc = acc + weights[2] * wide[1][at]
                    acc = acc + weights[3] * wide[2][at]
                    rounded = acc.astype(BF16)
                    adv_ref[f, level] = turn(rounded, 1, odd16, two16)
                    mix = mix_ref[f, level]
                    total = total + jnp.concatenate([mix, mix], axis=0) * rounded.astype(F32)
                rhs_ref[g, pl.ds(l8, ROWS, stride=8), :] = turn(total, 1, odd, two)
        half_ref[g] = rhs_ref[g].astype(BF16)


def advect(plan, fields, west, east):
    whole = pl.BlockSpec(memory_space=pltpu.VMEM)
    return pl.pallas_call(
        advect_kernel,
        in_specs=[whole] * 8,
        out_specs=[whole] * 3,
        out_shape=[
            jax.ShapeDtypeStruct((NF, LEV, ROWS, COLS), BF16),
            jax.ShapeDtypeStruct((G, 128, COLS), F32),
            jax.ShapeDtypeStruct((G, 128, COLS), BF16),
        ],
        scratch_shapes=[pltpu.VMEM((8, NF * ROWS, COLS), F32)],
        compiler_params=params(),
        name="advect",
    )(*plan, fields, west, east)


SLOTS = 20


def slot_of_lane(shape=(8, COLS)):
    return ((lane_iota(shape) + 3) & (COLS - 1)) // 6


def split3(x):
    a = x.astype(BF16)
    rest = x - a.astype(F32)
    b = rest.astype(BF16)
    c = (rest - b.astype(F32)).astype(BF16)
    return a, b, c


def prepare_kernel(
    mix_ref, shift_ref, frac_ref, mode_ref, cells_ref, source_ref, weight_ref, proj_ref,
    mix_out_ref, mask_ref, own_ref, matrix_ref, taps_ref, mode_out_ref,
    pick_ref, place_ref, in_row_ref, covered_ref, src_row_ref, wgt_ref, proj_out_ref,
):
    advect_plan(mix_ref, shift_ref, frac_ref, mix_out_ref, mask_ref, own_ref, matrix_ref, taps_ref)
    mode_out_ref[...] = mode_ref[...]
    proj_out_ref[...] = proj_ref[...]
    src = jnp.concatenate([source_ref[q : q + 1, :] for q in range(4)], axis=1)
    wgt = jnp.concatenate([weight_ref[q : q + 1, :] for q in range(4)], axis=1)
    wide = (COLS, 4 * OV)
    col = jnp.broadcast_to(src & (COLS - 1), wide)
    pick_ref[...] = jnp.where(lax.broadcasted_iota(jnp.int32, wide, 0) == col, 1.0, 0.0).astype(BF16)
    src_row_ref[...] = jnp.broadcast_to(src >> 7, (8, 4 * OV))
    wgt_ref[...] = jnp.broadcast_to(wgt, (8, 4 * OV))
    cells = cells_ref[...]
    sub = lax.broadcasted_iota(jnp.int32, (128, OV), 0)
    place = jnp.where(sub == jnp.broadcast_to(cells & (COLS - 1), (128, OV)), 1.0, 0.0).astype(BF16)
    place_ref[...] = place
    in_row = jnp.where((sub >> 3) == jnp.broadcast_to(cells >> 7, (128, OV)), 1.0, 0.0).astype(BF16)
    in_row_ref[...] = in_row
    nt = (((1,), (1,)), ((), ()))
    covered_ref[...] = lax.dot_general(in_row, place, nt, preferred_element_type=F32)


def prepare(*args):
    shapes = [
        ((NF, LEV, 8, COLS), F32),
        ((9, ROWS, COLS), jnp.int16),
        ((ROWS, COLS), jnp.int32),
        ((4, COLS, COLS), BF16),
        ((4, LEV, ROWS, COLS), F32),
        ((1, LEV), F32),
        ((COLS, 4 * OV), BF16),
        ((128, OV), BF16),
        ((128, OV), BF16),
        ((128, COLS), F32),
        ((8, 4 * OV), jnp.int32),
        ((8, 4 * OV), F32),
        ((LEV, LEV), F32),
    ]
    made = pl.pallas_call(
        prepare_kernel,
        in_specs=[pl.BlockSpec(memory_space=pltpu.SMEM)] + [pl.BlockSpec(memory_space=pltpu.VMEM)] * 7,
        out_shape=[jax.ShapeDtypeStruct(shape, dtype) for shape, dtype in shapes],
        compiler_params=params(),
        cost_estimate=pl.CostEstimate(flops=4_000_000, bytes_accessed=2_000_000, transcendentals=0),
        name="prepare",
    )(*args)
    return made[:5], made[5], made[6:]


def margin_kernel(
    rhs_ref, both_ref, pick_ref, place_ref, in_row_ref, covered_ref, src_row_ref, wgt_ref, proj_ref, b_ref, slots_ref
):
    other = 1 - lax.axis_index("panel")
    pick, place = pick_ref[...], place_ref[...]
    src_row, wgt = src_row_ref[...], wgt_ref[...]
    in_row = in_row_ref[...].astype(F32)
    covered = covered_ref[...] > 0.5
    nt = (((1,), (1,)), ((), ()))
    halves = jnp.concatenate([both_ref[other, lb] for lb in range(G)], axis=0)
    cols = jnp.dot(halves, pick, preferred_element_type=F32)
    rep = jnp.zeros((8 * G, 4 * OV), F32)
    for r in range(ROWS):
        weight = jnp.where(src_row == r, wgt, 0.0)
        rows = [cols[128 * lb + 8 * r : 128 * lb + 8 * r + 8] for lb in range(G)]
        rep = rep + jnp.concatenate([weight] * G, axis=0) * jnp.concatenate(rows, axis=0)
    rep = rep[:, :OV] + rep[:, OV : 2 * OV] + rep[:, 2 * OV : 3 * OV] + rep[:, 3 * OV :]
    spread = jnp.concatenate([in_row * jnp.concatenate([rep[8 * lb : 8 * lb + 8]] * ROWS, axis=0) for lb in range(G)], axis=0)
    placed = lax.dot_general(jnp.concatenate(split3(spread), axis=0), place, nt, preferred_element_type=F32)
    placed = placed[:384] + placed[384:768] + placed[768:]
    joined = [jnp.where(covered, placed[128 * lb : 128 * lb + 128], rhs_ref[lb]) for lb in range(G)]
    levels = jnp.concatenate(
        [jnp.concatenate([joined[lb][8 * r : 8 * r + 8] for lb in range(G)], axis=0) for r in range(ROWS)], axis=1
    )
    modal = jnp.dot(proj_ref[...], levels, precision=lax.Precision.HIGHEST, preferred_element_type=F32)
    for lb in range(G):
        for r in range(ROWS):
            b_ref[lb, 8 * r : 8 * r + 8, :] = modal[8 * lb : 8 * lb + 8, COLS * r : COLS * r + COLS]
    lat, lon = lax.axis_index("lat"), lax.axis_index("lon")
    place_in_square = 2 * (lat & 1) + (lon & 1)
    for lb in range(G):
        slots_ref[place_in_square ^ 2, lb] = b_ref[lb, pl.ds(pl.multiple_of(8 * 13 * (1 - (lat & 1)), 8), 24), :]
        acc = jnp.zeros((8, COLS), F32)
        for i in range(SLOTS):
            r = (i - 2) % ROWS
            acc = jnp.where(slot_of_lane() == i, roll_lanes(b_ref[lb, 8 * r : 8 * r + 8, :], 6 * i), acc)
        slots_ref[place_in_square ^ 1, lb, 0:8, :] = acc
        slots_ref[place_in_square ^ 3, lb, 0:8, :] = acc


def margin(rhs, both, lists):
    return pl.pallas_call(
        margin_kernel,
        out_shape=[
            jax.ShapeDtypeStruct((G, 128, COLS), F32),
            jax.ShapeDtypeStruct((4, G, 24, COLS), F32),
        ],
        compiler_params=params(),
        name="margin",
    )(rhs, both, *lists)


def second_kernel(b_ref, first_ref, got_ref, out_ref):
    lat, lon = lax.axis_index("lat"), lax.axis_index("lon")
    here = 2 * (lat & 1) + (lon & 1)
    there = 3 - here
    even = jnp.broadcast_to(lat & 1, (8, COLS)) == 0
    slot = slot_of_lane()
    for lb in range(G):
        out_ref[there ^ 2, lb, 0:24, :] = b_ref[lb, pl.ds(pl.multiple_of(8 * 13 * (lat & 1), 8), 24), :]
        out_ref[there ^ 2, lb, 24:32, :] = got_ref[here ^ 1, lb, 0:8, :]
        own = first_ref[here ^ 1, lb, 0:8, :]
        out_ref[there ^ 3, lb, 24:32, :] = own
        row = [got_ref[here ^ 2, lb, 8 * n : 8 * n + 8, :] for n in range(3)]
        with_south = jnp.where(slot == 18, roll_lanes(row[0], 6 * 18), jnp.where(slot == 19, roll_lanes(row[1], 6 * 19), own))
        with_north = jnp.where(slot == 0, row[1], jnp.where(slot == 1, roll_lanes(row[2], 6), own))
        out_ref[there ^ 1, lb, 24:32, :] = jnp.where(even, with_south, with_north)


def second(b, first, got):
    return pl.pallas_call(
        second_kernel,
        out_shape=jax.ShapeDtypeStruct((4, G, 32, COLS), F32),
        compiler_params=params(),
        name="second",
    )(b, first, got)


def images_kernel(shift_ref, b_ref, first_ref, second_ref, adv_ref, c_ref, u1_ref, u2_ref, s_ref, adv_hbm, sem):
    leaving = pltpu.make_async_copy(adv_ref, adv_hbm, sem)
    leaving.start()
    lat, lon = lax.axis_index("lat"), lax.axis_index("lon")
    one = jnp.float32(1.0)
    zero = jnp.float32(0.0)
    has_n = jnp.where(lat > 0, one, zero)
    has_s = jnp.where(lat < lax.axis_size("lat") - 1, one, zero)
    has_w = jnp.where(lon > 0, one, zero)
    has_e = jnp.where(lon < lax.axis_size("lon") - 1, one, zero)
    shape = (8 * G, COLS)
    lane = lane_iota(shape)
    first, last = lane == 0, lane == COLS - 1
    side = jnp.where(lane < 64, has_e, has_w)
    here = 2 * (lat & 1) + (lon & 1)
    there = 3 - here
    lat_even = jnp.broadcast_to(lat & 1, shape) == 0
    slot = slot_of_lane(shape)
    from_east = ((lane % 6) < 3) & (lane < 120)
    north_slot, south_slot = slot < 2, (slot == 18) | (slot == 19)
    inside = jnp.where(from_east, has_e, has_w)
    inside = jnp.where(north_slot, inside * has_n, jnp.where(south_slot, inside * has_s, inside)) > 0.5
    first_side = (lat_even & south_slot) | (~lat_even & north_slot)
    second_side = (lat_even & north_slot) | (~lat_even & south_slot)
    east_first = jnp.where(from_east, 1, 0) == jnp.broadcast_to(1 - (lon & 1), shape)

    def rows_of(ref, *at):
        return jnp.concatenate([ref[(*at[:-1], lb, at[-1])] for lb in range(G)], axis=0)

    def store(ref, j, value):
        for lb in range(G):
            ref[lb, 8 * j : 8 * j + 8, :] = value[8 * lb : 8 * lb + 8]

    def line(main, ext):
        return roll_lanes(jnp.where(last, ext, main), 1) + roll_lanes(jnp.where(first, ext, main), -1)

    def row_scale(j):
        return has_n if j < 0 else has_s if j >= ROWS else None

    modes = jnp.broadcast_to(shift_ref[...], (8 * G, LEV))
    diag = lane_iota((8 * G, LEV)) == lax.broadcasted_iota(jnp.int32, (8 * G, LEV), 0)
    a = jnp.broadcast_to(4.0 + jnp.sum(jnp.where(diag, modes, 0.0), axis=1, keepdims=True), shape)
    columns, forwarded = slice(0, 8), slice(24, 32)
    near = jnp.where(first_side, rows_of(first_ref, here ^ 3, columns), rows_of(first_ref, here ^ 1, columns))
    near = jnp.where(second_side, rows_of(second_ref, there ^ 2, forwarded), near)
    far = jnp.where(second_side, rows_of(second_ref, there ^ 3, forwarded), rows_of(second_ref, there ^ 1, forwarded))
    packed = jnp.where(inside, jnp.where(east_first, near, far), 0.0)

    def b_main(j):
        if 0 <= j < ROWS:
            return rows_of(b_ref, slice(8 * j, 8 * j + 8))
        n = j + 3 if j < 0 else j - ROWS
        rows = slice(8 * n, 8 * n + 8)
        one, two = rows_of(first_ref, here ^ 2, rows), rows_of(second_ref, there ^ 2, rows)
        if j < 0:
            return jnp.where(has_n > 0.5, jnp.where(lat_even, two, one), 0.0)
        return jnp.where(has_s > 0.5, jnp.where(lat_even, one, two), 0.0)

    bm = {j: b_main(j) for j in (-3, -2)}
    bx = {-2: packed}
    cm, cx, um, ux = {}, {}, {}, {}
    sums = [jnp.zeros(shape, F32) for _ in range(8)]
    for j in range(-2, ROWS + 4):
        if j <= ROWS + 1:
            bm[j + 1] = b_main(j + 1)
            if j + 1 <= ROWS + 1:
                bx[j + 1] = roll_lanes(packed, -6 * (j + 3))
            value = a * bm[j] - (bm[j - 1] + bm[j + 1] + line(bm[j], bx[j]))
            scale = row_scale(j)
            cm[j] = value if scale is None else value * scale
            if -1 <= j <= ROWS:
                value = (a * bx[j] - (bx[j - 1] + bx[j + 1] + line(bx[j], bm[j]))) * side
                cx[j] = value if scale is None else value * scale
            if 0 <= j < ROWS:
                store(c_ref, j, cm[j])
        i = j - 1
        if -1 <= i <= ROWS:
            value = 0.25 * (cm[i - 1] + cm[i + 1] + line(cm[i], cx[i]))
            scale = row_scale(i)
            um[i] = value if scale is None else value * scale
            if 0 <= i < ROWS:
                ux[i] = 0.25 * (cx[i - 1] + cx[i + 1] + line(cx[i], cm[i])) * side
                store(u1_ref, i, um[i])
        i = j - 2
        if 0 <= i < ROWS:
            u2 = 0.5 * (um[i - 1] + um[i + 1] + line(um[i], ux[i])) - cm[i]
            store(u2_ref, i, u2)
            b, c, u1 = b_main(i), cm[i], um[i]
            pairs = ((b, c), (b, u1), (b, u2), (c, c), (c, u1), (u1, u1), (u1, u2), (u2, u2))
            sums = [s + x * y for s, (x, y) in zip(sums, pairs)]
    lane, sub = lane_iota((8, COLS)), lax.broadcasted_iota(jnp.int32, (8, COLS), 0)
    sums_out = jnp.zeros((8, COLS), F32)
    for q in range(8):
        total = jnp.sum(sums[q], axis=1, keepdims=True)
        for lb in range(G):
            sums_out = jnp.where(lane == 8 * lb + q, total[8 * lb : 8 * lb + 8], sums_out)
    spread = jnp.zeros((8, COLS), F32)
    for m in range(4):
        spread = jnp.where((sub & 3) == m, roll_lanes(sums_out, 32 * m), spread)
    folded = jnp.concatenate([jnp.sum(spread[4 * h : 4 * h + 4], axis=0, keepdims=True) for h in range(2)], axis=0)
    for n in range(s_ref.shape[0]):
        s_ref[n] = folded
    leaving.wait()


def images(mode_shift, b, got_first, got_second, adv, copies):
    full = jax.ShapeDtypeStruct((G, 128, COLS), F32)
    return pl.pallas_call(
        images_kernel,
        in_specs=[pl.BlockSpec(memory_space=pltpu.VMEM)] * 5,
        out_specs=[pl.BlockSpec(memory_space=pltpu.VMEM)] * 4 + [pl.BlockSpec(memory_space=pltpu.HBM)],
        out_shape=[
            full,
            full,
            full,
            jax.ShapeDtypeStruct((copies, 2, COLS), F32),
            jax.ShapeDtypeStruct(adv.shape, adv.dtype),
        ],
        scratch_shapes=[pltpu.SemaphoreType.DMA(())],
        compiler_params=params(),
        name="images",
    )(mode_shift, b, got_first, got_second, adv)


def sum_copies(ref):
    parts = [ref[n] for n in range(ref.shape[0])]
    while len(parts) > 1:
        parts = [parts[n] + parts[n + 1] for n in range(0, len(parts), 2)]
    return parts[0]


def iterate_kernel(shift_ref, s_ref, b_ref, c_ref, u1_ref, u2_ref, sol_ref, res_ref):
    lane = lane_iota((8, COLS))
    total = sum_copies(s_ref)
    sub = lax.broadcasted_iota(jnp.int32, (8, COLS), 0)
    rows = jnp.where(sub < 4, jnp.broadcast_to(total[0:1], (8, COLS)), jnp.broadcast_to(total[1:2], (8, COLS)))
    sums = rows
    for m in range(1, 4):
        sums = jnp.where((sub & 3) == m, roll_lanes(rows, -32 * m), sums)
    for lb in range(G):
        diag = lane_iota((8, LEV)) == (lax.broadcasted_iota(jnp.int32, (8, LEV), 0) + 8 * lb)
        a = 4.0 + jnp.sum(jnp.where(diag, jnp.broadcast_to(shift_ref[...], (8, LEV)), 0.0), axis=1, keepdims=True)
        a = jnp.broadcast_to(a, (8, COLS))

        def inner(q):
            value = jnp.sum(jnp.where(lane == 8 * lb + q, sums, 0.0), axis=1, keepdims=True)
            return jnp.broadcast_to(value, (8, COLS))

        bc, bu1, bu2, cc, cu1, u1u1, u1u2, u2u2 = [inner(q) for q in range(8)]
        cu2 = 2.0 * u1u1 - cc
        l10 = cu1 / cc
        l20 = cu2 / cc
        d1 = u1u1 - l10 * cu1
        e1 = u1u2 - l10 * cu2
        l21 = e1 / d1
        d2 = u2u2 - l20 * cu2 - l21 * e1
        z0 = bc
        z1 = bu1 - l10 * z0
        z2 = bu2 - l20 * z0 - l21 * z1
        y2 = z2 / d2
        y1 = z1 / d1 - l21 * y2
        y0 = z0 / cc - l10 * y1 - l20 * y2
        for r in range(ROWS):
            rows = slice(8 * r, 8 * r + 8)
            b, c, u1, u2 = b_ref[lb, rows, :], c_ref[lb, rows, :], u1_ref[lb, rows, :], u2_ref[lb, rows, :]
            v1 = 0.25 * (a * b - c)
            v2 = 0.5 * (a * v1 - u1) - b
            at = pl.ds(lb * 128 + r, 8, stride=ROWS)
            sol_ref[at, :] = y0 * b + y1 * v1 + y2 * v2
            res_ref[at, :] = b - y0 * c - y1 * u1 - y2 * u2


def iterate(mode_shift, sums, b, c, u1, u2):
    out = jax.ShapeDtypeStruct((LEV * ROWS, COLS), F32)
    return pl.pallas_call(
        iterate_kernel,
        out_shape=[out, out],
        compiler_params=params(),
        name="iterate",
    )(mode_shift, sums, b, c, u1, u2)


def send(block, axis, by):
    count = lax.axis_size(axis)
    return lax.ppermute(block, axis, [(i, i + by) for i in range(count) if 0 <= i + by < count])


def relay_kernel(in_ref, out_ref):
    total = sum_copies(in_ref)
    for n in range(out_ref.shape[0]):
        out_ref[n] = total


def relay(parts, copies):
    return pl.pallas_call(
        relay_kernel,
        out_shape=jax.ShapeDtypeStruct((copies, 2, COLS), F32),
        compiler_params=params(),
        name="relay",
    )(parts)


def in_squares(slots, begin):
    lats, lons = lax.axis_size("lat"), lax.axis_size("lon")
    groups = [
        [((i + a) % lats) * lons + (j + b) % lons for a in (0, 1) for b in (0, 1)]
        for i in range(begin, lats, 2)
        for j in range(begin, lons, 2)
    ]
    return lax.all_to_all(slots, ("lat", "lon"), 0, 0, axis_index_groups=groups)


def per_device(fields, frac, shift, mix, proj, mode_shift, cells, source, weight):
    fields = fields[0]
    table = shift[0]
    plan, modes, lists = prepare(
        mix, table, frac[0], mode_shift.reshape(1, LEV), cells[0], source[0, 0].T, weight[0, 0].T, proj
    )
    packed, fields = pack(table, fields)
    west = send(packed, "lon", 1)
    east = send(pack_east(fields), "lon", -1)
    adv, rhs, half = advect(plan, fields, west, east)
    both = lax.all_gather(half, "panel")
    b, first = margin(rhs, both, lists)
    got_first = in_squares(first, 0)
    got_second = in_squares(second(b, first, got_first), 1)
    count = lax.axis_size("lon")
    rest = lax.axis_size("panel") * lax.axis_size("lat")
    c, u1, u2, sums, adv = images(modes, b, got_first, got_second, adv, count)
    sums = relay(lax.all_to_all(sums, "lon", 0, 0), rest)
    sums = lax.all_to_all(sums, ("panel", "lat"), 0, 0)
    sol, res = iterate(modes, sums, b, c, u1, u2)
    shape = (1, LEV, ROWS, COLS)
    return adv[None], sol.reshape(shape), res.reshape(shape)


def solution(mesh):
    wide = P("panel", None, None, "lat", "lon")
    flat = P("panel", None, "lat", "lon")
    table = P("panel", "lat", "lon", None)
    in_specs = (wide, flat, P("panel", "lat", None), P(), P(), P(), P("panel", "lat", "lon"), table, table)
    return jax.shard_map(per_device, mesh=mesh, in_specs=in_specs, out_specs=(wide, flat, flat), check_vma=False)
```

```python
import jax
import jax.numpy as jnp
from jax import lax
from jax.experimental import pallas as pl
from jax.experimental.pallas import tpu as pltpu
from jax.sharding import PartitionSpec as P

F32 = jnp.float32
BF16 = jnp.bfloat16
NF = 6
LEV = 24
ROWS = 16
COLS = 128
G = 3
OV = 256
VMEM_LIMIT = 48 * 1024 * 1024


def lane_iota(shape):
    return lax.broadcasted_iota(jnp.int32, shape, len(shape) - 1)


def roll_lanes(x, by):
    by = by % COLS
    if by == 0:
        return x
    return pltpu.roll(x, by, x.ndim - 1)


def params():
    return pltpu.CompilerParams(vmem_limit_bytes=VMEM_LIMIT)


def own_shift(shift_ref, lon):
    table = shift_ref[...]
    own = jnp.sum(jnp.where(lane_iota(table.shape) == lon, table, 0), axis=1, keepdims=True)
    return jnp.broadcast_to(own, (ROWS, COLS))


def half_bits(mask):
    return jnp.where(mask, 1, 0).astype(jnp.int16)


def lane_matrix(rule):
    source = lax.broadcasted_iota(jnp.int32, (COLS, COLS), 0)
    target = lax.broadcasted_iota(jnp.int32, (COLS, COLS), 1)
    return jnp.where(rule(source, target), 1.0, 0.0).astype(BF16)


def mirrored(source, target):
    return (target >= 32) & (source == jnp.where((target >> 5) == 2, target, (target + 64) & (COLS - 1)))


def pack_east_kernel(fields_ref, out_ref):
    pair = (lane_iota((ROWS, COLS)) >> 1).astype(jnp.int16)
    for g in range(G):
        acc = jnp.zeros((ROWS, COLS), BF16)
        for f in range(NF):
            for l8 in range(8):
                i = f * 8 + l8
                acc = jnp.where(pair == jnp.int16(i), roll_lanes(fields_ref[f, 8 * g + l8], 2 * i), acc)
        out_ref[g] = acc


def pack_east(fields):
    return pl.pallas_call(
        pack_east_kernel,
        in_specs=[pl.BlockSpec(memory_space=pltpu.VMEM)],
        out_specs=pl.BlockSpec(memory_space=pltpu.VMEM),
        out_shape=jax.ShapeDtypeStruct((G, ROWS, COLS), BF16),
        compiler_params=params(),
        name="pack_east",
    )(fields)


CHUNKS = 1
PER_CHUNK = LEV // CHUNKS


def pack_kernel(shift_hbm, fields_hbm, west_ref, kept_ref, shift_ref, scratch, mask_ref, matrix_ref, sems):
    table = pltpu.make_async_copy(shift_hbm, shift_ref, sems.at[CHUNKS])
    table.start()
    copies = []
    for n in range(CHUNKS):
        part = (slice(None), pl.ds(PER_CHUNK * n, PER_CHUNK))
        copies.append(pltpu.make_async_copy(fields_hbm.at[part], kept_ref.at[part], sems.at[n]))
        copies[-1].start()
    table.wait()
    pack_plan(shift_ref, mask_ref, matrix_ref)
    masks = [mask_ref[n] == 1 for n in range(2)]
    zero = jnp.zeros((ROWS, COLS), BF16)
    low = (lax.broadcasted_iota(jnp.int32, (NF * ROWS, COLS), 0) & 1) == 0
    for n in range(CHUNKS):
        copies[n].wait()
        for level in range(PER_CHUNK * n, PER_CHUNK * n + PER_CHUNK):
            parts = [
                jnp.concatenate([jnp.where(m, kept_ref[f, level], zero) for m in masks], axis=1) for f in range(NF)
            ]
            wide = jnp.dot(jnp.concatenate(parts, axis=0), matrix_ref[...], preferred_element_type=F32)
            scratch[level % 8] = jnp.where(low, wide[:, :COLS], wide[:, COLS:])
            pairs = scratch[level % 8, pl.ds(0, 8 * NF, stride=2), :] + scratch[level % 8, pl.ds(1, 8 * NF, stride=2), :]
            pairs = pairs.astype(BF16)
            for m in range(NF // 2):
                west_ref[m, level] = pairs[ROWS * m : ROWS * m + ROWS]


def pack_plan(shift_ref, mask_ref, matrix_ref):
    shift = own_shift(shift_ref, lax.axis_index("lon") + 1)
    lane = lane_iota((ROWS, COLS))
    mask_ref[0] = half_bits(lane >= COLS - 32 * shift)
    mask_ref[1] = half_bits(lane == COLS - 1 - 32 * shift)
    rules = (
        (lambda s, t: s == t, mirrored),
        (lambda s, t: ((s & 31) == 31) & (t == 31), lambda s, t: ((s & 31) == 31) & (t == 30)),
    )
    for m, pair in enumerate(rules):
        for n, rule in enumerate(pair):
            matrix_ref[COLS * m : COLS * m + COLS, COLS * n : COLS * n + COLS] = lane_matrix(rule)


def pack(shift, fields):
    return pl.pallas_call(
        pack_kernel,
        in_specs=[pl.BlockSpec(memory_space=pltpu.HBM)] * 2,
        out_specs=[pl.BlockSpec(memory_space=pltpu.VMEM)] * 2,
        out_shape=[
            jax.ShapeDtypeStruct((NF // 2, LEV, ROWS, COLS), BF16),
            jax.ShapeDtypeStruct((NF, LEV, ROWS, COLS), BF16),
        ],
        scratch_shapes=[
            pltpu.VMEM((ROWS, 32), jnp.int32),
            pltpu.VMEM((8, NF * ROWS, COLS), F32),
            pltpu.VMEM((2, ROWS, COLS), jnp.int16),
            pltpu.VMEM((2 * COLS, 2 * COLS), BF16),
            pltpu.SemaphoreType.DMA((CHUNKS + 1,)),
        ],
        compiler_params=params(),
        name="pack",
    )(*(pltpu.with_memory_space_constraint(x, pltpu.HBM) for x in (shift, fields)))


TAPS = (-1, 0, 1, 2)


def turn(x, sign, odd, two):
    x = jnp.where(odd, roll_lanes(x, 32 * sign), x)
    return jnp.where(two, roll_lanes(x, 64), x)


def advect_plan(mix_ref, shift_ref, frac_ref, mix_out_ref, mask_ref, shift_out_ref, matrix_ref, weight_ref):
    for f in range(NF):
        for level in range(LEV):
            mix_out_ref[f, level] = jnp.full((8, COLS), mix_ref[f, level], F32)
    shift = own_shift(shift_ref, lax.axis_index("lon"))
    shift_out_ref[...] = shift
    lane = lane_iota((ROWS, COLS))
    low = (lax.broadcasted_iota(jnp.int32, (ROWS, COLS), 0) & 1) == 0
    odd, two = (shift & 1) == 1, (shift & 2) == 2

    def beyond(j):
        at = ((lane - j + 32 * shift) & (COLS - 1)) - 32 * shift + j
        return (at < 0) | (at >= COLS)

    masks = [beyond(j) for j in TAPS]
    masks += [odd, two, lane < 2, ~low & ((lane >> 5) != 2), lane == jnp.where(low, 31, 30)]
    for n, mask in enumerate(masks):
        mask_ref[n] = half_bits(mask)
    rules = [lambda s, t, j=j: s == ((t + j) & (COLS - 1)) for j in TAPS if j]
    rules.append(lambda s, t: ((s == 30) | (s == 31)) & ((t & 31) == 0))
    for n, rule in enumerate(rules):
        matrix_ref[n] = lane_matrix(rule)
    for level in range(LEV):
        t = turn(frac_ref[level], -1, odd, two)
        tm1, tm2, tp1 = t - 1.0, t - 2.0, t + 1.0
        weight_ref[0, level] = -t * tm1 * tm2 * (1.0 / 6.0)
        weight_ref[1, level] = tp1 * tm1 * tm2 * 0.5
        weight_ref[2, level] = -tp1 * t * tm2 * 0.5
        weight_ref[3, level] = tp1 * t * tm1 * (1.0 / 6.0)


def advect_kernel(
    mix_ref, mask_ref, shift_ref, matrix_ref, weight_ref, fields_ref, west_ref, east_ref, adv_ref, rhs_ref, half_ref, scratch
):
    shift = shift_ref[...]
    lane = lane_iota((ROWS, COLS))
    odd, two = (shift & 1) == 1, (shift & 2) == 2
    bits = [mask_ref[n] == 1 for n in range(9)]
    masks, (odd16, two16, edge16, swap16, single16) = bits[:4], bits[4:]
    single_at = lane == ((COLS - 32 * shift) & (COLS - 1))
    zero = jnp.zeros((ROWS, COLS), BF16)

    @pl.loop(0, G)
    def _(g):
        east = east_ref[g]
        for batch in (range(8),):
            chosen = [[] for _ in TAPS]
            singles = []
            for l8 in batch:
                level = g * 8 + l8
                shared = jnp.concatenate([west_ref[n, level] for n in range(NF // 2)], axis=0).astype(F32)
                scratch[l8, pl.ds(0, 8 * NF, stride=2), :] = shared
                scratch[l8, pl.ds(1, 8 * NF, stride=2), :] = shared
            for l8 in batch:
                level = g * 8 + l8
                west = scratch[l8].astype(BF16)
                for f in range(NF):
                    other = west[ROWS * f : ROWS * f + ROWS]
                    singles.append(jnp.where(single16, other, zero))
                    other = jnp.where(swap16, roll_lanes(other, 64), other)
                    other = jnp.where(edge16, roll_lanes(east, -2 * (f * 8 + l8)), other)
                    own = fields_ref[f, level]
                    for n, mask in enumerate(masks):
                        chosen[n].append(jnp.where(mask, other, own))
            wide = [
                jnp.dot(jnp.concatenate(chosen[tap], axis=0), matrix_ref[n], preferred_element_type=F32)
                for n, tap in ((0, 0), (1, 2), (2, 3))
            ]
            column = jnp.dot(jnp.concatenate(singles, axis=0), matrix_ref[3], preferred_element_type=F32)
            for k, l8 in enumerate(batch):
                level = g * 8 + l8
                weights = [weight_ref[n, level] for n in range(4)]
                total = jnp.zeros((ROWS, COLS), F32)
                for f in range(NF):
                    i = k * NF + f
                    at = slice(ROWS * i, ROWS * i + ROWS)
                    acc = weights[0] * jnp.where(single_at, column[at], wide[0][at])
                    acc = acc + weights[1] * chosen[1][i].astype(F32)
                    acc = acc + weights[2] * wide[1][at]
                    acc = acc + weights[3] * wide[2][at]
                    rounded = acc.astype(BF16)
                    adv_ref[f, level] = turn(rounded, 1, odd16, two16)
                    mix = mix_ref[f, level]
                    total = total + jnp.concatenate([mix, mix], axis=0) * rounded.astype(F32)
                rhs_ref[g, pl.ds(l8, ROWS, stride=8), :] = turn(total, 1, odd, two)
        half_ref[g] = rhs_ref[g].astype(BF16)


def advect(plan, fields, west, east):
    whole = pl.BlockSpec(memory_space=pltpu.VMEM)
    return pl.pallas_call(
        advect_kernel,
        in_specs=[whole] * 8,
        out_specs=[whole] * 3,
        out_shape=[
            jax.ShapeDtypeStruct((NF, LEV, ROWS, COLS), BF16),
            jax.ShapeDtypeStruct((G, 128, COLS), F32),
            jax.ShapeDtypeStruct((G, 128, COLS), BF16),
        ],
        scratch_shapes=[pltpu.VMEM((8, NF * ROWS, COLS), F32)],
        compiler_params=params(),
        name="advect",
    )(*plan, fields, west, east)


SLOTS = 20


def slot_of_lane(shape=(8, COLS)):
    return ((lane_iota(shape) + 3) & (COLS - 1)) // 6


def split3(x):
    a = x.astype(BF16)
    rest = x - a.astype(F32)
    b = rest.astype(BF16)
    c = (rest - b.astype(F32)).astype(BF16)
    return a, b, c


def prepare_kernel(
    mix_ref, shift_ref, frac_ref, mode_ref, cells_ref, source_ref, weight_ref, proj_ref,
    mix_out_ref, mask_ref, own_ref, matrix_ref, taps_ref, mode_out_ref,
    pick_ref, place_ref, in_row_ref, covered_ref, src_row_ref, wgt_ref, proj_out_ref,
):
    advect_plan(mix_ref, shift_ref, frac_ref, mix_out_ref, mask_ref, own_ref, matrix_ref, taps_ref)
    mode_out_ref[...] = mode_ref[...]
    proj_out_ref[...] = proj_ref[...]
    src = jnp.concatenate([source_ref[q : q + 1, :] for q in range(4)], axis=1)
    wgt = jnp.concatenate([weight_ref[q : q + 1, :] for q in range(4)], axis=1)
    wide = (COLS, 4 * OV)
    col = jnp.broadcast_to(src & (COLS - 1), wide)
    pick_ref[...] = jnp.where(lax.broadcasted_iota(jnp.int32, wide, 0) == col, 1.0, 0.0).astype(BF16)
    src_row_ref[...] = jnp.broadcast_to(src >> 7, (8, 4 * OV))
    wgt_ref[...] = jnp.broadcast_to(wgt, (8, 4 * OV))
    cells = cells_ref[...]
    sub = lax.broadcasted_iota(jnp.int32, (128, OV), 0)
    place = jnp.where(sub == jnp.broadcast_to(cells & (COLS - 1), (128, OV)), 1.0, 0.0).astype(BF16)
    place_ref[...] = place
    in_row = jnp.where((sub >> 3) == jnp.broadcast_to(cells >> 7, (128, OV)), 1.0, 0.0).astype(BF16)
    in_row_ref[...] = in_row
    nt = (((1,), (1,)), ((), ()))
    covered_ref[...] = lax.dot_general(in_row, place, nt, preferred_element_type=F32)


def prepare(*args):
    shapes = [
        ((NF, LEV, 8, COLS), F32),
        ((9, ROWS, COLS), jnp.int16),
        ((ROWS, COLS), jnp.int32),
        ((4, COLS, COLS), BF16),
        ((4, LEV, ROWS, COLS), F32),
        ((1, LEV), F32),
        ((COLS, 4 * OV), BF16),
        ((128, OV), BF16),
        ((128, OV), BF16),
        ((128, COLS), F32),
        ((8, 4 * OV), jnp.int32),
        ((8, 4 * OV), F32),
        ((LEV, LEV), F32),
    ]
    made = pl.pallas_call(
        prepare_kernel,
        in_specs=[pl.BlockSpec(memory_space=pltpu.SMEM)] + [pl.BlockSpec(memory_space=pltpu.VMEM)] * 7,
        out_shape=[jax.ShapeDtypeStruct(shape, dtype) for shape, dtype in shapes],
        compiler_params=params(),
        cost_estimate=pl.CostEstimate(flops=4_000_000, bytes_accessed=2_000_000, transcendentals=0),
        name="prepare",
    )(*args)
    return made[:5], made[5], made[6:]


def margin_kernel(
    rhs_ref, both_ref, pick_ref, place_ref, in_row_ref, covered_ref, src_row_ref, wgt_ref, proj_ref, b_ref, slots_ref
):
    other = 1 - lax.axis_index("panel")
    pick, place = pick_ref[...], place_ref[...]
    src_row, wgt = src_row_ref[...], wgt_ref[...]
    in_row = in_row_ref[...].astype(F32)
    covered = covered_ref[...] > 0.5
    nt = (((1,), (1,)), ((), ()))
    halves = jnp.concatenate([both_ref[other, lb] for lb in range(G)], axis=0)
    cols = jnp.dot(halves, pick, preferred_element_type=F32)
    rep = jnp.zeros((8 * G, 4 * OV), F32)
    for r in range(ROWS):
        weight = jnp.where(src_row == r, wgt, 0.0)
        rows = [cols[128 * lb + 8 * r : 128 * lb + 8 * r + 8] for lb in range(G)]
        rep = rep + jnp.concatenate([weight] * G, axis=0) * jnp.concatenate(rows, axis=0)
    rep = rep[:, :OV] + rep[:, OV : 2 * OV] + rep[:, 2 * OV : 3 * OV] + rep[:, 3 * OV :]
    spread = jnp.concatenate([in_row * jnp.concatenate([rep[8 * lb : 8 * lb + 8]] * ROWS, axis=0) for lb in range(G)], axis=0)
    placed = lax.dot_general(jnp.concatenate(split3(spread), axis=0), place, nt, preferred_element_type=F32)
    placed = placed[:384] + placed[384:768] + placed[768:]
    joined = [jnp.where(covered, placed[128 * lb : 128 * lb + 128], rhs_ref[lb]) for lb in range(G)]
    levels = jnp.concatenate(
        [jnp.concatenate([joined[lb][8 * r : 8 * r + 8] for lb in range(G)], axis=0) for r in range(ROWS)], axis=1
    )
    modal = jnp.dot(proj_ref[...], levels, precision=lax.Precision.HIGHEST, preferred_element_type=F32)
    for lb in range(G):
        for r in range(ROWS):
            b_ref[lb, 8 * r : 8 * r + 8, :] = modal[8 * lb : 8 * lb + 8, COLS * r : COLS * r + COLS]
    lat, lon = lax.axis_index("lat"), lax.axis_index("lon")
    place_in_square = 2 * (lat & 1) + (lon & 1)
    for lb in range(G):
        slots_ref[place_in_square ^ 2, lb] = b_ref[lb, pl.ds(pl.multiple_of(8 * 13 * (1 - (lat & 1)), 8), 24), :]
        acc = jnp.zeros((8, COLS), F32)
        for i in range(SLOTS):
            r = (i - 2) % ROWS
            acc = jnp.where(slot_of_lane() == i, roll_lanes(b_ref[lb, 8 * r : 8 * r + 8, :], 6 * i), acc)
        slots_ref[place_in_square ^ 1, lb, 0:8, :] = acc
        slots_ref[place_in_square ^ 3, lb, 0:8, :] = acc


def margin(rhs, both, lists):
    return pl.pallas_call(
        margin_kernel,
        out_shape=[
            jax.ShapeDtypeStruct((G, 128, COLS), F32),
            jax.ShapeDtypeStruct((4, G, 24, COLS), F32),
        ],
        compiler_params=params(),
        name="margin",
    )(rhs, both, *lists)


def second_kernel(b_ref, first_ref, got_ref, out_ref):
    lat, lon = lax.axis_index("lat"), lax.axis_index("lon")
    here = 2 * (lat & 1) + (lon & 1)
    there = 3 - here
    even = jnp.broadcast_to(lat & 1, (8, COLS)) == 0
    slot = slot_of_lane()
    for lb in range(G):
        out_ref[there ^ 2, lb, 0:24, :] = b_ref[lb, pl.ds(pl.multiple_of(8 * 13 * (lat & 1), 8), 24), :]
        out_ref[there ^ 2, lb, 24:32, :] = got_ref[here ^ 1, lb, 0:8, :]
        own = first_ref[here ^ 1, lb, 0:8, :]
        out_ref[there ^ 3, lb, 24:32, :] = own
        row = [got_ref[here ^ 2, lb, 8 * n : 8 * n + 8, :] for n in range(3)]
        with_south = jnp.where(slot == 18, roll_lanes(row[0], 6 * 18), jnp.where(slot == 19, roll_lanes(row[1], 6 * 19), own))
        with_north = jnp.where(slot == 0, row[1], jnp.where(slot == 1, roll_lanes(row[2], 6), own))
        out_ref[there ^ 1, lb, 24:32, :] = jnp.where(even, with_south, with_north)


def second(b, first, got):
    return pl.pallas_call(
        second_kernel,
        out_shape=jax.ShapeDtypeStruct((4, G, 32, COLS), F32),
        compiler_params=params(),
        name="second",
    )(b, first, got)


def images_kernel(shift_ref, b_ref, first_ref, second_ref, adv_ref, c_ref, u1_ref, u2_ref, s_ref, adv_hbm, sem):
    leaving = pltpu.make_async_copy(adv_ref, adv_hbm, sem)
    leaving.start()
    lat, lon = lax.axis_index("lat"), lax.axis_index("lon")
    one = jnp.float32(1.0)
    zero = jnp.float32(0.0)
    has_n = jnp.where(lat > 0, one, zero)
    has_s = jnp.where(lat < lax.axis_size("lat") - 1, one, zero)
    has_w = jnp.where(lon > 0, one, zero)
    has_e = jnp.where(lon < lax.axis_size("lon") - 1, one, zero)
    shape = (8 * G, COLS)
    lane = lane_iota(shape)
    first, last = lane == 0, lane == COLS - 1
    side = jnp.where(lane < 64, has_e, has_w)
    here = 2 * (lat & 1) + (lon & 1)
    there = 3 - here
    lat_even = jnp.broadcast_to(lat & 1, shape) == 0
    slot = slot_of_lane(shape)
    from_east = ((lane % 6) < 3) & (lane < 120)
    north_slot, south_slot = slot < 2, (slot == 18) | (slot == 19)
    inside = jnp.where(from_east, has_e, has_w)
    inside = jnp.where(north_slot, inside * has_n, jnp.where(south_slot, inside * has_s, inside)) > 0.5
    first_side = (lat_even & south_slot) | (~lat_even & north_slot)
    second_side = (lat_even & north_slot) | (~lat_even & south_slot)
    east_first = jnp.where(from_east, 1, 0) == jnp.broadcast_to(1 - (lon & 1), shape)

    def rows_of(ref, *at):
        return jnp.concatenate([ref[(*at[:-1], lb, at[-1])] for lb in range(G)], axis=0)

    def store(ref, j, value):
        for lb in range(G):
            ref[lb, 8 * j : 8 * j + 8, :] = value[8 * lb : 8 * lb + 8]

    def line(main, ext):
        return roll_lanes(jnp.where(last, ext, main), 1) + roll_lanes(jnp.where(first, ext, main), -1)

    def row_scale(j):
        return has_n if j < 0 else has_s if j >= ROWS else None

    modes = jnp.broadcast_to(shift_ref[...], (8 * G, LEV))
    diag = lane_iota((8 * G, LEV)) == lax.broadcasted_iota(jnp.int32, (8 * G, LEV), 0)
    a = jnp.broadcast_to(4.0 + jnp.sum(jnp.where(diag, modes, 0.0), axis=1, keepdims=True), shape)
    columns, forwarded = slice(0, 8), slice(24, 32)
    near = jnp.where(first_side, rows_of(first_ref, here ^ 3, columns), rows_of(first_ref, here ^ 1, columns))
    near = jnp.where(second_side, rows_of(second_ref, there ^ 2, forwarded), near)
    far = jnp.where(second_side, rows_of(second_ref, there ^ 3, forwarded), rows_of(second_ref, there ^ 1, forwarded))
    packed = jnp.where(inside, jnp.where(east_first, near, far), 0.0)

    def b_main(j):
        if 0 <= j < ROWS:
            return rows_of(b_ref, slice(8 * j, 8 * j + 8))
        n = j + 3 if j < 0 else j - ROWS
        rows = slice(8 * n, 8 * n + 8)
        one, two = rows_of(first_ref, here ^ 2, rows), rows_of(second_ref, there ^ 2, rows)
        if j < 0:
            return jnp.where(has_n > 0.5, jnp.where(lat_even, two, one), 0.0)
        return jnp.where(has_s > 0.5, jnp.where(lat_even, one, two), 0.0)

    bm = {j: b_main(j) for j in (-3, -2)}
    bx = {-2: packed}
    cm, cx, um, ux = {}, {}, {}, {}
    sums = [jnp.zeros(shape, F32) for _ in range(8)]
    for j in range(-2, ROWS + 4):
        if j <= ROWS + 1:
            bm[j + 1] = b_main(j + 1)
            if j + 1 <= ROWS + 1:
                bx[j + 1] = roll_lanes(packed, -6 * (j + 3))
            value = a * bm[j] - (bm[j - 1] + bm[j + 1] + line(bm[j], bx[j]))
            scale = row_scale(j)
            cm[j] = value if scale is None else value * scale
            if -1 <= j <= ROWS:
                value = (a * bx[j] - (bx[j - 1] + bx[j + 1] + line(bx[j], bm[j]))) * side
                cx[j] = value if scale is None else value * scale
            if 0 <= j < ROWS:
                store(c_ref, j, cm[j])
        i = j - 1
        if -1 <= i <= ROWS:
            value = 0.25 * (cm[i - 1] + cm[i + 1] + line(cm[i], cx[i]))
            scale = row_scale(i)
            um[i] = value if scale is None else value * scale
            if 0 <= i < ROWS:
                ux[i] = 0.25 * (cx[i - 1] + cx[i + 1] + line(cx[i], cm[i])) * side
                store(u1_ref, i, um[i])
        i = j - 2
        if 0 <= i < ROWS:
            u2 = 0.5 * (um[i - 1] + um[i + 1] + line(um[i], ux[i])) - cm[i]
            store(u2_ref, i, u2)
            b, c, u1 = b_main(i), cm[i], um[i]
            pairs = ((b, c), (b, u1), (b, u2), (c, c), (c, u1), (u1, u1), (u1, u2), (u2, u2))
            sums = [s + x * y for s, (x, y) in zip(sums, pairs)]
    lane, sub = lane_iota((8, COLS)), lax.broadcasted_iota(jnp.int32, (8, COLS), 0)
    sums_out = jnp.zeros((8, COLS), F32)
    for q in range(8):
        total = jnp.sum(sums[q], axis=1, keepdims=True)
        for lb in range(G):
            sums_out = jnp.where(lane == 8 * lb + q, total[8 * lb : 8 * lb + 8], sums_out)
    spread = jnp.zeros((8, COLS), F32)
    for m in range(4):
        spread = jnp.where((sub & 3) == m, roll_lanes(sums_out, 32 * m), spread)
    folded = jnp.concatenate([jnp.sum(spread[4 * h : 4 * h + 4], axis=0, keepdims=True) for h in range(2)], axis=0)
    for n in range(s_ref.shape[0]):
        s_ref[n] = folded
    leaving.wait()


def images(mode_shift, b, got_first, got_second, adv, copies):
    full = jax.ShapeDtypeStruct((G, 128, COLS), F32)
    return pl.pallas_call(
        images_kernel,
        in_specs=[pl.BlockSpec(memory_space=pltpu.VMEM)] * 5,
        out_specs=[pl.BlockSpec(memory_space=pltpu.VMEM)] * 4 + [pl.BlockSpec(memory_space=pltpu.HBM)],
        out_shape=[
            full,
            full,
            full,
            jax.ShapeDtypeStruct((copies, 2, COLS), F32),
            jax.ShapeDtypeStruct(adv.shape, adv.dtype),
        ],
        scratch_shapes=[pltpu.SemaphoreType.DMA(())],
        compiler_params=params(),
        name="images",
    )(mode_shift, b, got_first, got_second, adv)


def sum_copies(ref):
    parts = [ref[n] for n in range(ref.shape[0])]
    while len(parts) > 1:
        parts = [parts[n] + parts[n + 1] for n in range(0, len(parts), 2)]
    return parts[0]


def iterate_kernel(shift_ref, s_ref, b_ref, c_ref, u1_ref, u2_ref, sol_ref, res_ref):
    lane = lane_iota((8, COLS))
    total = sum_copies(s_ref)
    sub = lax.broadcasted_iota(jnp.int32, (8, COLS), 0)
    rows = jnp.where(sub < 4, jnp.broadcast_to(total[0:1], (8, COLS)), jnp.broadcast_to(total[1:2], (8, COLS)))
    sums = rows
    for m in range(1, 4):
        sums = jnp.where((sub & 3) == m, roll_lanes(rows, -32 * m), sums)
    for lb in range(G):
        diag = lane_iota((8, LEV)) == (lax.broadcasted_iota(jnp.int32, (8, LEV), 0) + 8 * lb)
        a = 4.0 + jnp.sum(jnp.where(diag, jnp.broadcast_to(shift_ref[...], (8, LEV)), 0.0), axis=1, keepdims=True)
        a = jnp.broadcast_to(a, (8, COLS))

        def inner(q):
            value = jnp.sum(jnp.where(lane == 8 * lb + q, sums, 0.0), axis=1, keepdims=True)
            return jnp.broadcast_to(value, (8, COLS))

        bc, bu1, bu2, cc, cu1, u1u1, u1u2, u2u2 = [inner(q) for q in range(8)]
        cu2 = 2.0 * u1u1 - cc
        l10 = cu1 / cc
        l20 = cu2 / cc
        d1 = u1u1 - l10 * cu1
        e1 = u1u2 - l10 * cu2
        l21 = e1 / d1
        d2 = u2u2 - l20 * cu2 - l21 * e1
        z0 = bc
        z1 = bu1 - l10 * z0
        z2 = bu2 - l20 * z0 - l21 * z1
        y2 = z2 / d2
        y1 = z1 / d1 - l21 * y2
        y0 = z0 / cc - l10 * y1 - l20 * y2
        for r in range(ROWS):
            rows = slice(8 * r, 8 * r + 8)
            b, c, u1, u2 = b_ref[lb, rows, :], c_ref[lb, rows, :], u1_ref[lb, rows, :], u2_ref[lb, rows, :]
            v1 = 0.25 * (a * b - c)
            v2 = 0.5 * (a * v1 - u1) - b
            at = pl.ds(lb * 128 + r, 8, stride=ROWS)
            sol_ref[at, :] = y0 * b + y1 * v1 + y2 * v2
            res_ref[at, :] = b - y0 * c - y1 * u1 - y2 * u2


def iterate(mode_shift, sums, b, c, u1, u2):
    out = jax.ShapeDtypeStruct((LEV * ROWS, COLS), F32)
    return pl.pallas_call(
        iterate_kernel,
        out_shape=[out, out],
        compiler_params=params(),
        name="iterate",
    )(mode_shift, sums, b, c, u1, u2)


def send(block, axis, by):
    count = lax.axis_size(axis)
    return lax.ppermute(block, axis, [(i, i + by) for i in range(count) if 0 <= i + by < count])


def relay_kernel(in_ref, out_ref):
    total = sum_copies(in_ref)
    for n in range(out_ref.shape[0]):
        out_ref[n] = total


def relay(parts, copies):
    return pl.pallas_call(
        relay_kernel,
        out_shape=jax.ShapeDtypeStruct((copies, 2, COLS), F32),
        compiler_params=params(),
        name="relay",
    )(parts)


def in_squares(slots, begin):
    lats, lons = lax.axis_size("lat"), lax.axis_size("lon")
    groups = [
        [((i + a) % lats) * lons + (j + b) % lons for a in (0, 1) for b in (0, 1)]
        for i in range(begin, lats, 2)
        for j in range(begin, lons, 2)
    ]
    return lax.all_to_all(slots, ("lat", "lon"), 0, 0, axis_index_groups=groups)


def per_device(fields, frac, shift, mix, proj, mode_shift, cells, source, weight):
    fields = fields[0]
    table = shift[0]
    plan, modes, lists = prepare(
        mix, table, frac[0], mode_shift.reshape(1, LEV), cells[0], source[0, 0].T, weight[0, 0].T, proj
    )
    packed, fields = pack(table, fields)
    west = send(packed, "lon", 1)
    east = send(pack_east(fields), "lon", -1)
    adv, rhs, half = advect(plan, fields, west, east)
    both = lax.all_gather(half, "panel")
    b, first = margin(rhs, both, lists)
    got_first = in_squares(first, 0)
    got_second = in_squares(second(b, first, got_first), 1)
    count = lax.axis_size("lon")
    rest = lax.axis_size("panel") * lax.axis_size("lat")
    c, u1, u2, sums, adv = images(modes, b, got_first, got_second, adv, rest)
    sums = relay(lax.all_to_all(sums, ("panel", "lat"), 0, 0), count)
    sums = lax.all_to_all(sums, "lon", 0, 0)
    sol, res = iterate(modes, sums, b, c, u1, u2)
    shape = (1, LEV, ROWS, COLS)
    return adv[None], sol.reshape(shape), res.reshape(shape)


def solution(mesh):
    wide = P("panel", None, None, "lat", "lon")
    flat = P("panel", None, "lat", "lon")
    table = P("panel", "lat", "lon", None)
    in_specs = (wide, flat, P("panel", "lat", None), P(), P(), P(), P("panel", "lat", "lon"), table, table)
    return jax.shard_map(per_device, mesh=mesh, in_specs=in_specs, out_specs=(wide, flat, flat), check_vma=False)
```

```python
import jax
import jax.numpy as jnp
from jax import lax
from jax.experimental import pallas as pl
from jax.experimental.pallas import tpu as pltpu
from jax.sharding import PartitionSpec as P

F32 = jnp.float32
BF16 = jnp.bfloat16
NF = 6
LEV = 24
ROWS = 16
COLS = 128
G = 3
OV = 256
VMEM_LIMIT = 48 * 1024 * 1024


def lane_iota(shape):
    return lax.broadcasted_iota(jnp.int32, shape, len(shape) - 1)


def roll_lanes(x, by):
    by = by % COLS
    if by == 0:
        return x
    return pltpu.roll(x, by, x.ndim - 1)


def params():
    return pltpu.CompilerParams(vmem_limit_bytes=VMEM_LIMIT)


def own_shift(shift_ref, lon):
    table = shift_ref[...]
    own = jnp.sum(jnp.where(lane_iota(table.shape) == lon, table, 0), axis=1, keepdims=True)
    return jnp.broadcast_to(own, (ROWS, COLS))


def half_bits(mask):
    return jnp.where(mask, 1, 0).astype(jnp.int16)


def lane_matrix(rule):
    source = lax.broadcasted_iota(jnp.int32, (COLS, COLS), 0)
    target = lax.broadcasted_iota(jnp.int32, (COLS, COLS), 1)
    return jnp.where(rule(source, target), 1.0, 0.0).astype(BF16)


def mirrored(source, target):
    return (target >= 32) & (source == jnp.where((target >> 5) == 2, target, (target + 64) & (COLS - 1)))


def pack_east_kernel(fields_ref, out_ref):
    pair = (lane_iota((ROWS, COLS)) >> 1).astype(jnp.int16)
    for g in range(G):
        acc = jnp.zeros((ROWS, COLS), BF16)
        for f in range(NF):
            for l8 in range(8):
                i = f * 8 + l8
                acc = jnp.where(pair == jnp.int16(i), roll_lanes(fields_ref[f, 8 * g + l8], 2 * i), acc)
        out_ref[g] = acc


def pack_east(fields):
    return pl.pallas_call(
        pack_east_kernel,
        in_specs=[pl.BlockSpec(memory_space=pltpu.VMEM)],
        out_specs=pl.BlockSpec(memory_space=pltpu.VMEM),
        out_shape=jax.ShapeDtypeStruct((G, ROWS, COLS), BF16),
        compiler_params=params(),
        name="pack_east",
    )(fields)


CHUNKS = NF // 2


def pack_kernel(shift_hbm, fields_hbm, west_ref, kept_ref, shift_ref, scratch, mask_ref, matrix_ref, sems):
    table = pltpu.make_async_copy(shift_hbm, shift_ref, sems.at[CHUNKS])
    table.start()
    whole = pltpu.make_async_copy(fields_hbm, kept_ref, sems.at[0])
    whole.start()
    table.wait()
    pack_plan(shift_ref, mask_ref, matrix_ref)
    masks = [mask_ref[n] == 1 for n in range(2)]
    zero = jnp.zeros((ROWS, COLS), BF16)
    whole.wait()
    rows = 8 * 2 * ROWS
    low = (lax.broadcasted_iota(jnp.int32, (rows, COLS), 0) & 1) == 0
    for n in range(CHUNKS):
        for g in range(G):
            parts = [
                jnp.concatenate([jnp.where(m, kept_ref[2 * n + f, 8 * g + l8], zero) for m in masks], axis=1)
                for l8 in range(8)
                for f in range(2)
            ]
            wide = jnp.dot(jnp.concatenate(parts, axis=0), matrix_ref[...], preferred_element_type=F32)
            scratch[g] = jnp.where(low, wide[:, :COLS], wide[:, COLS:])
            pairs = scratch[g, pl.ds(0, rows // 2, stride=2), :] + scratch[g, pl.ds(1, rows // 2, stride=2), :]
            pairs = pairs.astype(BF16)
            for l8 in range(8):
                west_ref[n, 8 * g + l8] = pairs[ROWS * l8 : ROWS * l8 + ROWS]


def pack_plan(shift_ref, mask_ref, matrix_ref):
    shift = own_shift(shift_ref, lax.axis_index("lon") + 1)
    lane = lane_iota((ROWS, COLS))
    mask_ref[0] = half_bits(lane >= COLS - 32 * shift)
    mask_ref[1] = half_bits(lane == COLS - 1 - 32 * shift)
    rules = (
        (lambda s, t: s == t, mirrored),
        (lambda s, t: ((s & 31) == 31) & (t == 31), lambda s, t: ((s & 31) == 31) & (t == 30)),
    )
    for m, pair in enumerate(rules):
        for n, rule in enumerate(pair):
            matrix_ref[COLS * m : COLS * m + COLS, COLS * n : COLS * n + COLS] = lane_matrix(rule)


def pack(shift, fields):
    return pl.pallas_call(
        pack_kernel,
        in_specs=[pl.BlockSpec(memory_space=pltpu.HBM)] * 2,
        out_specs=[pl.BlockSpec(memory_space=pltpu.VMEM)] * 2,
        out_shape=[
            jax.ShapeDtypeStruct((NF // 2, LEV, ROWS, COLS), BF16),
            jax.ShapeDtypeStruct((NF, LEV, ROWS, COLS), BF16),
        ],
        scratch_shapes=[
            pltpu.VMEM((ROWS, 32), jnp.int32),
            pltpu.VMEM((G, 16 * ROWS, COLS), F32),
            pltpu.VMEM((2, ROWS, COLS), jnp.int16),
            pltpu.VMEM((2 * COLS, 2 * COLS), BF16),
            pltpu.SemaphoreType.DMA((CHUNKS + 1,)),
        ],
        compiler_params=params(),
        name="pack",
    )(*(pltpu.with_memory_space_constraint(x, pltpu.HBM) for x in (shift, fields)))


TAPS = (-1, 0, 1, 2)


def turn(x, sign, odd, two):
    x = jnp.where(odd, roll_lanes(x, 32 * sign), x)
    return jnp.where(two, roll_lanes(x, 64), x)


def advect_plan(mix_ref, shift_ref, frac_ref, mix_out_ref, mask_ref, shift_out_ref, matrix_ref, weight_ref):
    for f in range(NF):
        for level in range(LEV):
            mix_out_ref[f, level] = jnp.full((8, COLS), mix_ref[f, level], F32)
    shift = own_shift(shift_ref, lax.axis_index("lon"))
    shift_out_ref[...] = shift
    lane = lane_iota((ROWS, COLS))
    low = (lax.broadcasted_iota(jnp.int32, (ROWS, COLS), 0) & 1) == 0
    odd, two = (shift & 1) == 1, (shift & 2) == 2

    def beyond(j):
        at = ((lane - j + 32 * shift) & (COLS - 1)) - 32 * shift + j
        return (at < 0) | (at >= COLS)

    masks = [beyond(j) for j in TAPS]
    masks += [odd, two, lane < 2, ~low & ((lane >> 5) != 2), lane == jnp.where(low, 31, 30)]
    for n, mask in enumerate(masks):
        mask_ref[n] = half_bits(mask)
    rules = [lambda s, t, j=j: s == ((t + j) & (COLS - 1)) for j in TAPS if j]
    rules.append(lambda s, t: ((s == 30) | (s == 31)) & ((t & 31) == 0))
    for n, rule in enumerate(rules):
        matrix_ref[n] = lane_matrix(rule)
    for level in range(LEV):
        t = turn(frac_ref[level], -1, odd, two)
        tm1, tm2, tp1 = t - 1.0, t - 2.0, t + 1.0
        weight_ref[0, level] = -t * tm1 * tm2 * (1.0 / 6.0)
        weight_ref[1, level] = tp1 * tm1 * tm2 * 0.5
        weight_ref[2, level] = -tp1 * t * tm2 * 0.5
        weight_ref[3, level] = tp1 * t * tm1 * (1.0 / 6.0)


def advect_kernel(
    mix_ref, mask_ref, shift_ref, matrix_ref, weight_ref, fields_ref, west_ref, east_ref, adv_ref, rhs_ref, half_ref, scratch
):
    shift = shift_ref[...]
    lane = lane_iota((ROWS, COLS))
    odd, two = (shift & 1) == 1, (shift & 2) == 2
    bits = [mask_ref[n] == 1 for n in range(9)]
    masks, (odd16, two16, edge16, swap16, single16) = bits[:4], bits[4:]
    single_at = lane == ((COLS - 32 * shift) & (COLS - 1))
    zero = jnp.zeros((ROWS, COLS), BF16)

    @pl.loop(0, G)
    def _(g):
        east = east_ref[g]
        for batch in (range(8),):
            chosen = [[] for _ in TAPS]
            singles = []
            for l8 in batch:
                level = g * 8 + l8
                shared = jnp.concatenate([west_ref[n, level] for n in range(NF // 2)], axis=0).astype(F32)
                scratch[l8, pl.ds(0, 8 * NF, stride=2), :] = shared
                scratch[l8, pl.ds(1, 8 * NF, stride=2), :] = shared
            for l8 in batch:
                level = g * 8 + l8
                west = scratch[l8].astype(BF16)
                for f in range(NF):
                    other = west[ROWS * f : ROWS * f + ROWS]
                    singles.append(jnp.where(single16, other, zero))
                    other = jnp.where(swap16, roll_lanes(other, 64), other)
                    other = jnp.where(edge16, roll_lanes(east, -2 * (f * 8 + l8)), other)
                    own = fields_ref[f, level]
                    for n, mask in enumerate(masks):
                        chosen[n].append(jnp.where(mask, other, own))
            wide = [
                jnp.dot(jnp.concatenate(chosen[tap], axis=0), matrix_ref[n], preferred_element_type=F32)
                for n, tap in ((0, 0), (1, 2), (2, 3))
            ]
            column = jnp.dot(jnp.concatenate(singles, axis=0), matrix_ref[3], preferred_element_type=F32)
            for k, l8 in enumerate(batch):
                level = g * 8 + l8
                weights = [weight_ref[n, level] for n in range(4)]
                total = jnp.zeros((ROWS, COLS), F32)
                for f in range(NF):
                    i = k * NF + f
                    at = slice(ROWS * i, ROWS * i + ROWS)
                    acc = weights[0] * jnp.where(single_at, column[at], wide[0][at])
                    acc = acc + weights[1] * chosen[1][i].astype(F32)
                    acc = acc + weights[2] * wide[1][at]
                    acc = acc + weights[3] * wide[2][at]
                    rounded = acc.astype(BF16)
                    adv_ref[f, level] = turn(rounded, 1, odd16, two16)
                    mix = mix_ref[f, level]
                    total = total + jnp.concatenate([mix, mix], axis=0) * rounded.astype(F32)
                rhs_ref[g, pl.ds(l8, ROWS, stride=8), :] = turn(total, 1, odd, two)
        half_ref[g] = rhs_ref[g].astype(BF16)


def advect(plan, fields, west, east):
    whole = pl.BlockSpec(memory_space=pltpu.VMEM)
    return pl.pallas_call(
        advect_kernel,
        in_specs=[whole] * 8,
        out_specs=[whole] * 3,
        out_shape=[
            jax.ShapeDtypeStruct((NF, LEV, ROWS, COLS), BF16),
            jax.ShapeDtypeStruct((G, 128, COLS), F32),
            jax.ShapeDtypeStruct((G, 128, COLS), BF16),
        ],
        scratch_shapes=[pltpu.VMEM((8, NF * ROWS, COLS), F32)],
        compiler_params=params(),
        name="advect",
    )(*plan, fields, west, east)


SLOTS = 20


def slot_of_lane(shape=(8, COLS)):
    return ((lane_iota(shape) + 3) & (COLS - 1)) // 6


def split3(x):
    a = x.astype(BF16)
    rest = x - a.astype(F32)
    b = rest.astype(BF16)
    c = (rest - b.astype(F32)).astype(BF16)
    return a, b, c


def prepare_kernel(
    mix_ref, shift_ref, frac_ref, mode_ref, cells_ref, source_ref, weight_ref, proj_ref,
    mix_out_ref, mask_ref, own_ref, matrix_ref, taps_ref, mode_out_ref,
    pick_ref, place_ref, in_row_ref, covered_ref, src_row_ref, wgt_ref, proj_out_ref,
):
    advect_plan(mix_ref, shift_ref, frac_ref, mix_out_ref, mask_ref, own_ref, matrix_ref, taps_ref)
    mode_out_ref[...] = mode_ref[...]
    proj_out_ref[...] = proj_ref[...]
    src = jnp.concatenate([source_ref[q : q + 1, :] for q in range(4)], axis=1)
    wgt = jnp.concatenate([weight_ref[q : q + 1, :] for q in range(4)], axis=1)
    wide = (COLS, 4 * OV)
    col = jnp.broadcast_to(src & (COLS - 1), wide)
    pick_ref[...] = jnp.where(lax.broadcasted_iota(jnp.int32, wide, 0) == col, 1.0, 0.0).astype(BF16)
    src_row_ref[...] = jnp.broadcast_to(src >> 7, (8, 4 * OV))
    wgt_ref[...] = jnp.broadcast_to(wgt, (8, 4 * OV))
    cells = cells_ref[...]
    sub = lax.broadcasted_iota(jnp.int32, (128, OV), 0)
    place = jnp.where(sub == jnp.broadcast_to(cells & (COLS - 1), (128, OV)), 1.0, 0.0).astype(BF16)
    place_ref[...] = place
    in_row = jnp.where((sub >> 3) == jnp.broadcast_to(cells >> 7, (128, OV)), 1.0, 0.0).astype(BF16)
    in_row_ref[...] = in_row
    nt = (((1,), (1,)), ((), ()))
    covered_ref[...] = lax.dot_general(in_row, place, nt, preferred_element_type=F32)


def prepare(*args):
    shapes = [
        ((NF, LEV, 8, COLS), F32),
        ((9, ROWS, COLS), jnp.int16),
        ((ROWS, COLS), jnp.int32),
        ((4, COLS, COLS), BF16),
        ((4, LEV, ROWS, COLS), F32),
        ((1, LEV), F32),
        ((COLS, 4 * OV), BF16),
        ((128, OV), BF16),
        ((128, OV), BF16),
        ((128, COLS), F32),
        ((8, 4 * OV), jnp.int32),
        ((8, 4 * OV), F32),
        ((LEV, LEV), F32),
    ]
    made = pl.pallas_call(
        prepare_kernel,
        in_specs=[pl.BlockSpec(memory_space=pltpu.SMEM)] + [pl.BlockSpec(memory_space=pltpu.VMEM)] * 7,
        out_shape=[jax.ShapeDtypeStruct(shape, dtype) for shape, dtype in shapes],
        compiler_params=params(),
        cost_estimate=pl.CostEstimate(flops=4_000_000, bytes_accessed=2_000_000, transcendentals=0),
        name="prepare",
    )(*args)
    return made[:5], made[5], made[6:]


def margin_kernel(
    rhs_ref, both_ref, pick_ref, place_ref, in_row_ref, covered_ref, src_row_ref, wgt_ref, proj_ref, b_ref, slots_ref
):
    other = 1 - lax.axis_index("panel")
    pick, place = pick_ref[...], place_ref[...]
    src_row, wgt = src_row_ref[...], wgt_ref[...]
    in_row = in_row_ref[...].astype(F32)
    covered = covered_ref[...] > 0.5
    nt = (((1,), (1,)), ((), ()))
    halves = jnp.concatenate([both_ref[other, lb] for lb in range(G)], axis=0)
    cols = jnp.dot(halves, pick, preferred_element_type=F32)
    rep = jnp.zeros((8 * G, 4 * OV), F32)
    for r in range(ROWS):
        weight = jnp.where(src_row == r, wgt, 0.0)
        rows = [cols[128 * lb + 8 * r : 128 * lb + 8 * r + 8] for lb in range(G)]
        rep = rep + jnp.concatenate([weight] * G, axis=0) * jnp.concatenate(rows, axis=0)
    rep = rep[:, :OV] + rep[:, OV : 2 * OV] + rep[:, 2 * OV : 3 * OV] + rep[:, 3 * OV :]
    spread = jnp.concatenate([in_row * jnp.concatenate([rep[8 * lb : 8 * lb + 8]] * ROWS, axis=0) for lb in range(G)], axis=0)
    placed = lax.dot_general(jnp.concatenate(split3(spread), axis=0), place, nt, preferred_element_type=F32)
    placed = placed[:384] + placed[384:768] + placed[768:]
    joined = [jnp.where(covered, placed[128 * lb : 128 * lb + 128], rhs_ref[lb]) for lb in range(G)]
    levels = jnp.concatenate(
        [jnp.concatenate([joined[lb][8 * r : 8 * r + 8] for lb in range(G)], axis=0) for r in range(ROWS)], axis=1
    )
    modal = jnp.dot(proj_ref[...], levels, precision=lax.Precision.HIGHEST, preferred_element_type=F32)
    for lb in range(G):
        for r in range(ROWS):
            b_ref[lb, 8 * r : 8 * r + 8, :] = modal[8 * lb : 8 * lb + 8, COLS * r : COLS * r + COLS]
    lat, lon = lax.axis_index("lat"), lax.axis_index("lon")
    place_in_square = 2 * (lat & 1) + (lon & 1)
    for lb in range(G):
        slots_ref[place_in_square ^ 2, lb] = b_ref[lb, pl.ds(pl.multiple_of(8 * 13 * (1 - (lat & 1)), 8), 24), :]
        acc = jnp.zeros((8, COLS), F32)
        for i in range(SLOTS):
            r = (i - 2) % ROWS
            acc = jnp.where(slot_of_lane() == i, roll_lanes(b_ref[lb, 8 * r : 8 * r + 8, :], 6 * i), acc)
        slots_ref[place_in_square ^ 1, lb, 0:8, :] = acc
        slots_ref[place_in_square ^ 3, lb, 0:8, :] = acc


def margin(rhs, both, lists):
    return pl.pallas_call(
        margin_kernel,
        out_shape=[
            jax.ShapeDtypeStruct((G, 128, COLS), F32),
            jax.ShapeDtypeStruct((4, G, 24, COLS), F32),
        ],
        compiler_params=params(),
        name="margin",
    )(rhs, both, *lists)


def second_kernel(b_ref, first_ref, got_ref, out_ref):
    lat, lon = lax.axis_index("lat"), lax.axis_index("lon")
    here = 2 * (lat & 1) + (lon & 1)
    there = 3 - here
    even = jnp.broadcast_to(lat & 1, (8, COLS)) == 0
    slot = slot_of_lane()
    for lb in range(G):
        out_ref[there ^ 2, lb, 0:24, :] = b_ref[lb, pl.ds(pl.multiple_of(8 * 13 * (lat & 1), 8), 24), :]
        out_ref[there ^ 2, lb, 24:32, :] = got_ref[here ^ 1, lb, 0:8, :]
        own = first_ref[here ^ 1, lb, 0:8, :]
        out_ref[there ^ 3, lb, 24:32, :] = own
        row = [got_ref[here ^ 2, lb, 8 * n : 8 * n + 8, :] for n in range(3)]
        with_south = jnp.where(slot == 18, roll_lanes(row[0], 6 * 18), jnp.where(slot == 19, roll_lanes(row[1], 6 * 19), own))
        with_north = jnp.where(slot == 0, row[1], jnp.where(slot == 1, roll_lanes(row[2], 6), own))
        out_ref[there ^ 1, lb, 24:32, :] = jnp.where(even, with_south, with_north)


def second(b, first, got):
    return pl.pallas_call(
        second_kernel,
        out_shape=jax.ShapeDtypeStruct((4, G, 32, COLS), F32),
        compiler_params=params(),
        name="second",
    )(b, first, got)


def images_kernel(shift_ref, b_ref, first_ref, second_ref, adv_ref, c_ref, u1_ref, u2_ref, s_ref, adv_hbm, sem):
    leaving = pltpu.make_async_copy(adv_ref, adv_hbm, sem)
    leaving.start()
    lat, lon = lax.axis_index("lat"), lax.axis_index("lon")
    one = jnp.float32(1.0)
    zero = jnp.float32(0.0)
    has_n = jnp.where(lat > 0, one, zero)
    has_s = jnp.where(lat < lax.axis_size("lat") - 1, one, zero)
    has_w = jnp.where(lon > 0, one, zero)
    has_e = jnp.where(lon < lax.axis_size("lon") - 1, one, zero)
    shape = (8 * G, COLS)
    lane = lane_iota(shape)
    first, last = lane == 0, lane == COLS - 1
    side = jnp.where(lane < 64, has_e, has_w)
    here = 2 * (lat & 1) + (lon & 1)
    there = 3 - here
    lat_even = jnp.broadcast_to(lat & 1, shape) == 0
    slot = slot_of_lane(shape)
    from_east = ((lane % 6) < 3) & (lane < 120)
    north_slot, south_slot = slot < 2, (slot == 18) | (slot == 19)
    inside = jnp.where(from_east, has_e, has_w)
    inside = jnp.where(north_slot, inside * has_n, jnp.where(south_slot, inside * has_s, inside)) > 0.5
    first_side = (lat_even & south_slot) | (~lat_even & north_slot)
    second_side = (lat_even & north_slot) | (~lat_even & south_slot)
    east_first = jnp.where(from_east, 1, 0) == jnp.broadcast_to(1 - (lon & 1), shape)

    def rows_of(ref, *at):
        return jnp.concatenate([ref[(*at[:-1], lb, at[-1])] for lb in range(G)], axis=0)

    def store(ref, j, value):
        for lb in range(G):
            ref[lb, 8 * j : 8 * j + 8, :] = value[8 * lb : 8 * lb + 8]

    def line(main, ext):
        return roll_lanes(jnp.where(last, ext, main), 1) + roll_lanes(jnp.where(first, ext, main), -1)

    def row_scale(j):
        return has_n if j < 0 else has_s if j >= ROWS else None

    modes = jnp.broadcast_to(shift_ref[...], (8 * G, LEV))
    diag = lane_iota((8 * G, LEV)) == lax.broadcasted_iota(jnp.int32, (8 * G, LEV), 0)
    a = jnp.broadcast_to(4.0 + jnp.sum(jnp.where(diag, modes, 0.0), axis=1, keepdims=True), shape)
    columns, forwarded = slice(0, 8), slice(24, 32)
    near = jnp.where(first_side, rows_of(first_ref, here ^ 3, columns), rows_of(first_ref, here ^ 1, columns))
    near = jnp.where(second_side, rows_of(second_ref, there ^ 2, forwarded), near)
    far = jnp.where(second_side, rows_of(second_ref, there ^ 3, forwarded), rows_of(second_ref, there ^ 1, forwarded))
    packed = jnp.where(inside, jnp.where(east_first, near, far), 0.0)

    def b_main(j):
        if 0 <= j < ROWS:
            return rows_of(b_ref, slice(8 * j, 8 * j + 8))
        n = j + 3 if j < 0 else j - ROWS
        rows = slice(8 * n, 8 * n + 8)
        one, two = rows_of(first_ref, here ^ 2, rows), rows_of(second_ref, there ^ 2, rows)
        if j < 0:
            return jnp.where(has_n > 0.5, jnp.where(lat_even, two, one), 0.0)
        return jnp.where(has_s > 0.5, jnp.where(lat_even, one, two), 0.0)

    bm = {j: b_main(j) for j in (-3, -2)}
    bx = {-2: packed}
    cm, cx, um, ux = {}, {}, {}, {}
    sums = [jnp.zeros(shape, F32) for _ in range(8)]
    for j in range(-2, ROWS + 4):
        if j <= ROWS + 1:
            bm[j + 1] = b_main(j + 1)
            if j + 1 <= ROWS + 1:
                bx[j + 1] = roll_lanes(packed, -6 * (j + 3))
            value = a * bm[j] - (bm[j - 1] + bm[j + 1] + line(bm[j], bx[j]))
            scale = row_scale(j)
            cm[j] = value if scale is None else value * scale
            if -1 <= j <= ROWS:
                value = (a * bx[j] - (bx[j - 1] + bx[j + 1] + line(bx[j], bm[j]))) * side
                cx[j] = value if scale is None else value * scale
            if 0 <= j < ROWS:
                store(c_ref, j, cm[j])
        i = j - 1
        if -1 <= i <= ROWS:
            value = 0.25 * (cm[i - 1] + cm[i + 1] + line(cm[i], cx[i]))
            scale = row_scale(i)
            um[i] = value if scale is None else value * scale
            if 0 <= i < ROWS:
                ux[i] = 0.25 * (cx[i - 1] + cx[i + 1] + line(cx[i], cm[i])) * side
                store(u1_ref, i, um[i])
        i = j - 2
        if 0 <= i < ROWS:
            u2 = 0.5 * (um[i - 1] + um[i + 1] + line(um[i], ux[i])) - cm[i]
            store(u2_ref, i, u2)
            b, c, u1 = b_main(i), cm[i], um[i]
            pairs = ((b, c), (b, u1), (b, u2), (c, c), (c, u1), (u1, u1), (u1, u2), (u2, u2))
            sums = [s + x * y for s, (x, y) in zip(sums, pairs)]
    lane, sub = lane_iota((8, COLS)), lax.broadcasted_iota(jnp.int32, (8, COLS), 0)
    sums_out = jnp.zeros((8, COLS), F32)
    for q in range(8):
        total = jnp.sum(sums[q], axis=1, keepdims=True)
        for lb in range(G):
            sums_out = jnp.where(lane == 8 * lb + q, total[8 * lb : 8 * lb + 8], sums_out)
    spread = jnp.zeros((8, COLS), F32)
    for m in range(4):
        spread = jnp.where((sub & 3) == m, roll_lanes(sums_out, 32 * m), spread)
    folded = jnp.concatenate([jnp.sum(spread[4 * h : 4 * h + 4], axis=0, keepdims=True) for h in range(2)], axis=0)
    for n in range(s_ref.shape[0]):
        s_ref[n] = folded
    leaving.wait()


def images(mode_shift, b, got_first, got_second, adv, copies):
    full = jax.ShapeDtypeStruct((G, 128, COLS), F32)
    return pl.pallas_call(
        images_kernel,
        in_specs=[pl.BlockSpec(memory_space=pltpu.VMEM)] * 5,
        out_specs=[pl.BlockSpec(memory_space=pltpu.VMEM)] * 4 + [pl.BlockSpec(memory_space=pltpu.HBM)],
        out_shape=[
            full,
            full,
            full,
            jax.ShapeDtypeStruct((copies, 2, COLS), F32),
            jax.ShapeDtypeStruct(adv.shape, adv.dtype),
        ],
        scratch_shapes=[pltpu.SemaphoreType.DMA(())],
        compiler_params=params(),
        name="images",
    )(mode_shift, b, got_first, got_second, adv)


def sum_copies(ref):
    parts = [ref[n] for n in range(ref.shape[0])]
    while len(parts) > 1:
        parts = [parts[n] + parts[n + 1] for n in range(0, len(parts), 2)]
    return parts[0]


def iterate_kernel(shift_ref, s_ref, b_ref, c_ref, u1_ref, u2_ref, sol_ref, res_ref):
    lane = lane_iota((8, COLS))
    total = sum_copies(s_ref)
    sub = lax.broadcasted_iota(jnp.int32, (8, COLS), 0)
    rows = jnp.where(sub < 4, jnp.broadcast_to(total[0:1], (8, COLS)), jnp.broadcast_to(total[1:2], (8, COLS)))
    sums = rows
    for m in range(1, 4):
        sums = jnp.where((sub & 3) == m, roll_lanes(rows, -32 * m), sums)
    for lb in range(G):
        diag = lane_iota((8, LEV)) == (lax.broadcasted_iota(jnp.int32, (8, LEV), 0) + 8 * lb)
        a = 4.0 + jnp.sum(jnp.where(diag, jnp.broadcast_to(shift_ref[...], (8, LEV)), 0.0), axis=1, keepdims=True)
        a = jnp.broadcast_to(a, (8, COLS))

        def inner(q):
            value = jnp.sum(jnp.where(lane == 8 * lb + q, sums, 0.0), axis=1, keepdims=True)
            return jnp.broadcast_to(value, (8, COLS))

        bc, bu1, bu2, cc, cu1, u1u1, u1u2, u2u2 = [inner(q) for q in range(8)]
        cu2 = 2.0 * u1u1 - cc
        l10 = cu1 / cc
        l20 = cu2 / cc
        d1 = u1u1 - l10 * cu1
        e1 = u1u2 - l10 * cu2
        l21 = e1 / d1
        d2 = u2u2 - l20 * cu2 - l21 * e1
        z0 = bc
        z1 = bu1 - l10 * z0
        z2 = bu2 - l20 * z0 - l21 * z1
        y2 = z2 / d2
        y1 = z1 / d1 - l21 * y2
        y0 = z0 / cc - l10 * y1 - l20 * y2
        for r in range(ROWS):
            rows = slice(8 * r, 8 * r + 8)
            b, c, u1, u2 = b_ref[lb, rows, :], c_ref[lb, rows, :], u1_ref[lb, rows, :], u2_ref[lb, rows, :]
            v1 = 0.25 * (a * b - c)
            v2 = 0.5 * (a * v1 - u1) - b
            at = pl.ds(lb * 128 + r, 8, stride=ROWS)
            sol_ref[at, :] = y0 * b + y1 * v1 + y2 * v2
            res_ref[at, :] = b - y0 * c - y1 * u1 - y2 * u2


def iterate(mode_shift, sums, b, c, u1, u2):
    out = jax.ShapeDtypeStruct((LEV * ROWS, COLS), F32)
    return pl.pallas_call(
        iterate_kernel,
        out_shape=[out, out],
        compiler_params=params(),
        name="iterate",
    )(mode_shift, sums, b, c, u1, u2)


def send(block, axis, by):
    count = lax.axis_size(axis)
    return lax.ppermute(block, axis, [(i, i + by) for i in range(count) if 0 <= i + by < count])


def relay_kernel(in_ref, out_ref):
    total = sum_copies(in_ref)
    for n in range(out_ref.shape[0]):
        out_ref[n] = total


def relay(parts, copies):
    return pl.pallas_call(
        relay_kernel,
        out_shape=jax.ShapeDtypeStruct((copies, 2, COLS), F32),
        compiler_params=params(),
        name="relay",
    )(parts)


def in_squares(slots, begin):
    lats, lons = lax.axis_size("lat"), lax.axis_size("lon")
    groups = [
        [((i + a) % lats) * lons + (j + b) % lons for a in (0, 1) for b in (0, 1)]
        for i in range(begin, lats, 2)
        for j in range(begin, lons, 2)
    ]
    return lax.all_to_all(slots, ("lat", "lon"), 0, 0, axis_index_groups=groups)


def per_device(fields, frac, shift, mix, proj, mode_shift, cells, source, weight):
    fields = fields[0]
    table = shift[0]
    plan, modes, lists = prepare(
        mix, table, frac[0], mode_shift.reshape(1, LEV), cells[0], source[0, 0].T, weight[0, 0].T, proj
    )
    packed, fields = pack(table, fields)
    west = send(packed, "lon", 1)
    east = send(pack_east(fields), "lon", -1)
    adv, rhs, half = advect(plan, fields, west, east)
    both = lax.all_gather(half, "panel")
    b, first = margin(rhs, both, lists)
    got_first = in_squares(first, 0)
    got_second = in_squares(second(b, first, got_first), 1)
    count = lax.axis_size("lon")
    rest = lax.axis_size("panel") * lax.axis_size("lat")
    c, u1, u2, sums, adv = images(modes, b, got_first, got_second, adv, rest)
    sums = relay(lax.all_to_all(sums, ("panel", "lat"), 0, 0), count)
    sums = lax.all_to_all(sums, "lon", 0, 0)
    sol, res = iterate(modes, sums, b, c, u1, u2)
    shape = (1, LEV, ROWS, COLS)
    return adv[None], sol.reshape(shape), res.reshape(shape)


def solution(mesh):
    wide = P("panel", None, None, "lat", "lon")
    flat = P("panel", None, "lat", "lon")
    table = P("panel", "lat", "lon", None)
    in_specs = (wide, flat, P("panel", "lat", None), P(), P(), P(), P("panel", "lat", "lon"), table, table)
    return jax.shard_map(per_device, mesh=mesh, in_specs=in_specs, out_specs=(wide, flat, flat), check_vma=False)
```
